128 devices in a mesh: rep: 32 (over z_hi, y, x), shard: 4 (over z_lo, core).
Axes of the slice: x: 4, y: 4, z: 4 (z_hi: 2, z_lo: 2; z = z_hi * 2 + z_lo), core: 2. Of those that a mesh axis runs over, the one named last changes fastest.
Arguments:
- hidden: bfloat16 [16384, 1024], P(('rep', 'shard')), may hold values from -6 to 6
- cotangent: bfloat16 [16384, 1024], P(('rep', 'shard')), may hold values from -6 to 6
- segment_ids: int32 [16384], P('rep'), may hold values from 0 to 2, as said below
- positions: int32 [16384], P('rep'), may hold values from 0 to 2560, as said below
- attention_gain: float32 [1024], P('shard'), may hold values from 0.1 to 1.9
- query_weight: float32 [1024, 2048], P('shard'), may hold values from -0.1875 to 0.1875
- key_weight: float32 [1024, 1024], P('shard'), may hold values from -0.1875 to 0.1875
- value_weight: float32 [1024, 1024], P('shard'), may hold values from -0.1875 to 0.1875
- query_gain: float32 [128], P('shard'), may hold values from 0.1 to 1.9
- key_gain: float32 [128], P('shard'), may hold values from 0.1 to 1.9
- headgate_weight: float32 [1024, 16], P('shard'), may hold values from -0.1875 to 0.1875
- headgate_bias: float32 [16], P('shard'), may hold values from -3 to 3
- output_weight: float32 [2048, 1024], P('shard'), may hold values from -3.5 to 3.5
- feedforward_gain: float32 [1024], P('shard'), may hold values from 0.1 to 1.9
- gate_weight: float32 [1024, 3072], P('shard'), may hold values from -0.1875 to 0.1875
- up_weight: float32 [1024, 3072], P('shard'), may hold values from -0.1875 to 0.1875
- down_weight: float32 [3072, 1024], P('shard'), may hold values from -0.109375 to 0.109375
Outputs:
- output: bfloat16 [16384, 1024], P(('rep', 'shard'))
- input_grad: bfloat16 [16384, 1024], P(('rep', 'shard'))
- grad_attention_gain: float32 [1024], P('shard')
- grad_query_weight: float32 [1024, 2048], P('shard')
- grad_key_weight: float32 [1024, 1024], P('shard')
- grad_value_weight: float32 [1024, 1024], P('shard')
- grad_query_gain: float32 [128], P('shard')
- grad_key_gain: float32 [128], P('shard')
- grad_headgate_weight: float32 [1024, 16], P('shard')
- grad_headgate_bias: float32 [16], P('shard')
- grad_output_weight: float32 [2048, 1024], P('shard')
- grad_feedforward_gain: float32 [1024], P('shard')
- grad_gate_weight: float32 [1024, 3072], P('shard')
- grad_up_weight: float32 [1024, 3072], P('shard')
- grad_down_weight: float32 [3072, 1024], P('shard')
The draws below stay inside these ranges and needn't reach their ends.
Inputs may be any that keep to these rules, and one draw needn't show every extreme that they name: `segment_ids`: within each sequence of 512 tokens the document numbers start at 0 and never fall. `positions`: positions rise by one from token to token within a document; each sequence's first token has position 0 and its last token position 2560.
All inputs are finite; a program needn't handle non-finite values.
Results may differ from the reference program's by a relative error of at most 0.029.
Values may be sent and summed in bfloat16 or wider, within the bound.
No kernel may reach another device: no remote copies, remote signals or barrier semaphores. Data moves between devices by JAX's collectives and lax.ppermute only.
A program may use at most 192 MiB of HBM per device.

```python
import math
import jax
import jax.numpy as jnp
from jax import lax

D = 1024
HQ = 16
KV = 8
HD = 128
FF = 3072
TOK_DEV = 128
SEQ = 512
TOKENS = 16384
N_REP = 32


def document_cuts(key):
    first_key, last_key, shift_key = jax.random.split(key, 3)
    first = jax.random.randint(first_key, (N_REP, 1), 1, TOK_DEV // 2 + 1)
    last = jax.random.randint(last_key, (N_REP, 1), SEQ - TOK_DEV // 2, SEQ)
    middle_shift = jax.random.randint(shift_key, (N_REP, 1), 0, 2048)
    shifts = jnp.concatenate([jnp.zeros((N_REP, 1), jnp.int32), middle_shift, last + 2049], 1)
    places = jnp.arange(SEQ, dtype=jnp.int32)[None, :]
    segment = (places >= first).astype(jnp.int32) + (places >= last).astype(jnp.int32)
    starts = jnp.concatenate([jnp.zeros((N_REP, 1), jnp.int32), first, last], 1)
    return (segment, starts, shifts, places)


def draw_segment_ids(key, part):
    segment, starts, shifts, places = document_cuts(key)
    return segment.reshape(-1)


def draw_positions(key, part):
    segment, starts, shifts, places = document_cuts(key)
    start_of = jnp.take_along_axis(starts, segment, 1)
    shift_of = jnp.take_along_axis(shifts, segment, 1)
    return (places - start_of + shift_of).reshape(-1)


def block_scale(rng, extent, shards, low, largest):
    def one(position, blocks):
        draws = jax.random.uniform(jax.random.fold_in(jax.random.fold_in(rng, 6), position), (blocks,), jnp.float32, low / len(shards), largest / len(shards))
        return jnp.repeat(jnp.exp(draws), extent[position] // blocks).reshape((-1,) + (1,) * (len(extent) - position - 1))

    gain = one(*shards[0])
    for cut in shards[1:]:
        gain = gain * one(*cut)
    return gain


def centred(stream_key, dims, deviation, bound, cuts=(), kind=jnp.bfloat16):
    gain = block_scale(stream_key, dims, cuts, -0.22, 0.18) if cuts else 1.0
    drawn = jax.random.normal(stream_key, dims, jnp.float32) * deviation * gain
    return jnp.minimum(jnp.maximum(drawn, -bound), bound).astype(kind)


def setup_inputs(seed: int = 0) -> dict:
    arg_keys = jax.random.split(jax.random.key(seed), 18)
    return {
        "hidden": centred(arg_keys[0], (TOKENS, D), 1.0, 6.0, ((0, 128),)),
        "cotangent": centred(arg_keys[1], (TOKENS, D), 1.0, 6.0, ((0, 128),)),
        "segment_ids": draw_segment_ids(jax.random.fold_in(arg_keys[17], 71), 0),
        "positions": draw_positions(jax.random.fold_in(arg_keys[17], 71), 0),
        "attention_gain": jnp.clip(1.0 + 0.18 * jax.random.normal(arg_keys[4], (D,), jnp.float32), 0.1, 1.9),
        "query_weight": centred(arg_keys[5], (D, HQ * HD), D ** -0.5, 0.1875, ((0, 4),), jnp.float32),
        "key_weight": centred(arg_keys[6], (D, KV * HD), D ** -0.5, 0.1875, ((0, 4),), jnp.float32),
        "value_weight": centred(arg_keys[7], (D, KV * HD), D ** -0.5, 0.1875, ((0, 4),), jnp.float32),
        "query_gain": jnp.clip(1.0 + 0.18 * jax.random.normal(arg_keys[8], (HD,), jnp.float32), 0.1, 1.9),
        "key_gain": jnp.clip(1.0 + 0.18 * jax.random.normal(arg_keys[9], (HD,), jnp.float32), 0.1, 1.9),
        "headgate_weight": centred(arg_keys[10], (D, HQ), D ** -0.5, 0.1875, ((0, 4),), jnp.float32),
        "headgate_bias": centred(arg_keys[11], (HQ,), 1.0, 3.0, ((0, 4),), jnp.float32),
        "output_weight": centred(arg_keys[12], (HQ * HD, D), 3 ** -0.5, 3.5, ((0, 4),), jnp.float32),
        "feedforward_gain": jnp.clip(1.0 + 0.18 * jax.random.normal(arg_keys[13], (D,), jnp.float32), 0.1, 1.9),
        "gate_weight": centred(arg_keys[14], (D, FF), D ** -0.5, 0.1875, ((0, 4),), jnp.float32),
        "up_weight": centred(arg_keys[15], (D, FF), D ** -0.5, 0.1875, ((0, 4),), jnp.float32),
        "down_weight": centred(arg_keys[16], (FF, D), FF ** -0.5, 0.109375, ((0, 4),), jnp.float32),
    }


@jax.custom_vjp
def low(v):
    return lax.optimization_barrier(v.astype(jnp.bfloat16)).astype(jnp.float32)

@jax.custom_vjp
def low_back(v):
    return v

def low_keep(v):
    return (low(v), None)

def low_pass(kept, grad):
    return (grad,)

def back_keep(v):
    return (v, None)

def back_low(kept, grad):
    return (low(grad),)
low.defvjp(low_keep, low_pass)
low_back.defvjp(back_keep, back_low)
epsilon = 1e-06
theta = 1000000.0
masked_score = -1e+30

def normed(value):
    return value * lax.rsqrt(lax.optimization_barrier(jnp.mean(value * value, -1, keepdims=True)) + epsilon)

def product(left, right):
    return jnp.dot(left, right, precision=lax.Precision.HIGHEST)

def tables(places, head_size):
    half = head_size // 2
    freq = jnp.power(jnp.float32(theta), -jnp.arange(half, dtype=jnp.float32) * 2.0 / head_size)
    angle = places.astype(jnp.float32)[:, None] * freq[None, :]
    return (jnp.cos(angle), jnp.sin(angle))

def rotate(value, cosine, sine):
    half = value.shape[-1] // 2
    first = value[..., :half]
    second = value[..., half:]
    cosine = cosine[:, None, :]
    sine = sine[:, None, :]
    return jnp.concatenate([first * cosine - second * sine, second * cosine + first * sine], -1)

def attend(items):
    query_seq, key_seq, value_seq, segment_seq = items
    group = HQ // KV
    query_group = query_seq.reshape(SEQ, KV, group, HD)
    scores = jnp.einsum('lkgh,skh->kgls', query_group, key_seq, precision=lax.Precision.HIGHEST)
    scores = low_back(scores * (1.0 / math.sqrt(HD)))
    places = jnp.arange(SEQ)
    allowed = (places[None, :] <= places[:, None]) & (segment_seq[:, None] == segment_seq[None, :])
    scores = jnp.where(allowed[None, None], scores, masked_score)
    probs = jax.nn.softmax(scores, axis=-1)
    attended = jnp.einsum('kgls,skh->lkgh', low(probs), value_seq, precision=lax.Precision.HIGHEST)
    return low_back(attended).reshape(SEQ, HQ, HD)

def forward(inputs, weights, segment_ids, positions):
    attention_gain, query_weight, key_weight, value_weight, query_gain, key_gain, headgate_weight, headgate_bias, output_weight, feedforward_gain, gate_weight, up_weight, down_weight = [low(w) for w in weights]
    attn_in = low(normed(inputs) * attention_gain)
    query_raw = low_back(product(attn_in, query_weight)).reshape(TOKENS, HQ, HD)
    key_raw = low_back(product(attn_in, key_weight)).reshape(TOKENS, KV, HD)
    value = low(low_back(product(attn_in, value_weight))).reshape(TOKENS, KV, HD)
    gate_logit = low_back(product(attn_in, headgate_weight) + headgate_bias)
    cosine, sine = tables(positions, HD)
    query = low(rotate(normed(query_raw) * query_gain, cosine, sine))
    key = low(rotate(normed(key_raw) * key_gain, cosine, sine))
    attended = lax.map(jax.checkpoint(attend), (query.reshape(N_REP, SEQ, HQ, HD), key.reshape(N_REP, SEQ, KV, HD), value.reshape(N_REP, SEQ, KV, HD), segment_ids.reshape(N_REP, SEQ)))
    attended = attended.reshape(TOKENS, HQ, HD)
    mixed = low(attended * jax.nn.sigmoid(gate_logit)[:, :, None]).reshape(TOKENS, HQ * HD)
    resid = inputs + low_back(product(mixed, output_weight))
    ffn_in = low(normed(resid) * feedforward_gain)
    gate_pre = low_back(product(ffn_in, gate_weight))
    up_pre = low_back(product(ffn_in, up_weight))
    act = low(jax.nn.silu(gate_pre) * up_pre)
    return resid + low_back(product(act, down_weight))

def reference(hidden, cotangent, segment_ids, positions, attention_gain, query_weight, key_weight, value_weight, query_gain, key_gain, headgate_weight, headgate_bias, output_weight, feedforward_gain, gate_weight, up_weight, down_weight):
    params = (attention_gain, query_weight, key_weight, value_weight, query_gain, key_gain, headgate_weight, headgate_bias, output_weight, feedforward_gain, gate_weight, up_weight, down_weight)

    def run(inputs, *weights):
        return forward(inputs, weights, segment_ids, positions)
    output, pull = jax.vjp(run, hidden.astype(jnp.float32), *params)
    grads = pull(cotangent.astype(jnp.float32))
    return (output.astype(jnp.bfloat16), grads[0].astype(jnp.bfloat16), grads[1], grads[2], grads[3], grads[4], grads[5], grads[6], grads[7], grads[8], grads[9], grads[10], grads[11], grads[12], grads[13])
```

```python
import functools
import math

import jax
import jax.numpy as jnp
from jax import lax
from jax.experimental import pallas as pl
from jax.experimental.pallas import tpu as pltpu
from jax.sharding import Mesh
from jax.sharding import PartitionSpec as P

EPS = 1e-06
THETA = 1000000.0
MASKED = -1e30
HEAD = 128
LOW = jnp.bfloat16
FULL = jnp.float32
AXES = ("zh", "y", "x", "zl", "core")
GROUP = ("zl", "core")
LANES = 128
STREAMS = (
    (("x", 1), ("x", 3), ("y", 1), ("y", 3)),
    (("x", 3), ("x", 1), ("y", 3), ("y", 1)),
    (("y", 1), ("y", 3), ("x", 1), ("x", 3)),
    (("y", 3), ("y", 1), ("x", 3), ("x", 1)),
)
SIZE = {"zh": 2, "y": 4, "x": 4, "zl": 2, "core": 2}
DEST = (0, 2, 1, 3)


def swap(value, axis, mask):
    return lax.ppermute(value, axis, [(i, i ^ mask) for i in range(SIZE[axis])])


def turn(value, step):
    return lax.ppermute(value, ("zh", "zl"), [(i, (i + step) % 4) for i in range(4)])


def place_block(stream, pos, mine_x, mine_y):
    rel = {"x": 0, "y": 0}
    for k, (axis, mask) in enumerate(STREAMS[stream]):
        bit = (pos >> (3 - k)) & 1
        rel[axis] = rel[axis] ^ (mask * bit)
    return (mine_y ^ rel["y"]) * 4 + (mine_x ^ rel["x"])


def dot(left, right):
    return jnp.dot(left, right, preferred_element_type=FULL)


def dot_t(left, right):
    return lax.dot_general(left, right, (((1,), (1,)), ((), ())), preferred_element_type=FULL)


def dot_tn(left, right):
    return lax.dot_general(left, right, (((0,), (0,)), ((), ())), preferred_element_type=FULL)


def spread_kernel(coords, left_c, right_c, left_r, right_r, *refs):
    outs, (held_c, held_r) = refs[:8], refs[8:]
    mine_x, mine_y, j = coords[0], coords[1], coords[2]
    panels = right_c.shape[1] // (4 * LANES)
    wide = panels * LANES
    rows_r = left_r.shape[1] // 16
    base = 4 * panels * 16
    for s in range(4):
        keep, send = outs[s], outs[4 + s]
        held_c[...] = dot_tn(left_c[...], right_c[:, s * wide : (s + 1) * wide]).astype(LOW)
        held_r[...] = dot_tn(left_r[...], right_r[:, s * 256 : (s + 1) * 256]).astype(LOW)

        for pos in range(16):
            block = place_block(s, pos, mine_x, mine_y)
            out, at = (keep, pos) if pos < 8 else (send, pos - 8)
            for d in range(4):
                row = pl.multiple_of((j ^ DEST[d]) * 256 + block * 16, 16)
                for p in range(panels):
                    low = (d * panels + p) * 16
                    out[at, low : low + 16, :] = held_c[pl.ds(row, 16), p * LANES : (p + 1) * LANES]
            row = pl.multiple_of(block * rows_r, 16)
            for p in range(2):
                low = base + p * rows_r
                out[at, low : low + rows_r, :] = held_r[pl.ds(row, rows_r), p * LANES : (p + 1) * LANES]


def spread(coords, left_c, right_c, left_r, right_r):
    panels = right_c.shape[1] // 512
    rows = 4 * panels * 16 + 2 * (left_r.shape[1] // 16)
    vmem = pl.BlockSpec(memory_space=pltpu.VMEM)
    return pl.pallas_call(
        spread_kernel,
        out_shape=[jax.ShapeDtypeStruct((8, rows, LANES), LOW)] * 8,
        in_specs=[pl.BlockSpec(memory_space=pltpu.SMEM)] + [vmem] * 4,
        out_specs=[vmem] * 8,
        scratch_shapes=[
            pltpu.VMEM((left_c.shape[1], panels * LANES), LOW),
            pltpu.VMEM((left_r.shape[1], 256), LOW),
        ],
        compiler_params=pltpu.CompilerParams(vmem_limit_bytes=48 * 2**20),
        cost_estimate=pl.CostEstimate(
            flops=2 * 512 * (left_c.shape[1] * right_c.shape[1] + left_r.shape[1] * right_r.shape[1]),
            bytes_accessed=2 * 16 * 4 * rows * LANES,
            transcendentals=0,
        ),
    )(coords, left_c, right_c, left_r, right_r)


def settle_kernel(widths, coords, *refs):
    ins, outs = refs[:8], refs[8:]
    mine_x, mine_y, j = coords[0], coords[1], coords[2]
    panels = sum(widths) // 512
    rows_r = outs[-1].shape[0] // 16
    base = 4 * panels * 16
    spots = []
    for t in range(4 * panels):
        col, w = t * LANES, 0
        while col >= widths[w]:
            col, w = col - widths[w], w + 1
        spots.append((w, col))

    for s in range(4):
        for pos in range(16):
            block = place_block(s, pos, mine_x, mine_y)
            got, at = (ins[s], pos) if pos < 8 else (ins[4 + s], pos - 8)
            row = pl.multiple_of(block * 16, 16)
            for r in range(4):
                for p in range(panels):
                    w, col = spots[s * panels + p]
                    lane = pl.multiple_of((j ^ r) * widths[w] + col, LANES)
                    low = (r * panels + p) * 16
                    outs[w][pl.ds(row, 16), pl.ds(lane, LANES)] = got[at, low : low + 16, :].astype(FULL)
            row = pl.multiple_of(block * rows_r, 16)
            for p in range(2):
                low = base + p * rows_r
                lane = s * 256 + p * LANES
                outs[-1][pl.ds(row, rows_r), lane : lane + LANES] = got[at, low : low + rows_r, :].astype(FULL)


def settle(coords, pieces, widths, rows_r):
    vmem = pl.BlockSpec(memory_space=pltpu.VMEM)
    shapes = [(256, 4 * w) for w in widths] + [(rows_r, 1024)]
    return pl.pallas_call(
        functools.partial(settle_kernel, widths),
        out_shape=[jax.ShapeDtypeStruct(s, FULL) for s in shapes],
        in_specs=[pl.BlockSpec(memory_space=pltpu.SMEM)] + [vmem] * 8,
        out_specs=[vmem] * len(shapes),
        compiler_params=pltpu.CompilerParams(vmem_limit_bytes=48 * 2**20),
        cost_estimate=pl.CostEstimate(
            flops=0, bytes_accessed=6 * sum(a * b for a, b in shapes), transcendentals=0
        ),
    )(coords, *pieces)


def sum_over_replicas(pieces, panels):
    kept, sent = list(pieces[:4]), list(pieces[4:])
    for k in range(4):
        got = [swap(sent[s], *STREAMS[s][k]) for s in range(4)]
        both = [kept[s] + got[s] for s in range(4)]
        if k < 3:
            half = 4 >> k
            kept, sent = [b[:half] for b in both], [b[half:] for b in both]
    whole = jnp.concatenate(both, 0)
    base = 4 * panels * 16
    columns = whole[:, :base].reshape(4, 4, panels * 16, LANES)
    rows = whole[:, base:]
    got = swap(columns[:, 2:], "core", 1)
    mine = jnp.stack([columns[:, 0], got[:, 0]], 1).reshape(4, base // 2, LANES)
    other = jnp.stack([columns[:, 1], got[:, 1]], 1).reshape(4, base // 2, LANES)
    mine = jnp.concatenate([mine, rows], 1)
    mine = mine + swap(mine, "zh", 1)
    other = turn(other, 1) + turn(other, -1)
    whole = jnp.concatenate([mine[:, : base // 2], other, mine[:, base // 2 :]], 1)
    held = [whole[s : s + 1] for s in range(4)]
    for k in (3, 2, 1):
        got = [swap(held[s], *STREAMS[s][k]) for s in range(4)]
        held = [jnp.concatenate([held[s], got[s]], 0) for s in range(4)]
    return held + [swap(held[s], *STREAMS[s][0]) for s in range(4)]


def group_gather(part):
    beside = swap(part, "core", 1)
    across = swap(part, "zl", 1)
    return jnp.stack([part, beside, across, swap(across, "core", 1)])


def group_scatter(parts):
    got = swap(jnp.stack([parts[1], parts[3]]).astype(LOW), "core", 1).astype(FULL)
    mine, other = parts[0] + got[0], parts[2] + got[1]
    return mine + swap(other.astype(LOW), "zl", 1).astype(FULL)


def take_columns(weights, widths, j):
    blocks = [
        jnp.concatenate(
            [lax.dynamic_slice_in_dim(w, (j ^ r) * n, n, 1) for w, n in zip(weights, widths)], 1
        ).astype(LOW)
        for r in range(4)
    ]
    got = swap(jnp.stack([blocks[1], blocks[3]]), "core", 1)
    ahead, behind = turn(blocks[2], 1), turn(got[1], -1)
    rel = jnp.stack([blocks[0], got[0], ahead, behind])
    return jnp.concatenate(
        [lax.dynamic_index_in_dim(rel, j ^ r, 0, False) for r in range(4)], 0
    )


def inverse_rms(value):
    return lax.rsqrt(jnp.mean(value * value, -1, keepdims=True) + EPS)


def norm_back(grad, normal, inverse):
    return inverse * (grad - normal * jnp.mean(grad * normal, -1, keepdims=True))


def rotate(value, cosine, sine):
    first, second = value[..., :64], value[..., 64:]
    return jnp.concatenate([first * cosine - second * sine, second * cosine + first * sine], -1)


def body(
    hidden,
    cotangent,
    segment_ids,
    positions,
    attention_gain,
    query_weight,
    key_weight,
    value_weight,
    query_gain,
    key_gain,
    headgate_weight,
    headgate_bias,
    output_weight,
    feedforward_gain,
    gate_weight,
    up_weight,
    down_weight,
):
    zl, core = lax.axis_index("zl"), lax.axis_index("core")
    j = zl * 2 + core
    coords = jnp.stack([lax.axis_index("x"), lax.axis_index("y"), j]).astype(jnp.int32)
    order = j ^ jnp.arange(4)

    small = jnp.concatenate(
        [
            attention_gain,
            feedforward_gain,
            query_gain,
            key_gain,
            headgate_bias,
            headgate_weight.reshape(-1),
            jnp.zeros(5120 - 4676, FULL),
        ]
    ).astype(LOW)
    small = lax.all_gather(small.reshape(40, 128), GROUP, axis=0, tiled=True).reshape(4, 5120).astype(FULL)
    gain_first = small[:, :256].reshape(1024)
    gain_second = small[:, 256:512].reshape(1024)
    gain_query = small[:, 512:544].reshape(128)
    gain_key = small[:, 544:576].reshape(128)
    head_bias = lax.dynamic_slice_in_dim(small[:, 576:580].reshape(16), 4 * j, 4)
    head_weight = lax.dynamic_slice_in_dim(small[:, 580:4676].reshape(1024, 16), 4 * j, 4, 1).astype(LOW)

    tokens = group_gather(hidden).reshape(512, 1024)
    weight_qkv = take_columns((query_weight, key_weight, value_weight), (512, 256, 256), j)
    grads = group_gather(cotangent).reshape(512, 1024)
    weight_gu = take_columns((gate_weight, up_weight), (768, 768), j)
    weight_o = output_weight.astype(LOW)
    weight_d = down_weight.astype(LOW)

    segs = jnp.take(segment_ids.reshape(4, 128), order, axis=0).reshape(512)
    spots = jnp.take(positions.reshape(4, 128), order, axis=0).reshape(512)
    index = (order[:, None] * 128 + jnp.arange(128)[None, :]).reshape(512)
    allowed = (index[None, :] <= index[:, None]) & (segs[:, None] == segs[None, :])
    freq = jnp.power(jnp.float32(THETA), -jnp.arange(64, dtype=FULL) * 2.0 / HEAD)
    angle = spots.astype(FULL)[:, None] * freq[None, :]
    cosine, sine = jnp.cos(angle)[:, None, :], jnp.sin(angle)[:, None, :]
    scale = 1.0 / math.sqrt(HEAD)

    x = tokens.astype(FULL)
    inv_first = inverse_rms(x)
    normed_first = x * inv_first
    attn_in = (normed_first * gain_first).astype(LOW)
    raw = dot(attn_in, weight_qkv)
    query_raw = raw[:, :512].reshape(512, 4, HEAD)
    key_raw = raw[:, 512:768].reshape(512, 2, HEAD)
    value = raw[:, 768:].astype(LOW).reshape(512, 2, HEAD)
    logit = dot(attn_in, head_weight) + head_bias
    inv_q, inv_k = inverse_rms(query_raw), inverse_rms(key_raw)
    norm_q, norm_k = query_raw * inv_q, key_raw * inv_k
    query = rotate(norm_q * gain_query, cosine, sine).astype(LOW)
    key = rotate(norm_k * gain_key, cosine, sine).astype(LOW)
    q4 = query.reshape(512, 2, 2, HEAD)
    scores = jnp.einsum("lkgh,skh->kgls", q4, key, preferred_element_type=FULL) * scale
    scores = jnp.where(allowed, scores, MASKED)
    expo = jnp.exp(scores - jnp.max(scores, -1, keepdims=True))
    probs = expo / jnp.sum(expo, -1, keepdims=True)
    probs_low = probs.astype(LOW)
    attended = jnp.einsum("kgls,skh->lkgh", probs_low, value, preferred_element_type=FULL).reshape(512, 4, HEAD)
    gate = jax.nn.sigmoid(logit)
    mixed = (attended * gate[:, :, None]).astype(LOW).reshape(512, 512)
    resid = hidden.astype(FULL) + group_scatter(dot(mixed, weight_o).reshape(4, 128, 1024))

    inv_second = inverse_rms(resid)
    normed_second = resid * inv_second
    ffn_in = group_gather((normed_second * gain_second).astype(LOW)).reshape(512, 1024)
    gu = dot(ffn_in, weight_gu)
    gate_pre, up_pre = gu[:, :768], gu[:, 768:]
    sigma = jax.nn.sigmoid(gate_pre)
    swish = gate_pre * sigma
    act = (swish * up_pre).astype(LOW)
    grad_act = dot_t(grads, weight_d)
    grad_gate = (grad_act * up_pre * sigma * (1.0 + gate_pre * (1.0 - sigma))).astype(LOW)
    grad_up = (grad_act * swish).astype(LOW)
    grad_gu = jnp.concatenate([grad_gate, grad_up], 1)
    grad_ffn = group_scatter(dot_t(grad_gu, weight_gu).reshape(4, 128, 1024))
    output = (resid + group_scatter(dot(act, weight_d).reshape(4, 128, 1024))).astype(LOW)
    first = sum_over_replicas(spread(coords, ffn_in, grad_gu, act, grads), 3)
    grad_g, grad_u, grad_d = settle(coords, first, (768, 768), 768)

    grad_gain_second = jnp.sum(grad_ffn * normed_second, 0)
    grad_resid = cotangent.astype(FULL) + norm_back(grad_ffn * gain_second, normed_second, inv_second)
    resid_low = group_gather(grad_resid.astype(LOW)).reshape(512, 1024)

    grad_mixed = dot_t(resid_low, weight_o).reshape(512, 4, HEAD)
    grad_logit = (jnp.sum(grad_mixed * attended, -1) * gate * (1.0 - gate)).astype(LOW)
    grad_attended = (grad_mixed * gate[:, :, None]).astype(LOW).reshape(512, 2, 2, HEAD)
    grad_probs = jnp.einsum("lkgh,skh->kgls", grad_attended, value, preferred_element_type=FULL)
    grad_value = jnp.einsum("kgls,lkgh->skh", probs_low, grad_attended, preferred_element_type=FULL)
    grad_scores = (probs * (grad_probs - jnp.sum(probs * grad_probs, -1, keepdims=True))).astype(LOW)
    grad_query = jnp.einsum("kgls,skh->lkgh", grad_scores, key, preferred_element_type=FULL) * scale
    grad_key = jnp.einsum("kgls,lkgh->skh", grad_scores, q4, preferred_element_type=FULL) * scale

    def head_back(grad, normal, inverse, gain):
        turned = rotate(grad, cosine, -sine)
        return jnp.sum(turned * normal, (0, 1)), norm_back(turned * gain, normal, inverse).astype(LOW)

    grad_qgain, grad_q = head_back(grad_query.reshape(512, 4, HEAD), norm_q, inv_q, gain_query)
    grad_kgain, grad_k = head_back(grad_key, norm_k, inv_k, gain_key)
    grad_qkv = jnp.concatenate(
        [grad_q.reshape(512, 512), grad_k.reshape(512, 256), grad_value.astype(LOW).reshape(512, 256)], 1
    )
    grad_in = dot_t(grad_qkv, weight_qkv) + dot_t(grad_logit, head_weight)
    second = sum_over_replicas(spread(coords, attn_in, grad_qkv, mixed, resid_low), 2)
    grad_qw, grad_kw, grad_vw, grad_ow = settle(coords, second, (512, 256, 256), 512)
    grad_headgate = dot_tn(attn_in, grad_logit)
    grad_headbias = jnp.sum(grad_logit.astype(FULL), 0)
    grad_gain_first = jnp.sum(grad_in * normed_first, 0)
    mine = group_scatter(grad_in.reshape(4, 128, 1024))
    own = hidden.astype(FULL)
    inv_own = inverse_rms(own)
    input_grad = (grad_resid + norm_back(mine * gain_first, own * inv_own, inv_own)).astype(LOW)

    small = jnp.concatenate(
        [grad_gain_first, grad_gain_second, grad_qgain, grad_kgain, grad_headgate.reshape(-1), grad_headbias]
    )
    small = jnp.pad(small, (0, 6528 - small.shape[0])).reshape(51, 128)
    for axis, mask in STREAMS[0] + (("zh", 1),):
        small = small + swap(small, axis, mask)
    gains = small[:18]
    heads = lax.dynamic_update_slice_in_dim(jnp.zeros((4, 33, 128), FULL), small[None, 18:], j, 0).reshape(132, 128)
    small = jnp.concatenate([gains, heads])
    for axis in GROUP:
        small = small + swap(small, axis, 1)
    heads = small[18:].reshape(4, 33 * 128)
    heads_w = heads[:, :4096].reshape(4, 1024, 4).transpose(1, 0, 2).reshape(-1)
    small = jnp.concatenate([small[:18].reshape(-1), heads_w, heads[:, 4096:4100].reshape(-1)])

    def quarter(start, size):
        return lax.dynamic_slice_in_dim(small, start + j * size, size)

    return (
        output,
        input_grad,
        quarter(0, 256),
        grad_qw,
        grad_kw,
        grad_vw,
        quarter(2048, 32),
        quarter(2176, 32),
        quarter(2304, 4096).reshape(256, 16),
        quarter(2304 + 16384, 4),
        grad_ow,
        quarter(1024, 256),
        grad_g,
        grad_u,
        grad_d,
    )


def solution(mesh):
    grid = Mesh(mesh.devices.reshape(2, 4, 4, 2, 2), AXES)
    tokens, split, copies = P(AXES, None), P(GROUP, None), P(("zh", "y", "x"))
    line = P(GROUP)
    return jax.shard_map(
        body,
        mesh=grid,
        in_specs=(
            tokens,
            tokens,
            copies,
            copies,
            line,
            split,
            split,
            split,
            line,
            line,
            split,
            line,
            split,
            line,
            split,
            split,
            split,
        ),
        out_specs=(
            tokens,
            tokens,
            line,
            split,
            split,
            split,
            line,
            line,
            split,
            line,
            split,
            line,
            split,
            split,
            split,
        ),
        check_vma=False,
    )
```

```python
import functools
import math

import jax
import jax.numpy as jnp
from jax import lax
from jax.experimental import pallas as pl
from jax.experimental.pallas import tpu as pltpu
from jax.sharding import Mesh
from jax.sharding import PartitionSpec as P

EPS = 1e-06
THETA = 1000000.0
MASKED = -1e30
HEAD = 128
SCALE = 1.0 / math.sqrt(HEAD)
LOW = jnp.bfloat16
FULL = jnp.float32
AXES = ("zh", "y", "x", "zl", "core")
GROUP = ("zl", "core")
LANES = 128


def swap(value, axis):
    return lax.ppermute(value, axis, [(0, 1), (1, 0)])


def turn(value, step):
    return lax.ppermute(value, ("zh", "zl"), [(i, (i + step) % 4) for i in range(4)])


def swap_far(value):
    return lax.ppermute(value, ("zh", "zl"), [(0, 3), (3, 0), (1, 2), (2, 1)])


def swap_plane(value, axis, mask):
    pairs = []
    for y in range(4):
        for x in range(4):
            for core in range(2):
                to_y, to_x = (y, x ^ mask) if axis == core else (y ^ mask, x)
                pairs.append(((y * 4 + x) * 2 + core, (to_y * 4 + to_x) * 2 + core))
    return lax.ppermute(value, ("y", "x", "core"), pairs)


def dot(left, right):
    return jnp.dot(left, right, preferred_element_type=FULL)


def dot_t(left, right):
    return lax.dot_general(left, right, (((1,), (1,)), ((), ())), preferred_element_type=FULL)


def dot_tn(left, right):
    return lax.dot_general(left, right, (((0,), (0,)), ((), ())), preferred_element_type=FULL)


VMEM = pl.BlockSpec(memory_space=pltpu.VMEM)
SMEM = pl.BlockSpec(memory_space=pltpu.SMEM)


def held_bytes(shape, kind):
    shape = (1,) * (2 - len(shape)) + tuple(shape)
    size = math.prod(shape[:-2]) * (-(-shape[-2] // 16) * 16) * (-(-shape[-1] // LANES) * LANES)
    return size * jnp.dtype(kind).itemsize


class Late:
    def __init__(self, source, target, done):
        self.copy, self.target, self.open = pltpu.make_async_copy(source, target, done), target, True
        self.copy.start()

    def ready(self):
        if self.open:
            self.copy.wait()
        self.open = False
        return self.target


class Early:
    def __init__(self, source, target, done):
        self.copy, self.source, self.sent = pltpu.make_async_copy(source, target, done), source, False

    def send(self):
        if not self.sent:
            self.copy.start()
        self.sent = True


def call(kernel, coords, ins, outs, scratch, late=(), early=(), least=0, wait=()):
    ins = list(ins)
    n_ins, n_outs, n_scratch = len(ins), len(outs), len(scratch)
    moving = [(ins[i].shape, ins[i].dtype) for i in late] + [outs[i] for i in early]

    def run(coords, *refs):
        refs = list(refs)
        del refs[n_ins : n_ins + len(wait)]
        done = refs.pop() if moving else None
        buffers = refs[n_ins + n_outs + n_scratch :]
        refs = refs[: n_ins + n_outs + n_scratch]
        for k, i in enumerate(late):
            refs[i] = Late(refs[i], buffers[k], done.at[k])
        sending = []
        for k, i in enumerate(early):
            k += len(late)
            sending.append(Early(buffers[k], refs[n_ins + i], done.at[k]))
            refs[n_ins + i] = sending[-1]
        kernel(coords, *refs)
        for i in late:
            refs[i].ready()
        for out in sending:
            out.send()
        for out in sending:
            out.copy.wait()

    need = sum(held_bytes(a.shape, a.dtype) for a in ins) + sum(held_bytes(*o) for o in [*outs, *scratch])
    anywhere = pl.BlockSpec(memory_space=pltpu.HBM)
    buffers = [pltpu.VMEM(shape, kind) for shape, kind in [*scratch, *moving]]
    return pl.pallas_call(
        run,
        out_shape=[jax.ShapeDtypeStruct(shape, kind) for shape, kind in outs],
        in_specs=[SMEM] + [anywhere if i in late else VMEM for i in range(n_ins)] + [pl.BlockSpec(memory_space=pl.ANY)] * len(wait),
        out_specs=[anywhere if i in early else VMEM for i in range(n_outs)],
        scratch_shapes=buffers + ([pltpu.SemaphoreType.DMA((len(moving),))] if moving else []),
        compiler_params=pltpu.CompilerParams(vmem_limit_bytes=max(need + 8 * 2**20, least * 2**20)),
        cost_estimate=pl.CostEstimate(flops=1, bytes_accessed=1, transcendentals=0),
    )(coords, *ins, *wait)


def lanes(index, width):
    return pl.ds(pl.multiple_of(index * width, LANES), width)


def rows(index, height):
    return pl.ds(pl.multiple_of(index * height, 16), height)


def inverse_rms(value):
    return lax.rsqrt(jnp.mean(value * value, -1, keepdims=True) + EPS)


def norm_back(grad, normal, inverse):
    return inverse * (grad - normal * jnp.mean(grad * normal, -1, keepdims=True))


def cut_kernel(widths, coords, *refs):
    ins, outs = refs[: len(widths)], refs[-4:]
    small = refs[len(widths) : -4]
    j = coords[2]
    for out, r in zip(outs, (1, 3, 2, 0)):
        at = 0
        for w, n in zip(ins, widths):
            out[0:256, at : at + n] = w[:, lanes(j ^ r, n)].astype(LOW)
            at += n
    if small:
        heads, line = small
        line = jnp.concatenate([line[...], jnp.zeros((15, 768), FULL)], 0)
        tile = jnp.concatenate([heads[...], line], 1).astype(LOW)
        for out in outs:
            out[256:272, :] = tile


def take_columns(coords, weights, widths, small=()):
    shape = (272 if small else 256, sum(widths))
    outs = [(shape, LOW)] * 4
    beside, across, other, mine = call(
        functools.partial(cut_kernel, widths), coords, [*weights, *small], outs, [], least=50
    )
    return mine, swap(beside, "core"), other, swap(across, "core")


def first_kernel(coords, t0, t1, t2, t3, w0, w1, w2, w3, wo, cos, sin, segs, bias, *refs):
    (keep, send, attn_in, raw, qk, val, probs, attended, gates, mixed, hw, gains, cos_rel, sin_rel) = refs[:14]
    (wo_low, mask) = refs[14:]
    (attn_out, raw_out, qk_out, val_out, probs_out, att_out, gates_out, mixed_out) = refs[2:10]
    attn_in, raw, qk, val, probs, attended, gates, mixed = [r.source for r in refs[2:10]]
    cos_out, sin_out = refs[12:14]
    cos_rel, sin_rel = cos_out.source, sin_out.source
    j = coords[2]
    tokens, weights = (t0, t1, t2, t3), (w0, w1, w2, w3)
    hw[...] = jnp.zeros_like(hw)
    gains[...] = jnp.zeros_like(gains)
    gain_q, gain_k = jnp.zeros((16, LANES), FULL), jnp.zeros((16, LANES), FULL)
    for r in range(4):
        small = weights[r][256:272, :]
        hw[0:16, lanes(j ^ r, 256)] = small[:, 0:256]
        small = small[:, 256:].astype(FULL)
        gains[0:1, lanes(j ^ r, 256)] = small[0:1, 0:256]
        gains[1:2, lanes(j ^ r, 256)] = small[0:1, 256:512]
        gain_q += pltpu.roll(small[:, 512:640], (j ^ r) * 32, 1)
        gain_k += pltpu.roll(small[:, 640:768], (j ^ r) * 32, 1)
        cos_rel[r * 128 : r * 128 + 128, :] = cos.ready()[rows(j ^ r, 128), :]
        sin_rel[r * 128 : r * 128 + 128, :] = sin.ready()[rows(j ^ r, 128), :]
    gains[2:3, 0:128] = gain_q[0:1]
    gains[2:3, 128:256] = gain_k[0:1]
    for r in range(4):
        x = tokens[r][0:128, :].astype(FULL)
        attn_in[r * 128 : r * 128 + 128, :] = (x * inverse_rms(x) * gains[0:1, :]).astype(LOW)

    attn_out.send()
    cos_out.send()
    sin_out.send()

    logit = dot_t(attn_in[...], hw[...])
    logit = pltpu.roll(logit, (32 - j) * 4 & 127, 1) + bias[...].astype(LOW).astype(FULL)
    gates[...] = jax.nn.sigmoid(logit)
    gates_out.send()
    for n in range(4):
        total = dot(attn_in[:, lanes(j, 256)], w0[0:256, n * 256 : n * 256 + 256])
        for r in range(1, 4):
            total += dot(attn_in[:, lanes(j ^ r, 256)], weights[r][0:256, n * 256 : n * 256 + 256])
        if n < 3:
            raw[:, n * 256 : n * 256 + 256] = total
        else:
            val[...] = total.astype(LOW)
    raw_out.send()
    val_out.send()
    for h in range(6):
        at = slice(h * 128, h * 128 + 128)
        part = raw[:, at]
        gain = gains[2:3, 0:128] if h < 4 else gains[2:3, 128:256]
        part = part * inverse_rms(part) * gain
        qk[:, at] = (part * cos_rel[...] + pltpu.roll(part, 64, 1) * sin_rel[...]).astype(LOW)

    qk_out.send()
    lane = lax.broadcasted_iota(jnp.int32, (128, 128), 1)
    line = lax.broadcasted_iota(jnp.int32, (128, 128), 0)
    for c in range(4):
        seg_q = jnp.broadcast_to(segs[pl.ds(j ^ c, 1), :], (128, 128)).T
        for b in range(4):
            seg_k = segs[pl.ds(j ^ b, 1), :]
            earlier = lane + (j ^ b) * 128 <= line + (j ^ c) * 128
            mask[c * 128 : c * 128 + 128, b * 128 : b * 128 + 128] = jnp.where(
                earlier & (seg_q == seg_k), 0.0, MASKED
            )
    for h in range(4):
        kv = h // 2
        for c in range(2):
            at = slice(c * 256, c * 256 + 256)
            scores = dot_t(qk[at, h * 128 : h * 128 + 128], qk[:, 512 + kv * 128 : 640 + kv * 128])
            scores = scores * SCALE + mask[at, :]
            expo = jnp.exp(scores - jnp.max(scores, -1, keepdims=True))
            part = (expo / jnp.sum(expo, -1, keepdims=True)).astype(LOW)
            probs[h, at, :] = part
            result = dot(part, val[:, kv * 128 : kv * 128 + 128])
            attended[at, h * 128 : h * 128 + 128] = result
            mixed[at, h * 128 : h * 128 + 128] = (result * gates[at, h : h + 1]).astype(LOW)
    probs_out.send()
    att_out.send()
    mixed_out.send()
    wo_low[...] = wo.ready()[...].astype(LOW)
    for n in range(4):
        at = slice(n * 256, n * 256 + 256)
        result = dot(mixed[...], wo_low[:, at])
        for c in range(2):
            keep[c, :, at] = result[c * 256 : c * 256 + 128]
            send[c, :, at] = result[c * 256 + 128 : c * 256 + 256].astype(LOW)


def attention_forward(coords, tokens, weights, wo, cos, sin, segs, bias):
    outs = [
        ((2, 128, 1024), FULL),
        ((2, 128, 1024), LOW),
        ((512, 1024), LOW),
        ((512, 768), FULL),
        ((512, 768), LOW),
        ((512, 256), LOW),
        ((4, 512, 512), LOW),
        ((512, 512), FULL),
        ((512, 128), FULL),
        ((512, 512), LOW),
        ((128, 1024), LOW),
        ((8, 1024), FULL),
        ((512, 128), FULL),
        ((512, 128), FULL),
    ]
    return call(
        first_kernel,
        coords,
        [*tokens, *weights, wo, cos, sin, segs, bias],
        outs,
        [((512, 1024), LOW), ((512, 512), FULL)],
        (9, 10, 8),
        (2, 3, 4, 5, 6, 7, 8, 9, 12, 13),
    )


def ffn_kernel(coords, f_own, f_got, w0, w1, w2, w3, wd, g0, g1, g2, g3, *refs):
    (keep, send, ffn, grads, grad_gu, act, wd_low) = refs
    j = coords[2]
    weights = (w0, w1, w2, w3)
    for r, g in enumerate((g0, g1, g2, g3)):
        ffn[r * 128 : r * 128 + 128, :] = (f_got if r % 2 else f_own)[r // 2]
        grads[r * 128 : r * 128 + 128, :] = g[...]
    wd_low[...] = wd[...].astype(LOW)
    for m in range(2):
        at = slice(m * 256, m * 256 + 256)
        for n in range(3):
            low, high = slice(n * 256, n * 256 + 256), slice(768 + n * 256, 1024 + n * 256)
            gate = dot(ffn[at, lanes(j, 256)], w0[:, low])
            up = dot(ffn[at, lanes(j, 256)], w0[:, high])
            for r in range(1, 4):
                gate += dot(ffn[at, lanes(j ^ r, 256)], weights[r][:, low])
                up += dot(ffn[at, lanes(j ^ r, 256)], weights[r][:, high])
            back = dot_t(grads[at, :], wd_low[low, :])
            sigma = jax.nn.sigmoid(gate)
            swish = gate * sigma
            act[at, low] = (swish * up).astype(LOW)
            grad_gu[at, low] = (back * up * sigma * (1.0 + gate * (1.0 - sigma))).astype(LOW)
            grad_gu[at, high] = (back * swish).astype(LOW)
    for r in range(4):
        part = dot_t(grad_gu[...], weights[r][...])
        for t in range(2):
            keep[t, :, lanes(j ^ r, 256)] = part[t * 256 : t * 256 + 128]
            send[t, :, lanes(j ^ r, 256)] = part[t * 256 + 128 : t * 256 + 256].astype(LOW)


def feed_forward(coords, ffn_in, weights, wd, grads):
    outs = [
        ((2, 128, 1024), FULL),
        ((2, 128, 1024), LOW),
        ((512, 1024), LOW),
        ((512, 1024), LOW),
        ((512, 1536), LOW),
        ((512, 768), LOW),
        ((768, 1024), LOW),
    ]
    return call(
        ffn_kernel,
        coords,
        [*ffn_in, *weights, wd, *grads],
        outs,
        [],
    )


def down_kernel(coords, act, wd_low, keep, send):
    for c in range(4):
        result = dot(act[c * 128 : c * 128 + 128, :], wd_low[...])
        if c % 2:
            send[c // 2] = result.astype(LOW)
        else:
            keep[c // 2] = result


def down(coords, act, wd_low, wait):
    outs = [((2, 128, 1024), FULL), ((2, 128, 1024), LOW)]
    return call(down_kernel, coords, [act, wd_low], outs, [], wait=wait)


def back_kernel(coords, *refs):
    (l_own, l_got, wo, qk, val, probs, attended, gates, raw, attn_in, hw) = refs[:11]
    (w0, w1, w2, w3, t0, t1, t2, t3, gains, cos, sin, gain_second) = refs[11:23]
    (keep, send, grad_qkv, small, resid_low) = refs[23:28]
    (wo_low, grad_scores) = refs[28:]
    j = coords[2]
    wo_low[...] = wo.ready()[...].astype(LOW)
    for r in range(4):
        resid_low[r * 128 : r * 128 + 128, :] = (l_got if r % 2 else l_own)[r // 2]
    lane = lax.broadcasted_iota(jnp.int32, (512, LANES), 1)
    grad_logit = jnp.zeros((512, LANES), FULL)
    gain_sums = []
    gates, attended, val, probs, qk, raw = [r.ready() for r in (gates, attended, val, probs, qk, raw)]
    cos, sin, gains = [r.ready() for r in (cos, sin, gains)]

    def head_back(grad, at, gain):
        part = raw[:, at]
        inverse = inverse_rms(part)
        normal = part * inverse
        turned = grad * cos[...] - pltpu.roll(grad, 64, 1) * sin[...]
        gain_sums.append(jnp.sum(turned * normal, 0, keepdims=True))
        grad_qkv[:, at] = norm_back(turned * gain, normal, inverse).astype(LOW)

    for kv in range(2):
        key_at = slice(512 + kv * 128, 640 + kv * 128)
        grad_key = grad_value = None
        for h in (2 * kv, 2 * kv + 1):
            at = slice(h * 128, h * 128 + 128)
            grad_mixed = dot_t(resid_low[...], wo_low[at, :])
            gate = gates[:, h : h + 1]
            grad_gate = jnp.sum(grad_mixed * attended[:, at], -1, keepdims=True) * gate * (1.0 - gate)
            grad_logit = jnp.where(lane == h, grad_gate, grad_logit)
            grad_att = (grad_mixed * gate).astype(LOW)
            for c in range(2):
                line = slice(c * 256, c * 256 + 256)
                grad_probs = dot_t(grad_att[line], val[:, kv * 128 : kv * 128 + 128])
                part = probs[h, line, :].astype(FULL)
                inner = jnp.sum(part * grad_probs, -1, keepdims=True)
                grad_scores[line, :] = (part * (grad_probs - inner)).astype(LOW)
            head_back(dot(grad_scores[...], qk[:, key_at]) * SCALE, at, gains[2:3, 0:128])
            more_key = dot_tn(grad_scores[...], qk[:, at])
            more_value = dot_tn(probs[h], grad_att)
            grad_key = more_key if grad_key is None else grad_key + more_key
            grad_value = more_value if grad_value is None else grad_value + more_value
        head_back(grad_key * SCALE, key_at, gains[2:3, 128:256])
        grad_qkv[:, 768 + kv * 128 : 896 + kv * 128] = grad_value.astype(LOW)

    weights, tokens = [[r.ready() for r in group] for group in ((w0, w1, w2, w3), (t0, t1, t2, t3))]
    attn_in, hw = attn_in.ready(), hw.ready()
    grad_logit = grad_logit.astype(LOW)
    grad_bias = jnp.sum(grad_logit.astype(FULL), 0, keepdims=True)
    grad_hw = dot_tn(grad_logit, attn_in[...])
    spread_logit = pltpu.roll(grad_logit.astype(FULL), j * 4, 1).astype(LOW)
    inverses = []
    for r in range(4):
        x = tokens[r][0:128, :].astype(FULL)
        inverses.append(inverse_rms(x))
    small[...] = jnp.zeros_like(small)

    def put(row, value):
        small[row // 4, row % 4 : row % 4 + 1, :] = value

    for r in range(4):
        at = lanes(j ^ r, 256)
        part = dot_t(grad_qkv[...], weights[r][0:256, :]) + dot(spread_logit, hw[:, at])
        total = jnp.zeros((1, 256), FULL)
        for t in range(4):
            piece = part[t * 128 : t * 128 + 128]
            normal = tokens[t][0:128, at].astype(FULL) * inverses[t]
            total += jnp.sum(piece * normal, 0, keepdims=True)
            if t % 2:
                send[t // 2, :, at] = piece.astype(LOW)
            else:
                keep[t // 2, :, at] = piece
        block = (j ^ r) // 2
        for i in range(2):
            small[block, pl.ds((j ^ r) % 2 * 2 + i, 1), :] = total[:, i * 128 : i * 128 + 128]
    for i in range(8):
        put(8 + i, gain_second[0:1, i * 128 : i * 128 + 128])
    put(16, gain_sums[0] + gain_sums[1] + gain_sums[3] + gain_sums[4])
    put(17, gain_sums[2] + gain_sums[5])
    put(18, grad_bias)
    for h in range(4):
        for i in range(8):
            put(24 + h * 8 + i, grad_hw[h : h + 1, i * 128 : i * 128 + 128])


def attention_backward(coords, ins):
    outs = [
        ((2, 128, 1024), FULL),
        ((2, 128, 1024), LOW),
        ((512, 1024), LOW),
        ((16, 8, 128), FULL),
        ((512, 1024), LOW),
    ]
    scratch = [((512, 1024), LOW), ((512, 512), LOW)]
    return call(back_kernel, coords, ins, outs, scratch, range(2, 22))


def spread_kernel(with_small, coords, left_c, right_own, right_got, left_r, right_r, *refs):
    if with_small:
        small_own, small_got, *refs = refs
    outs, (turned_c, turned_r, held_c, held_r) = refs[:4], refs[4:]
    first, second, j = coords[0], coords[1], coords[2]
    panels = right_own.shape[1] // LANES
    rows_r = left_r.shape[1] // 16
    part = 2 * panels * 16 + (16 if with_small else 0)
    spots = [((first ^ m) * 4 + (second ^ n), outs[m], n) for m in (1, 2, 3, 0) for n in range(4)]
    for d in range(2):
        turned = left_c[:, lanes(j ^ (2 * d), 256)].T
        turned_c[d] = turned
        for t in range(4):
            turned_c[2 + d, :, t * 128 : t * 128 + 128] = turned[:, (t ^ 1) * 128 : (t ^ 1) * 128 + 128]
    turned_r[...] = left_r[...].T
    for src, right in enumerate((right_own, right_got)):
        for d in range(2):
            held_c[...] = dot(turned_c[2 * src + d], right[...]).astype(LOW)
            for block, out, n in spots:
                for p in range(panels):
                    low = (1 - d) * part + (src * panels + p) * 16
                    out[n, low : low + 16, :] = held_c[rows(block, 16), p * LANES : (p + 1) * LANES]
    held_r[...] = dot(turned_r[...], right_r[...]).astype(LOW)
    for block, out, n in spots:
        if with_small:
            tile = jnp.concatenate([small_own[block], small_got[block]], 0).astype(LOW)
            out[n, part - 16 : part, :] = tile
            out[n, 2 * part - 16 : 2 * part, :] = tile
        for p in range(8):
            low = 2 * part + p * rows_r
            out[n, low : low + rows_r, :] = held_r[rows(block, rows_r), p * LANES : (p + 1) * LANES]


def spread(coords, left_c, right_own, right_got, left_r, right_r, small=()):
    panels = right_own.shape[1] // LANES
    part = 2 * panels * 16 + (16 if small else 0)
    height = 2 * part + left_r.shape[1] // 2
    scratch = [
        ((4, 256, 512), LOW),
        ((left_r.shape[1], 512), LOW),
        ((256, panels * LANES), LOW),
        ((left_r.shape[1], 1024), LOW),
    ]
    pieces = call(
        functools.partial(spread_kernel, bool(small)),
        coords,
        [left_c, right_own, right_got, left_r, right_r, *small],
        [((4, height, LANES), LOW)] * 4,
        scratch,
    )
    return pieces, part


def first_sum_kernel(coords, a, b, c, d, *outs):
    for n in range(4):
        outs[n][...] = (a[n].astype(FULL) + b[n].astype(FULL) + c[n].astype(FULL) + d[n].astype(FULL)).astype(LOW)


def second_sum_kernel(coords, a, b, c, d, other, mine):
    total = (a[...].astype(FULL) + b[...].astype(FULL) + c[...].astype(FULL) + d[...].astype(FULL)).astype(LOW)
    part = other.shape[0]
    other[...] = total[:part]
    mine[...] = total[part:]


def third_sum_kernel(coords, ahead, behind, mine, far, out):
    part = ahead.shape[0]
    out[0:part, :] = (ahead[...].astype(FULL) + behind[...].astype(FULL)).astype(LOW)
    out[part:, :] = (mine[...].astype(FULL) + far[...].astype(FULL)).astype(LOW)


def pack_kernel(coords, a, b, c, d, out):
    for n, ref in enumerate((a, b, c, d)):
        out[n] = ref[...]


def send_first(pieces):
    return [pieces[0]] + [swap_plane(pieces[m], 0, m) for m in (1, 2, 3)]


def send_second(parts):
    return [parts[0]] + [swap_plane(parts[m], 1, m) for m in (1, 2, 3)]


def send_across(other, mine):
    return [turn(other, 1), turn(other, -1), mine, turn(mine, 2)]


def send_back(held, axis):
    return [held] + [swap_plane(held, axis, m) for m in (1, 2, 3)]


def first_sum(coords, got, wait=()):
    height = got[0].shape[1]
    return call(first_sum_kernel, coords, got, [((height, LANES), LOW)] * 4, [], wait=wait)


def second_sum(coords, got, part):
    outs = [((part, LANES), LOW), ((got[0].shape[0] - part, LANES), LOW)]
    return call(second_sum_kernel, coords, got, outs, [])


def third_sum(coords, got, wait=()):
    outs = [((got[0].shape[0] + got[2].shape[0], LANES), LOW)]
    return call(third_sum_kernel, coords, got, outs, [], wait=wait)[0]


def pack(coords, got, wait=()):
    return call(pack_kernel, coords, got, [((4, *got[0].shape), LOW)], [], wait=wait)[0]


def together(*values):
    return lax.optimization_barrier(values)


def settle_kernel(widths, with_small, coords, *refs):
    ins, outs = refs[:4], refs[4:]
    first, second, j = coords[0], coords[1], coords[2]
    panels = sum(widths) // LANES
    out_r = outs[len(widths)]
    rows_r = out_r.shape[0] // 16
    spots = []
    for t in range(panels):
        col, w = t * LANES, 0
        while col >= widths[w]:
            col, w = col - widths[w], w + 1
        spots.append((w, col))
    if with_small:
        total, heads = refs[-2:]
        total[...] = jnp.zeros_like(total)

    part = 2 * panels * 16 + (16 if with_small else 0)
    for m in range(4):
        for n in range(4):
            block = (first ^ m) * 4 + (second ^ n)
            got = ins[m]
            line = rows(block, 16)
            for r in range(4):
                base = (1 - r // 2) * part + (r % 2) * panels * 16
                for p, (w, col) in enumerate(spots):
                    lane = pl.ds(pl.multiple_of((j ^ r) * widths[w] + col, LANES), LANES)
                    low = base + p * 16
                    outs[w][line, lane] = got[n, low : low + 16, :].astype(FULL)
            for p in range(8):
                low = 2 * part + p * rows_r
                lane = slice(p * LANES, (p + 1) * LANES)
                out_r[rows(block, rows_r), lane] = got[n, low : low + rows_r, :].astype(FULL)
            if with_small:
                for z in range(2):
                    tile = got[n, (1 - z) * part + part - 16 : (1 - z) * part + part, :].astype(FULL)
                    for src in range(2):
                        value = tile[src * 8 : src * 8 + 8]
                        heads[j ^ (2 * z + src), block] = value
                        total[block] += value
    if with_small:
        gain_first, gain_second, gain_q, gain_k, bias, hw = outs[len(widths) + 1 : len(widths) + 7]
        for i in range(2):
            at = slice(i * 128, i * 128 + 128)
            gain_first[:, at] = total[j // 2, pl.ds(j % 2 * 2 + i, 1), :]
            gain_second[:, at] = total[2 + j // 2, pl.ds(j % 2 * 2 + i, 1), :]
        shift = (4 - j) * 32 & 127
        turned = pltpu.roll(total[4], shift, 1)
        gain_q[...] = turned[0:1, :32]
        gain_k[...] = turned[1:2, :32]
        bias[...] = heads[j, 4][2:3, :4]
        lines = []
        for q in range(4):
            for h in range(4):
                start = 24 + h * 8
                lines.append(
                    jnp.concatenate(
                        [heads[q, start // 4 + j // 2, pl.ds(j % 2 * 2 + i, 1), :] for i in range(2)], 1
                    )
                )
        whole = jnp.concatenate(lines + [jnp.zeros((112, 256), FULL)], 0)
        hw[...] = whole.T[:, :16]


def settle(coords, pieces, widths, rows_r, with_small, wait):
    outs = [((256, 4 * w), FULL) for w in widths] + [((rows_r, 1024), FULL)]
    scratch = []
    if with_small:
        outs += [((1, n), FULL) for n in (256, 256, 32, 32, 4)] + [((256, 16), FULL)]
        scratch = [((16, 8, 128), FULL), ((4, 16, 8, 128), FULL)]
    return call(functools.partial(settle_kernel, widths, with_small), coords, pieces, outs, scratch, wait=wait)


def group_gather(part):
    beside = swap(part, "core")
    across = swap(part, "zl")
    return part, beside, across, swap(across, "core")


def add_kernel(coords, keep, got, total, low):
    value = keep[...] + got[...].astype(FULL)
    total[...] = value
    low[...] = value.astype(LOW)


def chip_sum(coords, keep, send, wait=()):
    outs = [((2, 128, 1024), FULL), ((2, 128, 1024), LOW)]
    return call(add_kernel, coords, [keep, swap(send, "core")], outs, [], wait=wait)


def group_scatter(coords, keep, send, wait):
    total, low = chip_sum(coords, keep, send, wait)
    return total[0] + swap(low[1], "zl").astype(FULL)


def resid_kernel(coords, total, got, h0, h2, gains, resid, low):
    for d, hidden in enumerate((h0, h2)):
        value = hidden[...].astype(FULL) + (total[d] + got[1 - d].astype(FULL))
        resid[d] = value
        low[d] = (value * inverse_rms(value) * gains[1:2, :]).astype(LOW)


def residual(coords, total, got, h0, h2, gains):
    outs = [((2, 128, 1024), FULL), ((2, 128, 1024), LOW)]
    return call(resid_kernel, coords, [total, got, h0, h2, gains], outs, [])


def turn_kernel(coords, total, got, g0, g2, resid, gains, grad_resid, low, gain_sum):
    for d, upstream in enumerate((g0, g2)):
        value = resid[d]
        inverse = inverse_rms(value)
        normal = value * inverse
        grad = total[d] + got[1 - d].astype(FULL)
        back = upstream[...].astype(FULL) + norm_back(grad * gains[1:2, :], normal, inverse)
        low[d] = back.astype(LOW)
        if d == 0:
            grad_resid[...] = back
            gain_sum[...] = jnp.sum(grad * normal, 0, keepdims=True)


def turn_back(coords, total, got, g0, g2, resid, gains, wait):
    outs = [((128, 1024), FULL), ((2, 128, 1024), LOW), ((1, 1024), FULL)]
    return call(turn_kernel, coords, [total, got, g0, g2, resid, gains], outs, [], wait=wait)


def body(
    hidden,
    cotangent,
    segment_ids,
    positions,
    attention_gain,
    query_weight,
    key_weight,
    value_weight,
    query_gain,
    key_gain,
    headgate_weight,
    headgate_bias,
    output_weight,
    feedforward_gain,
    gate_weight,
    up_weight,
    down_weight,
):
    core = lax.axis_index("core")
    x_at, y_at = lax.axis_index("x"), lax.axis_index("y")
    j = lax.axis_index("zl") * 2 + core
    coords = jnp.stack([jnp.where(core == 0, x_at, y_at), jnp.where(core == 0, y_at, x_at), j]).astype(jnp.int32)

    across = swap(hidden, "zl")
    cut_gu, got_gu, other_gu, across_gu = take_columns(coords, (gate_weight, up_weight), (768, 768))
    across, cut_gu, query_weight, key_weight, value_weight = together(
        across, cut_gu, query_weight, key_weight, value_weight
    )
    tokens = (hidden, swap(hidden, "core"), across, swap(across, "core"))
    line = [attention_gain, feedforward_gain, jnp.pad(query_gain, (0, 96)), jnp.pad(key_gain, (0, 96))]
    small = (headgate_weight.T, jnp.concatenate(line)[None])
    mine, got, other, across = take_columns(coords, (query_weight, key_weight, value_weight), (512, 256, 256), small)
    weight_qkv = [mine, got, swap_far(other), swap(across, "zl")]
    mine, got, other, across = cut_gu, got_gu, other_gu, across_gu
    weight_qkv[2], other = together(weight_qkv[2], other)
    weight_gu = [mine, got, swap_far(other), across]
    weight_qkv[3], cotangent = together(weight_qkv[3], cotangent)
    grads = list(group_gather(cotangent))

    freq = jnp.power(jnp.float32(THETA), -jnp.arange(64, dtype=FULL) * 2.0 / HEAD)
    angle = positions.astype(FULL)[:, None] * freq[None, :]
    cosine, sine = jnp.cos(angle), jnp.sin(angle)
    cosine, sine = jnp.concatenate([cosine, cosine], 1), jnp.concatenate([-sine, sine], 1)
    bias = jnp.pad(headgate_bias, (0, 124))[None]

    (keep, send, attn_in, raw, qk, val, probs, attended, gates, mixed, hw, gains, cosine, sine) = attention_forward(
        coords, tokens, weight_qkv, output_weight, cosine, sine, segment_ids.reshape(4, 128), bias
    )
    weight_gu[2], late = together(weight_gu[2], weight_gu[3])
    weight_gu[3] = swap_far(late)
    weight_gu[2], grads[2], send = together(weight_gu[2], grads[2], send)
    total, low = chip_sum(coords, keep, send)
    got = swap(low, "zl")
    resid, ffn_in = residual(coords, total, got, tokens[0], tokens[2], gains)
    keep, send, ffn, grads_all, grad_gu, act, wd_low = feed_forward(
        coords, (ffn_in, swap(ffn_in, "core")), weight_gu, down_weight, grads
    )
    total, low = chip_sum(coords, keep, send)
    low, grad_gu = together(low, grad_gu)
    pieces, part = spread(coords, ffn, grad_gu, swap(grad_gu, "core"), act, grads_all)
    got = swap(low, "zl")
    first = send_first(pieces)
    grad_resid, resid_low, grad_gain_second = turn_back(
        coords, total, got, grads[0], grads[2], resid, gains, (pieces[0],)
    )
    keep, send, grad_qkv, small, resid_low = attention_backward(
        coords,
        [resid_low, swap(resid_low, "core"), output_weight, qk, val, probs, attended, gates, raw, attn_in, hw]
        + [*weight_qkv, *tokens, gains, cosine, sine, grad_gain_second],
    )
    pieces, part_second = spread(
        coords, attn_in, grad_qkv, swap(grad_qkv, "core"), mixed, resid_low, (small, swap(small, "core"))
    )
    first = first_sum(coords, first, (pieces[0],))
    first = second_sum(coords, send_second(first), part)
    first, pieces = together(first, pieces)
    second = send_first(pieces)
    first = third_sum(coords, send_across(*first), (second[1],))
    first = pack(coords, send_back(first, 1), second[2:])
    second = first_sum(coords, second)
    near = [swap_plane(first, 0, m) for m in (1, 3)]
    second = second_sum(coords, send_second(second), part_second)
    second = third_sum(coords, send_across(*second), near)
    first, near = together(first, near)
    first = [first, near[0], swap_plane(first, 0, 2), near[1]]
    output = (resid[0] + group_scatter(coords, *down(coords, act, wd_low, (second,)), ())).astype(LOW)
    mine = group_scatter(coords, keep, send, (second,))
    second = pack(coords, send_back(second, 1))
    grad_g, grad_u, grad_d = settle(coords, first, (768, 768), 768, False, (second,))
    second = send_back(second, 0)
    own = hidden.astype(FULL)
    inv_own = inverse_rms(own)
    input_grad = (grad_resid + norm_back(mine * gains[0], own * inv_own, inv_own)).astype(LOW)

    (grad_q, grad_k, grad_v, grad_o, small_first, small_second, small_q, small_k, small_bias, grad_hw) = settle(
        coords, second, (512, 256, 256), 512, True, (grad_d,)
    )
    return (
        output,
        input_grad,
        small_first.reshape(256),
        grad_q,
        grad_k,
        grad_v,
        small_q.reshape(32),
        small_k.reshape(32),
        grad_hw,
        small_bias.reshape(4),
        grad_o,
        small_second.reshape(256),
        grad_g,
        grad_u,
        grad_d,
    )


def solution(mesh):
    grid = Mesh(mesh.devices.reshape(2, 4, 4, 2, 2), AXES)
    tokens, split, copies = P(AXES, None), P(GROUP, None), P(("zh", "y", "x"))
    line = P(GROUP)
    weights = (line, split, split, split, line, line, split, line, split, line, split, split, split)
    return jax.shard_map(
        body,
        mesh=grid,
        in_specs=(tokens, tokens, copies, copies, *weights),
        out_specs=(tokens, tokens, *weights),
        check_vma=False,
    )
```

```python
import functools
import math

import jax
import jax.numpy as jnp
from jax import lax
from jax.experimental import pallas as pl
from jax.experimental.pallas import tpu as pltpu
from jax.sharding import Mesh
from jax.sharding import PartitionSpec as P

EPS = 1e-06
THETA = 1000000.0
MASKED = -1e30
HEAD = 128
SCALE = 1.0 / math.sqrt(HEAD)
LOW = jnp.bfloat16
FULL = jnp.float32
AXES = ("zh", "y", "x", "zl", "core")
GROUP = ("zl", "core")
LANES = 128


def swap(value, axis):
    return lax.ppermute(value, axis, [(0, 1), (1, 0)])


def turn(value, step):
    return lax.ppermute(value, ("zh", "zl"), [(i, (i + step) % 4) for i in range(4)])


def swap_far(value):
    return lax.ppermute(value, ("zh", "zl"), [(0, 3), (3, 0), (1, 2), (2, 1)])


def swap_plane(value, axis, mask):
    pairs = []
    for y in range(4):
        for x in range(4):
            for core in range(2):
                to_y, to_x = (y, x ^ mask) if axis == core else (y ^ mask, x)
                pairs.append(((y * 4 + x) * 2 + core, (to_y * 4 + to_x) * 2 + core))
    return lax.ppermute(value, ("y", "x", "core"), pairs)


def dot(left, right):
    return jnp.dot(left, right, preferred_element_type=FULL)


def dot_t(left, right):
    return lax.dot_general(left, right, (((1,), (1,)), ((), ())), preferred_element_type=FULL)


def dot_tn(left, right):
    return lax.dot_general(left, right, (((0,), (0,)), ((), ())), preferred_element_type=FULL)


VMEM = pl.BlockSpec(memory_space=pltpu.VMEM)
SMEM = pl.BlockSpec(memory_space=pltpu.SMEM)


def held_bytes(shape, kind):
    shape = (1,) * (2 - len(shape)) + tuple(shape)
    size = math.prod(shape[:-2]) * (-(-shape[-2] // 16) * 16) * (-(-shape[-1] // LANES) * LANES)
    return size * jnp.dtype(kind).itemsize


class Late:
    def __init__(self, source, target, done):
        self.copy, self.target, self.open = pltpu.make_async_copy(source, target, done), target, True
        self.copy.start()

    def ready(self):
        if self.open:
            self.copy.wait()
        self.open = False
        return self.target


class Early:
    def __init__(self, source, target, done):
        self.copy, self.source, self.sent = pltpu.make_async_copy(source, target, done), source, False

    def send(self):
        if not self.sent:
            self.copy.start()
        self.sent = True


def call(kernel, coords, ins, outs, scratch, late=(), early=(), least=0, wait=(), flops=1):
    ins = list(ins)
    n_ins, n_outs, n_scratch = len(ins), len(outs), len(scratch)
    moving = [(ins[i].shape, ins[i].dtype) for i in late] + [outs[i] for i in early]

    def run(coords, *refs):
        refs = list(refs)
        del refs[n_ins : n_ins + len(wait)]
        done = refs.pop() if moving else None
        buffers = refs[n_ins + n_outs + n_scratch :]
        refs = refs[: n_ins + n_outs + n_scratch]
        for k, i in enumerate(late):
            refs[i] = Late(refs[i], buffers[k], done.at[k])
        sending = []
        for k, i in enumerate(early):
            k += len(late)
            sending.append(Early(buffers[k], refs[n_ins + i], done.at[k]))
            refs[n_ins + i] = sending[-1]
        kernel(coords, *refs)
        for i in late:
            refs[i].ready()
        for out in sending:
            out.send()
        for out in sending:
            out.copy.wait()

    need = sum(held_bytes(a.shape, a.dtype) for a in ins) + sum(held_bytes(*o) for o in [*outs, *scratch])
    anywhere = pl.BlockSpec(memory_space=pltpu.HBM)
    buffers = [pltpu.VMEM(shape, kind) for shape, kind in [*scratch, *moving]]
    return pl.pallas_call(
        run,
        out_shape=[jax.ShapeDtypeStruct(shape, kind) for shape, kind in outs],
        in_specs=[SMEM] + [anywhere if i in late else VMEM for i in range(n_ins)] + [pl.BlockSpec(memory_space=pl.ANY)] * len(wait),
        out_specs=[anywhere if i in early else VMEM for i in range(n_outs)],
        scratch_shapes=buffers + ([pltpu.SemaphoreType.DMA((len(moving),))] if moving else []),
        compiler_params=pltpu.CompilerParams(vmem_limit_bytes=max(need + 8 * 2**20, least * 2**20)),
        cost_estimate=pl.CostEstimate(flops=flops, bytes_accessed=1, transcendentals=0),
    )(coords, *ins, *wait)


def lanes(index, width):
    return pl.ds(pl.multiple_of(index * width, LANES), width)


def rows(index, height):
    return pl.ds(pl.multiple_of(index * height, 16), height)


def inverse_rms(value):
    return lax.rsqrt(jnp.mean(value * value, -1, keepdims=True) + EPS)


def norm_back(grad, normal, inverse):
    return inverse * (grad - normal * jnp.mean(grad * normal, -1, keepdims=True))


def cut_kernel(widths, small, coords, *refs):
    ins, outs = refs[: len(widths)], refs[len(widths) + 2 * small :]
    j = coords[2]
    if small:
        heads, line = refs[len(widths) : len(widths) + 2]
        line = jnp.concatenate([line[...], jnp.zeros((15, 768), FULL)], 0)
        tile = jnp.concatenate([heads[...], line], 1).astype(LOW)
    third = [(3, 0, 256)] if small else [(3, 0, 128), (3, 128, 128)]
    for out, (r, first, count) in zip(outs, [(1, 0, 256), *third, (2, 0, 256), (0, 0, 256)]):
        at = 0
        for w, n in zip(ins, widths):
            out[0:count, at : at + n] = w[first : first + count, lanes(j ^ r, n)].astype(LOW)
            at += n
        if small:
            out[256:272, :] = tile


def take_columns(coords, weights, widths, small=(), wait=()):
    heights = (272,) * 4 if small else (256, 128, 128, 256, 256)
    beside, *across, other, mine = call(
        functools.partial(cut_kernel, widths, bool(small)),
        coords,
        [*weights, *small],
        [((n, sum(widths)), LOW) for n in heights],
        [],
        least=50,
        wait=wait,
    )
    return mine, swap(beside, "core"), other, *[swap(piece, "core") for piece in across]


def first_kernel(coords, t0, t1, t2, t3, w0, w1, w2, w3, wo, cos, sin, segs, bias, *refs):
    (keep, send, attn_in, raw, qk, val, probs, attended, gates, mixed, hw, gains, cos_rel, sin_rel) = refs[:14]
    (wo_low, mask) = refs[14:]
    (attn_out, raw_out, qk_out, val_out, probs_out, att_out, gates_out, mixed_out) = refs[2:10]
    attn_in, raw, qk, val, probs, attended, gates, mixed = [r.source for r in refs[2:10]]
    cos_out, sin_out = refs[12:14]
    cos_rel, sin_rel = cos_out.source, sin_out.source
    j = coords[2]
    tokens, weights = (t0, t1, t2, t3), (w0, w1, w2, w3)
    hw[...] = jnp.zeros_like(hw)
    gains[...] = jnp.zeros_like(gains)
    gain_q, gain_k = jnp.zeros((16, LANES), FULL), jnp.zeros((16, LANES), FULL)
    for r in range(4):
        small = weights[r][256:272, :]
        hw[0:16, lanes(j ^ r, 256)] = small[:, 0:256]
        small = small[:, 256:].astype(FULL)
        gains[0:1, lanes(j ^ r, 256)] = small[0:1, 0:256]
        gains[1:2, lanes(j ^ r, 256)] = small[0:1, 256:512]
        gain_q += pltpu.roll(small[:, 512:640], (j ^ r) * 32, 1)
        gain_k += pltpu.roll(small[:, 640:768], (j ^ r) * 32, 1)
        cos_rel[r * 128 : r * 128 + 128, :] = cos.ready()[rows(j ^ r, 128), :]
        sin_rel[r * 128 : r * 128 + 128, :] = sin.ready()[rows(j ^ r, 128), :]
    gains[2:3, 0:128] = gain_q[0:1]
    gains[2:3, 128:256] = gain_k[0:1]
    for r in range(4):
        x = tokens[r][0:128, :].astype(FULL)
        attn_in[r * 128 : r * 128 + 128, :] = (x * inverse_rms(x) * gains[0:1, :]).astype(LOW)

    attn_out.send()
    cos_out.send()
    sin_out.send()

    logit = dot_t(attn_in[...], hw[...])
    logit = pltpu.roll(logit, (32 - j) * 4 & 127, 1) + bias[...].astype(LOW).astype(FULL)
    gates[...] = jax.nn.sigmoid(logit)
    gates_out.send()
    for n in range(4):
        total = dot(attn_in[:, lanes(j, 256)], w0[0:256, n * 256 : n * 256 + 256])
        for r in range(1, 4):
            total += dot(attn_in[:, lanes(j ^ r, 256)], weights[r][0:256, n * 256 : n * 256 + 256])
        if n < 3:
            raw[:, n * 256 : n * 256 + 256] = total
        else:
            val[...] = total.astype(LOW)
    raw_out.send()
    val_out.send()
    for h in range(6):
        at = slice(h * 128, h * 128 + 128)
        part = raw[:, at]
        gain = gains[2:3, 0:128] if h < 4 else gains[2:3, 128:256]
        part = part * inverse_rms(part) * gain
        qk[:, at] = (part * cos_rel[...] + pltpu.roll(part, 64, 1) * sin_rel[...]).astype(LOW)

    qk_out.send()
    lane = lax.broadcasted_iota(jnp.int32, (128, 128), 1)
    line = lax.broadcasted_iota(jnp.int32, (128, 128), 0)
    for c in range(4):
        seg_q = jnp.broadcast_to(segs[pl.ds(j ^ c, 1), :], (128, 128)).T
        for b in range(4):
            seg_k = segs[pl.ds(j ^ b, 1), :]
            earlier = lane + (j ^ b) * 128 <= line + (j ^ c) * 128
            mask[c * 128 : c * 128 + 128, b * 128 : b * 128 + 128] = jnp.where(
                earlier & (seg_q == seg_k), 0.0, MASKED
            )
    for h in range(4):
        kv = h // 2
        for c in range(2):
            at = slice(c * 256, c * 256 + 256)
            scores = dot_t(qk[at, h * 128 : h * 128 + 128], qk[:, 512 + kv * 128 : 640 + kv * 128])
            scores = scores * SCALE + mask[at, :]
            expo = jnp.exp(scores - jnp.max(scores, -1, keepdims=True))
            part = (expo / jnp.sum(expo, -1, keepdims=True)).astype(LOW)
            probs[h, at, :] = part
            result = dot(part, val[:, kv * 128 : kv * 128 + 128])
            attended[at, h * 128 : h * 128 + 128] = result
            mixed[at, h * 128 : h * 128 + 128] = (result * gates[at, h : h + 1]).astype(LOW)
    probs_out.send()
    att_out.send()
    mixed_out.send()
    wo_low[...] = wo.ready()[...].astype(LOW)
    for n in range(4):
        at = slice(n * 256, n * 256 + 256)
        result = dot(mixed[...], wo_low[:, at])
        for c in range(2):
            keep[c, :, at] = result[c * 256 : c * 256 + 128]
            send[c, :, at] = result[c * 256 + 128 : c * 256 + 256].astype(LOW)


def attention_forward(coords, tokens, weights, wo, cos, sin, segs, bias):
    outs = [
        ((2, 128, 1024), FULL),
        ((2, 128, 1024), LOW),
        ((512, 1024), LOW),
        ((512, 768), FULL),
        ((512, 768), LOW),
        ((512, 256), LOW),
        ((4, 512, 512), LOW),
        ((512, 512), FULL),
        ((512, 128), FULL),
        ((512, 512), LOW),
        ((128, 1024), LOW),
        ((8, 1024), FULL),
        ((512, 128), FULL),
        ((512, 128), FULL),
    ]
    return call(
        first_kernel,
        coords,
        [*tokens, *weights, wo, cos, sin, segs, bias],
        outs,
        [((512, 1024), LOW), ((512, 512), FULL)],
        (9, 10, 8),
        (2, 3, 4, 5, 6, 7, 8, 9, 12, 13),
    )


def ffn_kernel(coords, f_own, f_got, w0, w1, w2, w3_low, w3_high, wd, g0, g1, g2, g3, *refs):
    (keep, send, ffn, grads, grad_gu, act, wd_low, w3) = refs
    j = coords[2]
    weights = (w0, w1, w2, w3)
    w3[0:128, :] = w3_low[...]
    w3[128:256, :] = w3_high[...]
    for r, g in enumerate((g0, g1, g2, g3)):
        ffn[r * 128 : r * 128 + 128, :] = (f_got if r % 2 else f_own)[r // 2]
        grads[r * 128 : r * 128 + 128, :] = g[...]
    wd_low[...] = wd[...].astype(LOW)
    for m in range(2):
        at = slice(m * 256, m * 256 + 256)
        for n in range(3):
            low, high = slice(n * 256, n * 256 + 256), slice(768 + n * 256, 1024 + n * 256)
            gate = dot(ffn[at, lanes(j, 256)], w0[:, low])
            up = dot(ffn[at, lanes(j, 256)], w0[:, high])
            for r in range(1, 4):
                gate += dot(ffn[at, lanes(j ^ r, 256)], weights[r][:, low])
                up += dot(ffn[at, lanes(j ^ r, 256)], weights[r][:, high])
            back = dot_t(grads[at, :], wd_low[low, :])
            sigma = jax.nn.sigmoid(gate)
            swish = gate * sigma
            act[at, low] = (swish * up).astype(LOW)
            grad_gu[at, low] = (back * up * sigma * (1.0 + gate * (1.0 - sigma))).astype(LOW)
            grad_gu[at, high] = (back * swish).astype(LOW)
    for r in range(4):
        part = dot_t(grad_gu[...], weights[r][...])
        for t in range(2):
            keep[t, :, lanes(j ^ r, 256)] = part[t * 256 : t * 256 + 128]
            send[t, :, lanes(j ^ r, 256)] = part[t * 256 + 128 : t * 256 + 256].astype(LOW)


def feed_forward(coords, ffn_in, weights, wd, grads):
    outs = [
        ((2, 128, 1024), FULL),
        ((2, 128, 1024), LOW),
        ((512, 1024), LOW),
        ((512, 1024), LOW),
        ((512, 1536), LOW),
        ((512, 768), LOW),
        ((768, 1024), LOW),
    ]
    return call(
        ffn_kernel,
        coords,
        [*ffn_in, *weights, wd, *grads],
        outs,
        [((256, 1536), LOW)],
    )


def down_kernel(coords, act, wd_low, keep, send):
    for c in range(4):
        result = dot(act[c * 128 : c * 128 + 128, :], wd_low[...])
        if c % 2:
            send[c // 2] = result.astype(LOW)
        else:
            keep[c // 2] = result


def down(coords, act, wd_low, wait):
    outs = [((2, 128, 1024), FULL), ((2, 128, 1024), LOW)]
    return call(down_kernel, coords, [act, wd_low], outs, [], wait=wait)


def heads_back(kv, refs, resid_low, wo_low, grad_scores, out):
    (qk, val, probs, attended, gates, raw, gains, cos, sin) = refs
    lane = lax.broadcasted_iota(jnp.int32, (512, LANES), 1)
    grad_logit = jnp.zeros((512, LANES), FULL)
    gain_sums = []

    def head_back(grad, at, gain, to):
        part = raw[:, at]
        inverse = inverse_rms(part)
        normal = part * inverse
        turned = grad * cos[...] - pltpu.roll(grad, 64, 1) * sin[...]
        gain_sums.append(jnp.sum(turned * normal, 0, keepdims=True))
        out[:, to : to + 128] = norm_back(turned * gain, normal, inverse).astype(LOW)

    key_at = slice(512 + kv * 128, 640 + kv * 128)
    grad_key = grad_value = None
    for n, h in enumerate((2 * kv, 2 * kv + 1)):
        at = slice(h * 128, h * 128 + 128)
        grad_mixed = dot_t(resid_low[...], wo_low[n * 128 : n * 128 + 128, :])
        gate = gates[:, h : h + 1]
        grad_gate = jnp.sum(grad_mixed * attended[:, at], -1, keepdims=True) * gate * (1.0 - gate)
        grad_logit = jnp.where(lane == h, grad_gate, grad_logit)
        grad_att = (grad_mixed * gate).astype(LOW)
        for c in range(2):
            line = slice(c * 256, c * 256 + 256)
            grad_probs = dot_t(grad_att[line], val[:, kv * 128 : kv * 128 + 128])
            part = probs[h, line, :].astype(FULL)
            inner = jnp.sum(part * grad_probs, -1, keepdims=True)
            grad_scores[line, :] = (part * (grad_probs - inner)).astype(LOW)
        head_back(dot(grad_scores[...], qk[:, key_at]) * SCALE, at, gains[2:3, 0:128], n * 128)
        more_key = dot_tn(grad_scores[...], qk[:, at])
        more_value = dot_tn(probs[h], grad_att)
        grad_key = more_key if grad_key is None else grad_key + more_key
        grad_value = more_value if grad_value is None else grad_value + more_value
    head_back(grad_key * SCALE, key_at, gains[2:3, 128:256], 256)
    out[:, 384:512] = grad_value.astype(LOW)
    return grad_logit, gain_sums


def back_first_kernel(coords, l_own, l_got, wo, qk, val, probs, attended, gates, raw, gains, cos, sin, *refs):
    (out, resid_low, logit, sums, wo_low, grad_scores) = refs
    wo_low[...] = wo.ready()[0:256, :].astype(LOW)
    for r in range(4):
        resid_low[r * 128 : r * 128 + 128, :] = (l_got if r % 2 else l_own)[r // 2]
    refs = [r.ready() for r in (qk, val, probs, attended, gates, raw, gains, cos, sin)]
    grad_logit, gain_sums = heads_back(0, refs, resid_low, wo_low, grad_scores, out)
    logit[...] = grad_logit
    sums[...] = jnp.zeros_like(sums)
    for i, value in enumerate(gain_sums):
        sums[i : i + 1, :] = value


def back_kernel(coords, *refs):
    (resid_low, wo, qk, val, probs, attended, gates, raw, gains, cos, sin, out_first, logit, sums) = refs[:14]
    (attn_in, hw, w0, w1, w2, w3, t0, t1, t2, t3, gain_second) = refs[14:25]
    (keep, send, out, small) = refs[25:29]
    (wo_low, grad_scores, grad_qkv) = refs[29:]
    j = coords[2]
    wo_low[...] = wo.ready()[256:512, :].astype(LOW)
    refs = [r.ready() for r in (qk, val, probs, attended, gates, raw, gains, cos, sin)]
    grad_logit, gain_sums = heads_back(1, refs, resid_low, wo_low, grad_scores, out)
    for kv, part in enumerate((out_first, out)):
        grad_qkv[:, kv * 256 : kv * 256 + 256] = part[:, 0:256]
        grad_qkv[:, 512 + kv * 128 : 640 + kv * 128] = part[:, 256:384]
        grad_qkv[:, 768 + kv * 128 : 896 + kv * 128] = part[:, 384:512]

    weights, tokens = [[r.ready() for r in group] for group in ((w0, w1, w2, w3), (t0, t1, t2, t3))]
    attn_in, hw = attn_in.ready(), hw.ready()
    grad_logit = (grad_logit + logit[...]).astype(LOW)
    grad_bias = jnp.sum(grad_logit.astype(FULL), 0, keepdims=True)
    grad_hw = dot_tn(grad_logit, attn_in[...])
    spread_logit = pltpu.roll(grad_logit.astype(FULL), j * 4, 1).astype(LOW)
    inverses = []
    for r in range(4):
        x = tokens[r][0:128, :].astype(FULL)
        inverses.append(inverse_rms(x))
    small[...] = jnp.zeros_like(small)

    def put(row, value):
        small[row // 4, row % 4 : row % 4 + 1, :] = value

    for r in range(4):
        at = lanes(j ^ r, 256)
        part = dot_t(grad_qkv[...], weights[r][0:256, :]) + dot(spread_logit, hw[:, at])
        total = jnp.zeros((1, 256), FULL)
        for t in range(4):
            piece = part[t * 128 : t * 128 + 128]
            normal = tokens[t][0:128, at].astype(FULL) * inverses[t]
            total += jnp.sum(piece * normal, 0, keepdims=True)
            if t % 2:
                send[t // 2, :, at] = piece.astype(LOW)
            else:
                keep[t // 2, :, at] = piece
        block = (j ^ r) // 2
        for i in range(2):
            small[block, pl.ds((j ^ r) % 2 * 2 + i, 1), :] = total[:, i * 128 : i * 128 + 128]
    for i in range(8):
        put(8 + i, gain_second[0:1, i * 128 : i * 128 + 128])
    put(16, gain_sums[0] + gain_sums[1] + sums[0:1, :] + sums[1:2, :])
    put(17, gain_sums[2] + sums[2:3, :])
    put(18, grad_bias)
    for h in range(4):
        for i in range(8):
            put(24 + h * 8 + i, grad_hw[h : h + 1, i * 128 : i * 128 + 128])


def back_first(coords, resid_low, wo, saved):
    outs = [((512, 512), LOW), ((512, 1024), LOW), ((512, 128), FULL), ((8, 128), FULL)]
    scratch = [((256, 1024), LOW), ((512, 512), LOW)]
    return call(back_first_kernel, coords, [*resid_low, wo, *saved], outs, scratch, range(2, 12), flops=3*10**9)


def back_second(coords, resid_low, wo, saved, first, others, wait):
    outs = [((2, 128, 1024), FULL), ((2, 128, 1024), LOW), ((512, 512), LOW), ((16, 8, 128), FULL)]
    scratch = [((256, 1024), LOW), ((512, 512), LOW), ((512, 1024), LOW)]
    ins = [resid_low, wo, *saved, *first, *others]
    late = [*range(1, 11), *range(14, 24)]
    return call(back_kernel, coords, ins, outs, scratch, late, wait=wait)


KEPT, SENT, MASKS = ((0, 3), (0, 1)), ((1, 2), (3, 2)), ((1, 3), (3, 1))


def spread_kernel(n_right, with_small, coords, left_c, *refs):
    rights, (left_r, right_r, *refs) = refs[: 2 * n_right], refs[2 * n_right :]
    if with_small:
        small_own, small_got, *refs = refs
    outs, (turned_c, turned_r, held_c, held_r) = refs[:4], refs[4:]
    first, second, j = coords[0], coords[1], coords[2]
    wide = rights[0].shape[1] // LANES
    panels = wide * n_right
    rows_r = left_r.shape[1] // 16
    part = 2 * panels * 16 + (16 if with_small else 0)
    edge = outs[0].shape[1]
    blocks = [(m, n, (first ^ m) * 4 + (second ^ n)) for m in (1, 2, 3, 0) for n in range(4)]

    def put(m, n, low, value):
        stream = 0 if low < edge else 1
        sent = m in SENT[stream]
        at = (SENT if sent else KEPT)[stream].index(m) * 4 + n
        low -= edge * stream
        outs[2 * sent + stream][at, low : low + value.shape[0], :] = value

    for d in range(2):
        turned = left_c[:, lanes(j ^ (2 * d), 256)].T
        turned_c[d] = turned
        for t in range(4):
            turned_c[2 + d, :, t * 128 : t * 128 + 128] = turned[:, (t ^ 1) * 128 : (t ^ 1) * 128 + 128]
    turned_r[...] = left_r[...].T
    for k, right in enumerate(rights):
        src, start = k // n_right, k % n_right * wide
        for d in range(2):
            held_c[...] = dot(turned_c[2 * src + d], right[...]).astype(LOW)
            for m, n, block in blocks:
                for p in range(wide):
                    low = (1 - d) * part + (src * panels + start + p) * 16
                    put(m, n, low, held_c[rows(block, 16), p * LANES : (p + 1) * LANES])
    held_r[...] = dot(turned_r[...], right_r[...]).astype(LOW)
    for m, n, block in blocks:
        if with_small:
            tile = jnp.concatenate([small_own[block], small_got[block]], 0).astype(LOW)
            put(m, n, part - 16, tile)
            put(m, n, 2 * part - 16, tile)
        for p in range(8):
            put(m, n, 2 * part + p * rows_r, held_r[rows(block, rows_r), p * LANES : (p + 1) * LANES])


def spread(coords, left_c, own, got, left_r, right_r, small=(), wait=()):
    wide = own[0].shape[1]
    panels = wide * len(own) // LANES
    part = 2 * panels * 16 + (16 if small else 0)
    height = 2 * part + left_r.shape[1] // 2
    scratch = [
        ((4, 256, 512), LOW),
        ((left_r.shape[1], 512), LOW),
        ((256, wide), LOW),
        ((left_r.shape[1], 1024), LOW),
    ]
    pieces = call(
        functools.partial(spread_kernel, len(own), bool(small)),
        coords,
        [left_c, *own, *got, left_r, right_r, *small],
        [((8, height // 2, LANES), LOW)] * 4,
        scratch,
        wait=wait,
    )
    return pieces, part


def plus(a, b):
    return (a.astype(FULL) + b.astype(FULL)).astype(LOW)


def half_sum_kernel(coords, p, q, got_p, got_q, *outs):
    half = p.shape[0] // 2
    for kept, sent, mine, got in ((outs[0], outs[2], p, got_p), (outs[1], outs[3], q, got_q)):
        kept[...] = plus(mine[0:half], got[0:half])
        sent[...] = plus(mine[half:], got[half:])


def turn_sum_kernel(coords, p, q, got_p, got_q, *outs):
    for s, (mine, got) in enumerate(((p, got_p), (q, got_q))):
        for at in range(2):
            outs[s][at] = plus(mine[KEPT[s][at]], got[KEPT[s][at]])
            outs[2 + s][at] = plus(mine[SENT[s][at]], got[SENT[s][at]])


def last_sum_kernel(coords, p, q, got_p, got_q, other, mine):
    part, edge = other.shape[0], p.shape[1]
    p, q = plus(p[0], got_p[0]), plus(q[0], got_q[0])
    other[...] = p[:part]
    mine[0 : edge - part, :] = p[part:]
    mine[edge - part :, :] = q


def cross_sum_kernel(coords, ahead, behind, mine, far, p, q):
    part, edge = ahead.shape[0], p.shape[1]
    p[0, 0:part, :] = plus(ahead[...], behind[...])
    mine = plus(mine[...], far[...])
    p[0, part:, :] = mine[: edge - part]
    q[0] = mine[edge - part :]


def join_kernel(coords, p, q, got_p, got_q, both_p, both_q):
    half = p.shape[0]
    for both, mine, got in ((both_p, p, got_p), (both_q, q, got_q)):
        both[0:half] = mine[...]
        both[half:] = got[...]


def pack_kernel(coords, p, q, got_p, got_q, all_p, all_q):
    for s, (whole, mine, got) in enumerate(((all_p, p, got_p), (all_q, q, got_q))):
        for at in range(2):
            whole[KEPT[s][at]] = mine[at]
            whole[SENT[s][at]] = got[at]


def exchange(pieces, axis, step):
    return [*pieces[:2], *[swap_plane(pieces[2 + s], axis, MASKS[s][step]) for s in range(2)]]


def merge(coords, kernel, got, counts, wait, flops=4 * 10**9):
    outs = [((n, *got[0].shape[1:]), LOW) for n in counts]
    return call(kernel, coords, got, outs, [], wait=wait, flops=flops)


def send_across(other, mine):
    return [turn(other, 1), turn(other, -1), mine, turn(mine, 2)]


def last_sum(coords, got, part, wait):
    outs = [((part, LANES), LOW), ((2 * got[0].shape[1] - part, LANES), LOW)]
    return call(last_sum_kernel, coords, got, outs, [], wait=wait, flops=4 * 10**9)


def cross_sum(coords, got, wait):
    edge = (got[0].shape[0] + got[2].shape[0]) // 2
    return call(cross_sum_kernel, coords, got, [((1, edge, LANES), LOW)] * 2, [], wait=wait, flops=4 * 10**9)


def together(*values):
    return lax.optimization_barrier(values)


def settle_kernel(widths, with_small, coords, *refs):
    ins, outs = refs[:4], refs[4:]
    first, second, j = coords[0], coords[1], coords[2]
    panels = sum(widths) // LANES
    out_r = outs[len(widths)]
    rows_r = out_r.shape[0] // 16
    spots = []
    for kv in range(2 if with_small else 1):
        for w, width in enumerate(widths):
            count = width // LANES // (2 if with_small else 1)
            spots += [(w, (kv * count + i) * LANES) for i in range(count)]
    if with_small:
        total, heads = refs[-2:]
        total[...] = jnp.zeros_like(total)

    part = 2 * panels * 16 + (16 if with_small else 0)
    edge = ins[0].shape[1]

    def take(m, n, low, height):
        stream = 0 if low < edge else 1
        came = m in SENT[stream]
        at = (SENT if came else KEPT)[stream].index(m) * 4 + n
        low -= edge * stream
        return ins[2 * came + stream][at, low : low + height, :].astype(FULL)

    for m in range(4):
        for n in range(4):
            block = (first ^ m) * 4 + (second ^ n)
            line = rows(block, 16)
            for r in range(4):
                base = (1 - r // 2) * part + (r % 2) * panels * 16
                for p, (w, col) in enumerate(spots):
                    lane = pl.ds(pl.multiple_of((j ^ r) * widths[w] + col, LANES), LANES)
                    low = base + p * 16
                    outs[w][line, lane] = take(m, n, low, 16)
            for p in range(8):
                low = 2 * part + p * rows_r
                lane = slice(p * LANES, (p + 1) * LANES)
                out_r[rows(block, rows_r), lane] = take(m, n, low, rows_r)
            if with_small:
                for z in range(2):
                    tile = take(m, n, (1 - z) * part + part - 16, 16)
                    for src in range(2):
                        value = tile[src * 8 : src * 8 + 8]
                        heads[j ^ (2 * z + src), block] = value
                        total[block] += value
    if not with_small:
        outs[-1][...] = jnp.zeros((8, LANES), FULL)
    if with_small:
        gain_first, gain_second, gain_q, gain_k, bias, hw = outs[len(widths) + 1 : len(widths) + 7]
        for i in range(2):
            at = slice(i * 128, i * 128 + 128)
            gain_first[:, at] = total[j // 2, pl.ds(j % 2 * 2 + i, 1), :]
            gain_second[:, at] = total[2 + j // 2, pl.ds(j % 2 * 2 + i, 1), :]
        shift = (4 - j) * 32 & 127
        turned = pltpu.roll(total[4], shift, 1)
        gain_q[...] = turned[0:1, :32]
        gain_k[...] = turned[1:2, :32]
        bias[...] = heads[j, 4][2:3, :4]
        lines = []
        for q in range(4):
            for h in range(4):
                start = 24 + h * 8
                lines.append(
                    jnp.concatenate(
                        [heads[q, start // 4 + j // 2, pl.ds(j % 2 * 2 + i, 1), :] for i in range(2)], 1
                    )
                )
        whole = jnp.concatenate(lines, 0)
        hw[...] = whole


def settle(coords, pieces, widths, rows_r, with_small, wait):
    outs = [((256, 4 * w), FULL) for w in widths] + [((rows_r, 1024), FULL)]
    scratch = []
    if with_small:
        outs += [((1, n), FULL) for n in (256, 256, 32, 32, 4)] + [((16, 256), FULL)]
        scratch = [((16, 8, 128), FULL), ((4, 16, 8, 128), FULL)]
    else:
        outs += [((8, LANES), FULL)]
    return call(functools.partial(settle_kernel, widths, with_small), coords, pieces, outs, scratch, wait=wait)


def group_gather(part):
    beside = swap(part, "core")
    across = swap(part, "zl")
    return part, beside, across, swap(across, "core")


def add_kernel(coords, keep, got, total, low):
    value = keep[...] + got[...].astype(FULL)
    total[...] = value
    low[...] = value.astype(LOW)


def chip_sum(coords, keep, send, wait=()):
    outs = [((2, 128, 1024), FULL), ((2, 128, 1024), LOW)]
    return call(add_kernel, coords, [keep, swap(send, "core")], outs, [], wait=wait)


def own_kernel(coords, keep, got, more_keep, more_got, *outs):
    (mine, more, low) = outs
    for s, (kept, came, own) in enumerate(((keep, got, mine), (more_keep, more_got, more))):
        own[...] = kept[0] + came[0].astype(FULL)
        low[s] = (kept[1] + came[1].astype(FULL)).astype(LOW)


def group_scatter(coords, first, second, wait):
    ins = [first[0], swap(first[1], "core"), second[0], swap(second[1], "core")]
    outs = [((128, 1024), FULL)] * 2 + [((2, 128, 1024), LOW)]
    mine, more, low = call(own_kernel, coords, ins, outs, [], wait=wait)
    return mine, more, swap(low, "zl")


def end_kernel(coords, mine, more, got, resid, grad_resid, hidden, gains, output, input_grad, flag):
    flag[...] = jnp.zeros((8, LANES), FULL)
    output[...] = (resid[0] + (mine[...] + got[0].astype(FULL))).astype(LOW)
    x = hidden[...].astype(FULL)
    inverse = inverse_rms(x)
    grad = (more[...] + got[1].astype(FULL)) * gains[0:1, :]
    input_grad[...] = (grad_resid[...] + norm_back(grad, x * inverse, inverse)).astype(LOW)


def finish(coords, ins, wait):
    return call(end_kernel, coords, ins, [((128, 1024), LOW)] * 2 + [((8, LANES), FULL)], [], wait=wait)


def resid_kernel(coords, total, got, h0, h2, gains, resid, low):
    for d, hidden in enumerate((h0, h2)):
        value = hidden[...].astype(FULL) + (total[d] + got[1 - d].astype(FULL))
        resid[d] = value
        low[d] = (value * inverse_rms(value) * gains[1:2, :]).astype(LOW)


def residual(coords, total, got, h0, h2, gains, wait):
    outs = [((2, 128, 1024), FULL), ((2, 128, 1024), LOW)]
    return call(resid_kernel, coords, [total, got, h0, h2, gains], outs, [], wait=wait)


def turn_kernel(coords, total, got, g0, g2, resid, gains, grad_resid, low, gain_sum):
    for d, upstream in enumerate((g0, g2)):
        value = resid[d]
        inverse = inverse_rms(value)
        normal = value * inverse
        grad = total[d] + got[1 - d].astype(FULL)
        back = upstream[...].astype(FULL) + norm_back(grad * gains[1:2, :], normal, inverse)
        low[d] = back.astype(LOW)
        if d == 0:
            grad_resid[...] = back
            gain_sum[...] = jnp.sum(grad * normal, 0, keepdims=True)


def turn_back(coords, total, got, g0, g2, resid, gains, wait):
    outs = [((128, 1024), FULL), ((2, 128, 1024), LOW), ((1, 1024), FULL)]
    return call(turn_kernel, coords, [total, got, g0, g2, resid, gains], outs, [], wait=wait)


def body(
    hidden,
    cotangent,
    segment_ids,
    positions,
    attention_gain,
    query_weight,
    key_weight,
    value_weight,
    query_gain,
    key_gain,
    headgate_weight,
    headgate_bias,
    output_weight,
    feedforward_gain,
    gate_weight,
    up_weight,
    down_weight,
):
    core = lax.axis_index("core")
    x_at, y_at = lax.axis_index("x"), lax.axis_index("y")
    j = lax.axis_index("zl") * 2 + core
    coords = jnp.stack([jnp.where(core == 0, x_at, y_at), jnp.where(core == 0, y_at, x_at), j]).astype(jnp.int32)

    freq = jnp.power(jnp.float32(THETA), -jnp.arange(64, dtype=FULL) * 2.0 / HEAD)
    angle = positions.astype(FULL)[:, None] * freq[None, :]
    cosine, sine = jnp.cos(angle), jnp.sin(angle)
    cosine, sine = jnp.concatenate([cosine, cosine], 1), jnp.concatenate([-sine, sine], 1)
    across = swap(hidden, "zl")
    across, gate_weight, up_weight = together(across, gate_weight, up_weight)
    tokens = (hidden, swap(hidden, "core"), across, swap(across, "core"))
    line = [attention_gain, feedforward_gain, jnp.pad(query_gain, (0, 96)), jnp.pad(key_gain, (0, 96))]
    small = (headgate_weight.T, jnp.concatenate(line)[None])
    mine, got, far, near = take_columns(coords, (query_weight, key_weight, value_weight), (512, 256, 256), small)
    far, near = swap_far(far), swap(near, "zl")
    mine_gu, got_gu, far_gu, last_gu, near_gu = take_columns(
        coords, (gate_weight, up_weight), (768, 768), (), (cosine,)
    )
    far, far_gu = together(far, far_gu)
    far_gu = swap_far(far_gu)
    near, cotangent, near_gu = together(near, cotangent, near_gu)
    grads = list(group_gather(cotangent))
    near_gu = swap(near_gu, "zl")
    weight_qkv = (mine, got, far, near)

    bias = jnp.pad(headgate_bias, (0, 124))[None]

    (keep, send, attn_in, raw, qk, val, probs, attended, gates, mixed, hw, gains, cosine, sine) = attention_forward(
        coords, tokens, weight_qkv, output_weight, cosine, sine, segment_ids.reshape(4, 128), bias
    )
    far_gu, last_gu = together(far_gu, last_gu)
    weight_gu = (mine_gu, got_gu, far_gu, swap_far(last_gu), near_gu)
    far_gu, near_gu, grads[2], send = together(far_gu, near_gu, grads[2], send)
    total, low = chip_sum(coords, keep, send)
    got = swap(low, "zl")
    resid, ffn_in = residual(coords, total, got, tokens[0], tokens[2], gains, weight_gu[3:4])
    keep, send, ffn, grads_all, grad_gu, act, wd_low = feed_forward(
        coords, (ffn_in, swap(ffn_in, "core")), weight_gu, down_weight, grads
    )
    total, low = chip_sum(coords, keep, send)
    low, grad_gu = together(low, grad_gu)
    pieces, part = spread(coords, ffn, [grad_gu], [swap(grad_gu, "core")], act, grads_all)
    got = swap(low, "zl")
    first = exchange(pieces, 0, 0)
    grad_resid, resid_low, grad_gain_second = turn_back(
        coords, total, got, grads[0], grads[2], resid, gains, (pieces[0],)
    )
    saved = (qk, val, probs, attended, gates, raw, gains, cosine, sine)
    front, resid_low, *others = back_first(coords, (resid_low, swap(resid_low, "core")), output_weight, saved)
    first = merge(coords, half_sum_kernel, first, (4,) * 4, (front,), 1)
    keep, send, back, small = back_second(
        coords,
        resid_low,
        output_weight,
        saved,
        (front, *others),
        (attn_in, hw, *weight_qkv, *tokens, grad_gain_second),
        first[:1],
    )
    first = exchange(first, 0, 1)
    pieces, part_second = spread(
        coords,
        attn_in,
        [front, back],
        [swap(front, "core"), swap(back, "core")],
        mixed,
        resid_low,
        (small, swap(small, "core")),
        first[2:],
    )
    second = exchange(pieces, 0, 0)
    first = exchange(merge(coords, turn_sum_kernel, first, (2,) * 4, pieces[:1], 1), 1, 0)
    sums = group_scatter(coords, down(coords, act, wd_low, first[:1]), (keep, send), ())
    first = exchange(merge(coords, half_sum_kernel, first, (1,) * 4, sums[:1], 1), 1, 1)
    second = exchange(merge(coords, half_sum_kernel, second, (4,) * 4, first[:1]), 0, 1)
    first = send_across(*last_sum(coords, first, part, (second[0], sums[2])))
    second = exchange(merge(coords, turn_sum_kernel, second, (2,) * 4, first[2:3]), 1, 0)
    first = cross_sum(coords, first, second[:1])
    second = exchange(merge(coords, half_sum_kernel, second, (1,) * 4, first[:1]), 1, 1)
    first = merge(coords, join_kernel, exchange(first * 2, 1, 1), (2, 2), second[:1])
    second = send_across(*last_sum(coords, second, part_second, first[:1]))
    first = merge(coords, pack_kernel, exchange(first * 2, 1, 0), (4, 4), second[2:3])
    second = cross_sum(coords, second, first[:1])
    first = merge(coords, join_kernel, exchange(first * 2, 0, 1), (8, 8), second[:1])
    second = merge(coords, join_kernel, exchange(second * 2, 1, 1), (2, 2), first[:1])
    second = merge(coords, pack_kernel, exchange(second * 2, 1, 0), (4, 4), ())
    first = exchange(first * 2, 0, 0)
    second = merge(coords, join_kernel, exchange(second * 2, 0, 1), (8, 8), first[2:])
    grad_g, grad_u, grad_d, settled = settle(coords, first, (768, 768), 768, False, second[:1])
    second = exchange(second * 2, 0, 0)
    output, input_grad, finished = finish(coords, [*sums, resid, grad_resid, hidden, gains], (settled,))
    (grad_q, grad_k, grad_v, grad_o, small_first, small_second, small_q, small_k, small_bias, grad_hw) = settle(
        coords, second, (512, 256, 256), 512, True, (finished,)
    )
    return (
        output,
        input_grad,
        small_first.reshape(256),
        grad_q,
        grad_k,
        grad_v,
        small_q.reshape(32),
        small_k.reshape(32),
        grad_hw.T,
        small_bias.reshape(4),
        grad_o,
        small_second.reshape(256),
        grad_g,
        grad_u,
        grad_d,
    )


def solution(mesh):
    grid = Mesh(mesh.devices.reshape(2, 4, 4, 2, 2), AXES)
    tokens, split, copies = P(AXES, None), P(GROUP, None), P(("zh", "y", "x"))
    line = P(GROUP)
    weights = (line, split, split, split, line, line, split, line, split, line, split, split, split)
    return jax.shard_map(
        body,
        mesh=grid,
        in_specs=(tokens, tokens, copies, copies, *weights),
        out_specs=(tokens, tokens, *weights),
        check_vma=False,
    )
```

```python
import functools
import math

import jax
import jax.numpy as jnp
from jax import lax
from jax.experimental import pallas as pl
from jax.experimental.pallas import tpu as pltpu
from jax.sharding import Mesh
from jax.sharding import PartitionSpec as P

EPS = 1e-06
THETA = 1000000.0
MASKED = -1e30
HEAD = 128
SCALE = 1.0 / math.sqrt(HEAD)
LOW = jnp.bfloat16
FULL = jnp.float32
AXES = ("zh", "y", "x", "zl", "core")
GROUP = ("zl", "core")
LANES = 128


def swap(value, axis):
    return lax.ppermute(value, axis, [(0, 1), (1, 0)])


def turn(value, step):
    return lax.ppermute(value, ("zh", "zl"), [(i, (i + step) % 4) for i in range(4)])


def swap_far(value):
    return lax.ppermute(value, ("zh", "zl"), [(0, 3), (3, 0), (1, 2), (2, 1)])


def swap_plane(value, axis, mask):
    pairs = []
    for y in range(4):
        for x in range(4):
            for core in range(2):
                to_y, to_x = (y, x ^ mask) if axis == core else (y ^ mask, x)
                pairs.append(((y * 4 + x) * 2 + core, (to_y * 4 + to_x) * 2 + core))
    return lax.ppermute(value, ("y", "x", "core"), pairs)


def dot(left, right):
    return jnp.dot(left, right, preferred_element_type=FULL)


def dot_t(left, right):
    return lax.dot_general(left, right, (((1,), (1,)), ((), ())), preferred_element_type=FULL)


def dot_tn(left, right):
    return lax.dot_general(left, right, (((0,), (0,)), ((), ())), preferred_element_type=FULL)


VMEM = pl.BlockSpec(memory_space=pltpu.VMEM)
SMEM = pl.BlockSpec(memory_space=pltpu.SMEM)


def held_bytes(shape, kind):
    shape = (1,) * (2 - len(shape)) + tuple(shape)
    size = math.prod(shape[:-2]) * (-(-shape[-2] // 16) * 16) * (-(-shape[-1] // LANES) * LANES)
    return size * jnp.dtype(kind).itemsize


class Late:
    def __init__(self, source, target, done):
        self.copy, self.target, self.open = pltpu.make_async_copy(source, target, done), target, True
        self.copy.start()

    def ready(self):
        if self.open:
            self.copy.wait()
        self.open = False
        return self.target


class Early:
    def __init__(self, source, target, done):
        self.copy, self.source, self.sent = pltpu.make_async_copy(source, target, done), source, False

    def send(self):
        if not self.sent:
            self.copy.start()
        self.sent = True


def call(kernel, coords, ins, outs, scratch, late=(), early=(), least=0, wait=(), flops=1):
    ins = list(ins)
    n_ins, n_outs, n_scratch = len(ins), len(outs), len(scratch)
    moving = [(ins[i].shape, ins[i].dtype) for i in late] + [outs[i] for i in early]

    def run(coords, *refs):
        refs = list(refs)
        del refs[n_ins : n_ins + len(wait)]
        done = refs.pop() if moving else None
        buffers = refs[n_ins + n_outs + n_scratch :]
        refs = refs[: n_ins + n_outs + n_scratch]
        for k, i in enumerate(late):
            refs[i] = Late(refs[i], buffers[k], done.at[k])
        sending = []
        for k, i in enumerate(early):
            k += len(late)
            sending.append(Early(buffers[k], refs[n_ins + i], done.at[k]))
            refs[n_ins + i] = sending[-1]
        kernel(coords, *refs)
        for i in late:
            refs[i].ready()
        for out in sending:
            out.send()
        for out in sending:
            out.copy.wait()

    need = sum(held_bytes(a.shape, a.dtype) for a in ins) + sum(held_bytes(*o) for o in [*outs, *scratch])
    anywhere = pl.BlockSpec(memory_space=pltpu.HBM)
    buffers = [pltpu.VMEM(shape, kind) for shape, kind in [*scratch, *moving]]
    return pl.pallas_call(
        run,
        out_shape=[jax.ShapeDtypeStruct(shape, kind) for shape, kind in outs],
        in_specs=[SMEM] + [anywhere if i in late else VMEM for i in range(n_ins)] + [pl.BlockSpec(memory_space=pl.ANY)] * len(wait),
        out_specs=[anywhere if i in early else VMEM for i in range(n_outs)],
        scratch_shapes=buffers + ([pltpu.SemaphoreType.DMA((len(moving),))] if moving else []),
        compiler_params=pltpu.CompilerParams(vmem_limit_bytes=max(need + 8 * 2**20, least * 2**20)),
        cost_estimate=pl.CostEstimate(flops=flops, bytes_accessed=1, transcendentals=0),
    )(coords, *ins, *wait)


def lanes(index, width):
    return pl.ds(pl.multiple_of(index * width, LANES), width)


def rows(index, height):
    return pl.ds(pl.multiple_of(index * height, 16), height)


def inverse_rms(value):
    return lax.rsqrt(jnp.mean(value * value, -1, keepdims=True) + EPS)


def norm_back(grad, normal, inverse):
    return inverse * (grad - normal * jnp.mean(grad * normal, -1, keepdims=True))


def cut_kernel(widths, small, coords, *refs):
    ins, outs = refs[: len(widths)], refs[len(widths) + 2 * small :]
    j = coords[2]
    if small:
        heads, line = refs[len(widths) : len(widths) + 2]
        line = jnp.concatenate([line[...], jnp.zeros((15, 768), FULL)], 0)
        tile = jnp.concatenate([heads[...], line], 1).astype(LOW)
    third = [(3, 0, 256), (2, 0, 256)] if small else [(3, 0, 128), (3, 128, 128), (2, 0, 192), (2, 192, 64)]
    for out, (r, first, count) in zip(outs, [(1, 0, 256), *third, (0, 0, 256)]):
        at = 0
        for w, n in zip(ins, widths):
            out[0:count, at : at + n] = w[first : first + count, lanes(j ^ r, n)].astype(LOW)
            at += n
        if small:
            out[256:272, :] = tile


def take_columns(coords, weights, widths, small=(), wait=()):
    heights = (272,) * 4 if small else (256, 128, 128, 192, 64, 256)
    beside, *rest, mine = call(
        functools.partial(cut_kernel, widths, bool(small)),
        coords,
        [*weights, *small],
        [((n, sum(widths)), LOW) for n in heights],
        [],
        least=50,
        wait=wait,
    )
    half = len(rest) // 2
    return mine, swap(beside, "core"), *[swap(piece, "core") for piece in rest[:half]], *rest[half:]


def first_kernel(coords, t0, t1, t2, t3, w0, w1, w2, w3, wo, cos, sin, segs, bias, *refs):
    (keep, send, attn_in, raw, qk, val, probs, attended, gates, mixed, hw, gains, cos_rel, sin_rel) = refs[:14]
    (wo_low, mask) = refs[14:]
    (attn_out, raw_out, qk_out, val_out, probs_out, att_out, gates_out, mixed_out) = refs[2:10]
    attn_in, raw, qk, val, probs, attended, gates, mixed = [r.source for r in refs[2:10]]
    cos_out, sin_out = refs[12:14]
    cos_rel, sin_rel = cos_out.source, sin_out.source
    j = coords[2]
    tokens, weights = (t0, t1, t2, t3), (w0, w1, w2, w3)
    hw[...] = jnp.zeros_like(hw)
    gains[...] = jnp.zeros_like(gains)
    gain_q, gain_k = jnp.zeros((16, LANES), FULL), jnp.zeros((16, LANES), FULL)
    for r in range(4):
        small = weights[r][256:272, :]
        hw[0:16, lanes(j ^ r, 256)] = small[:, 0:256]
        small = small[:, 256:].astype(FULL)
        gains[0:1, lanes(j ^ r, 256)] = small[0:1, 0:256]
        gains[1:2, lanes(j ^ r, 256)] = small[0:1, 256:512]
        gain_q += pltpu.roll(small[:, 512:640], (j ^ r) * 32, 1)
        gain_k += pltpu.roll(small[:, 640:768], (j ^ r) * 32, 1)
        cos_rel[r * 128 : r * 128 + 128, :] = cos.ready()[rows(j ^ r, 128), :]
        sin_rel[r * 128 : r * 128 + 128, :] = sin.ready()[rows(j ^ r, 128), :]
    gains[2:3, 0:128] = gain_q[0:1]
    gains[2:3, 128:256] = gain_k[0:1]
    for r in range(4):
        x = tokens[r][0:128, :].astype(FULL)
        attn_in[r * 128 : r * 128 + 128, :] = (x * inverse_rms(x) * gains[0:1, :]).astype(LOW)

    attn_out.send()
    cos_out.send()
    sin_out.send()

    logit = dot_t(attn_in[...], hw[...])
    logit = pltpu.roll(logit, (32 - j) * 4 & 127, 1) + bias[...].astype(LOW).astype(FULL)
    gates[...] = jax.nn.sigmoid(logit)
    gates_out.send()
    for n in range(4):
        total = dot(attn_in[:, lanes(j, 256)], w0[0:256, n * 256 : n * 256 + 256])
        for r in range(1, 4):
            total += dot(attn_in[:, lanes(j ^ r, 256)], weights[r][0:256, n * 256 : n * 256 + 256])
        if n < 3:
            raw[:, n * 256 : n * 256 + 256] = total
        else:
            val[...] = total.astype(LOW)
    raw_out.send()
    val_out.send()
    for h in range(6):
        at = slice(h * 128, h * 128 + 128)
        part = raw[:, at]
        gain = gains[2:3, 0:128] if h < 4 else gains[2:3, 128:256]
        part = part * inverse_rms(part) * gain
        qk[:, at] = (part * cos_rel[...] + pltpu.roll(part, 64, 1) * sin_rel[...]).astype(LOW)

    qk_out.send()
    lane = lax.broadcasted_iota(jnp.int32, (128, 128), 1)
    line = lax.broadcasted_iota(jnp.int32, (128, 128), 0)
    for c in range(4):
        seg_q = jnp.broadcast_to(segs[pl.ds(j ^ c, 1), :], (128, 128)).T
        for b in range(4):
            seg_k = segs[pl.ds(j ^ b, 1), :]
            earlier = lane + (j ^ b) * 128 <= line + (j ^ c) * 128
            mask[c * 128 : c * 128 + 128, b * 128 : b * 128 + 128] = jnp.where(
                earlier & (seg_q == seg_k), 0.0, MASKED
            )
    for h in range(4):
        kv = h // 2
        for c in range(2):
            at = slice(c * 256, c * 256 + 256)
            scores = dot_t(qk[at, h * 128 : h * 128 + 128], qk[:, 512 + kv * 128 : 640 + kv * 128])
            scores = scores * SCALE + mask[at, :]
            expo = jnp.exp(scores - jnp.max(scores, -1, keepdims=True))
            part = (expo * (1.0 / jnp.sum(expo, -1, keepdims=True))).astype(LOW)
            probs[h, at, :] = part
            result = dot(part, val[:, kv * 128 : kv * 128 + 128])
            attended[at, h * 128 : h * 128 + 128] = result
            mixed[at, h * 128 : h * 128 + 128] = (result * gates[at, h : h + 1]).astype(LOW)
    probs_out.send()
    att_out.send()
    mixed_out.send()
    wo_low[...] = wo.ready()[...].astype(LOW)
    for n in range(4):
        at = slice(n * 256, n * 256 + 256)
        result = dot(mixed[...], wo_low[:, at])
        for c in range(2):
            keep[c, :, at] = result[c * 256 : c * 256 + 128]
            send[c, :, at] = result[c * 256 + 128 : c * 256 + 256].astype(LOW)


def attention_forward(coords, tokens, weights, wo, cos, sin, segs, bias):
    outs = [
        ((2, 128, 1024), FULL),
        ((2, 128, 1024), LOW),
        ((512, 1024), LOW),
        ((512, 768), FULL),
        ((512, 768), LOW),
        ((512, 256), LOW),
        ((4, 512, 512), LOW),
        ((512, 512), FULL),
        ((512, 128), FULL),
        ((512, 512), LOW),
        ((128, 1024), LOW),
        ((8, 1024), FULL),
        ((512, 128), FULL),
        ((512, 128), FULL),
    ]
    return call(
        first_kernel,
        coords,
        [*tokens, *weights, wo, cos, sin, segs, bias],
        outs,
        [((512, 1024), LOW), ((512, 512), FULL)],
        (9, 10, 8),
        (2, 3, 4, 5, 6, 7, 8, 9, 12, 13),
    )


def ffn_kernel(coords, f_own, f_got, w0, w1, w2_low, w2_high, w3_low, w3_high, wd, g0, g1, g2, g3, *refs):
    (keep, send, ffn, grads, grad_gu, act, wd_low, w2, w3) = refs
    j = coords[2]
    weights = (w0, w1, w2, w3)
    w2[0:192, :] = w2_low[...]
    w2[192:256, :] = w2_high[...]
    w3[0:128, :] = w3_low[...]
    w3[128:256, :] = w3_high[...]
    for r, g in enumerate((g0, g1, g2, g3)):
        ffn[r * 128 : r * 128 + 128, :] = (f_got if r % 2 else f_own)[r // 2]
        grads[r * 128 : r * 128 + 128, :] = g[...]
    wd_low[...] = wd[...].astype(LOW)
    for m in range(2):
        at = slice(m * 256, m * 256 + 256)
        for n in range(3):
            low, high = slice(n * 256, n * 256 + 256), slice(768 + n * 256, 1024 + n * 256)
            gate = dot(ffn[at, lanes(j, 256)], w0[:, low])
            up = dot(ffn[at, lanes(j, 256)], w0[:, high])
            for r in range(1, 4):
                gate += dot(ffn[at, lanes(j ^ r, 256)], weights[r][:, low])
                up += dot(ffn[at, lanes(j ^ r, 256)], weights[r][:, high])
            back = dot_t(grads[at, :], wd_low[low, :])
            sigma = jax.nn.sigmoid(gate)
            swish = gate * sigma
            act[at, low] = (swish * up).astype(LOW)
            grad_gu[at, low] = (back * up * sigma * (1.0 + gate * (1.0 - sigma))).astype(LOW)
            grad_gu[at, high] = (back * swish).astype(LOW)
    for r in range(4):
        part = dot_t(grad_gu[...], weights[r][...])
        for t in range(2):
            keep[t, :, lanes(j ^ r, 256)] = part[t * 256 : t * 256 + 128]
            send[t, :, lanes(j ^ r, 256)] = part[t * 256 + 128 : t * 256 + 256].astype(LOW)


def feed_forward(coords, ffn_in, weights, wd, grads):
    outs = [
        ((2, 128, 1024), FULL),
        ((2, 128, 1024), LOW),
        ((512, 1024), LOW),
        ((512, 1024), LOW),
        ((512, 1536), LOW),
        ((512, 768), LOW),
        ((768, 1024), LOW),
    ]
    return call(
        ffn_kernel,
        coords,
        [*ffn_in, *weights, wd, *grads],
        outs,
        [((256, 1536), LOW)] * 2,
    )


def down_kernel(coords, act, wd_low, keep, send):
    for c in range(4):
        result = dot(act[c * 128 : c * 128 + 128, :], wd_low[...])
        if c % 2:
            send[c // 2] = result.astype(LOW)
        else:
            keep[c // 2] = result


def down(coords, act, wd_low, wait):
    outs = [((2, 128, 1024), FULL), ((2, 128, 1024), LOW)]
    return call(down_kernel, coords, [act, wd_low], outs, [], wait=wait)


def heads_back(kv, refs, resid_low, wo_low, grad_scores, out):
    (qk, val, probs, attended, gates, raw, gains, cos, sin) = refs
    lane = lax.broadcasted_iota(jnp.int32, (512, LANES), 1)
    grad_logit = jnp.zeros((512, LANES), FULL)
    gain_sums = []

    def head_back(grad, at, gain, to):
        part = raw[:, at]
        inverse = inverse_rms(part)
        normal = part * inverse
        turned = grad * cos[...] - pltpu.roll(grad, 64, 1) * sin[...]
        gain_sums.append(jnp.sum(turned * normal, 0, keepdims=True))
        out[:, to : to + 128] = norm_back(turned * gain, normal, inverse).astype(LOW)

    key_at = slice(512 + kv * 128, 640 + kv * 128)
    grad_key = grad_value = None
    for n, h in enumerate((2 * kv, 2 * kv + 1)):
        at = slice(h * 128, h * 128 + 128)
        grad_mixed = dot_t(resid_low[...], wo_low[n * 128 : n * 128 + 128, :])
        gate = gates[:, h : h + 1]
        grad_gate = jnp.sum(grad_mixed * attended[:, at], -1, keepdims=True) * gate * (1.0 - gate)
        grad_logit = jnp.where(lane == h, grad_gate, grad_logit)
        grad_att = (grad_mixed * gate).astype(LOW)
        for c in range(2):
            line = slice(c * 256, c * 256 + 256)
            grad_probs = dot_t(grad_att[line], val[:, kv * 128 : kv * 128 + 128])
            part = probs[h, line, :].astype(FULL)
            inner = jnp.sum(part * grad_probs, -1, keepdims=True)
            grad_scores[line, :] = (part * (grad_probs - inner)).astype(LOW)
        head_back(dot(grad_scores[...], qk[:, key_at]) * SCALE, at, gains[2:3, 0:128], n * 128)
        more_key = dot_tn(grad_scores[...], qk[:, at])
        more_value = dot_tn(probs[h], grad_att)
        grad_key = more_key if grad_key is None else grad_key + more_key
        grad_value = more_value if grad_value is None else grad_value + more_value
    head_back(grad_key * SCALE, key_at, gains[2:3, 128:256], 256)
    out[:, 384:512] = grad_value.astype(LOW)
    return grad_logit, gain_sums


def back_first_kernel(coords, l_own, l_got, wo, qk, val, probs, attended, gates, raw, gains, cos, sin, *refs):
    (out, resid_low, logit, sums, wo_low, grad_scores) = refs
    wo_low[...] = wo.ready()[0:256, :].astype(LOW)
    for r in range(4):
        resid_low[r * 128 : r * 128 + 128, :] = (l_got if r % 2 else l_own)[r // 2]
    refs = [r.ready() for r in (qk, val, probs, attended, gates, raw, gains, cos, sin)]
    grad_logit, gain_sums = heads_back(0, refs, resid_low, wo_low, grad_scores, out)
    logit[...] = grad_logit
    sums[...] = jnp.zeros_like(sums)
    for i, value in enumerate(gain_sums):
        sums[i : i + 1, :] = value


def back_kernel(coords, *refs):
    (resid_low, wo, qk, val, probs, attended, gates, raw, gains, cos, sin, out_first, logit, sums) = refs[:14]
    (attn_in, hw, w0, w1, w2, w3, t0, t1, t2, t3, gain_second) = refs[14:25]
    (keep, send, out, small) = refs[25:29]
    (wo_low, grad_scores, grad_qkv) = refs[29:]
    j = coords[2]
    wo_low[...] = wo.ready()[256:512, :].astype(LOW)
    refs = [r.ready() for r in (qk, val, probs, attended, gates, raw, gains, cos, sin)]
    grad_logit, gain_sums = heads_back(1, refs, resid_low, wo_low, grad_scores, out)
    for kv, part in enumerate((out_first, out)):
        grad_qkv[:, kv * 256 : kv * 256 + 256] = part[:, 0:256]
        grad_qkv[:, 512 + kv * 128 : 640 + kv * 128] = part[:, 256:384]
        grad_qkv[:, 768 + kv * 128 : 896 + kv * 128] = part[:, 384:512]

    weights, tokens = [[r.ready() for r in group] for group in ((w0, w1, w2, w3), (t0, t1, t2, t3))]
    attn_in, hw = attn_in.ready(), hw.ready()
    grad_logit = (grad_logit + logit[...]).astype(LOW)
    grad_bias = jnp.sum(grad_logit.astype(FULL), 0, keepdims=True)
    grad_hw = dot_tn(grad_logit, attn_in[...])
    spread_logit = pltpu.roll(grad_logit.astype(FULL), j * 4, 1).astype(LOW)
    inverses = []
    for r in range(4):
        x = tokens[r][0:128, :].astype(FULL)
        inverses.append(inverse_rms(x))
    small[...] = jnp.zeros_like(small)

    def put(row, value):
        small[row // 4, row % 4 : row % 4 + 1, :] = value

    for r in range(4):
        at = lanes(j ^ r, 256)
        part = dot_t(grad_qkv[...], weights[r][0:256, :]) + dot(spread_logit, hw[:, at])
        total = jnp.zeros((1, 256), FULL)
        for t in range(4):
            piece = part[t * 128 : t * 128 + 128]
            normal = tokens[t][0:128, at].astype(FULL) * inverses[t]
            total += jnp.sum(piece * normal, 0, keepdims=True)
            if t % 2:
                send[t // 2, :, at] = piece.astype(LOW)
            else:
                keep[t // 2, :, at] = piece
        block = (j ^ r) // 2
        for i in range(2):
            small[block, pl.ds((j ^ r) % 2 * 2 + i, 1), :] = total[:, i * 128 : i * 128 + 128]
    for i in range(8):
        put(8 + i, gain_second[0:1, i * 128 : i * 128 + 128])
    put(16, gain_sums[0] + gain_sums[1] + sums[0:1, :] + sums[1:2, :])
    put(17, gain_sums[2] + sums[2:3, :])
    put(18, grad_bias)
    for h in range(4):
        for i in range(8):
            put(24 + h * 8 + i, grad_hw[h : h + 1, i * 128 : i * 128 + 128])


def back_first(coords, resid_low, wo, saved):
    outs = [((512, 512), LOW), ((512, 1024), LOW), ((512, 128), FULL), ((8, 128), FULL)]
    scratch = [((256, 1024), LOW), ((512, 512), LOW)]
    return call(back_first_kernel, coords, [*resid_low, wo, *saved], outs, scratch, range(2, 12), flops=3*10**9)


def back_second(coords, resid_low, wo, saved, first, others, wait):
    outs = [((2, 128, 1024), FULL), ((2, 128, 1024), LOW), ((512, 512), LOW), ((16, 8, 128), FULL)]
    scratch = [((256, 1024), LOW), ((512, 512), LOW), ((512, 1024), LOW)]
    ins = [resid_low, wo, *saved, *first, *others]
    late = [*range(1, 11), *range(14, 24)]
    return call(back_kernel, coords, ins, outs, scratch, late, wait=wait)


KEPT, SENT, MASKS = ((0, 3), (0, 1)), ((1, 2), (3, 2)), ((1, 3), (3, 1))


def spread_kernel(n_right, with_small, coords, left_c, *refs):
    rights, (left_r, right_r, *refs) = refs[: 2 * n_right], refs[2 * n_right :]
    if with_small:
        small_own, small_got, *refs = refs
    outs, (turned_c, turned_r, held_c, held_r) = refs[:4], refs[4:]
    first, second, j = coords[0], coords[1], coords[2]
    wide = rights[0].shape[1] // LANES
    panels = wide * n_right
    rows_r = left_r.shape[1] // 16
    part = 2 * panels * 16 + (16 if with_small else 0)
    edge = outs[0].shape[1]
    blocks = [(m, n, (first ^ m) * 4 + (second ^ n)) for m in (1, 2, 3, 0) for n in range(4)]

    def put(m, n, low, value):
        stream = 0 if low < edge else 1
        sent = m in SENT[stream]
        at = (SENT if sent else KEPT)[stream].index(m) * 4 + n
        low -= edge * stream
        outs[2 * sent + stream][at, low : low + value.shape[0], :] = value

    for d in range(2):
        turned = left_c[:, lanes(j ^ (2 * d), 256)].T
        turned_c[d] = turned
        for t in range(4):
            turned_c[2 + d, :, t * 128 : t * 128 + 128] = turned[:, (t ^ 1) * 128 : (t ^ 1) * 128 + 128]
    turned_r[...] = left_r[...].T
    for k, right in enumerate(rights):
        src, start = k // n_right, k % n_right * wide
        for d in range(2):
            held_c[...] = dot(turned_c[2 * src + d], right[...]).astype(LOW)
            for m, n, block in blocks:
                for p in range(wide):
                    low = (1 - d) * part + (src * panels + start + p) * 16
                    put(m, n, low, held_c[rows(block, 16), p * LANES : (p + 1) * LANES])
    held_r[...] = dot(turned_r[...], right_r[...]).astype(LOW)
    for m, n, block in blocks:
        if with_small:
            tile = jnp.concatenate([small_own[block], small_got[block]], 0).astype(LOW)
            put(m, n, part - 16, tile)
            put(m, n, 2 * part - 16, tile)
        for p in range(8):
            put(m, n, 2 * part + p * rows_r, held_r[rows(block, rows_r), p * LANES : (p + 1) * LANES])


def spread(coords, left_c, own, got, left_r, right_r, small=(), wait=()):
    wide = own[0].shape[1]
    panels = wide * len(own) // LANES
    part = 2 * panels * 16 + (16 if small else 0)
    height = 2 * part + left_r.shape[1] // 2
    scratch = [
        ((4, 256, 512), LOW),
        ((left_r.shape[1], 512), LOW),
        ((256, wide), LOW),
        ((left_r.shape[1], 1024), LOW),
    ]
    pieces = call(
        functools.partial(spread_kernel, len(own), bool(small)),
        coords,
        [left_c, *own, *got, left_r, right_r, *small],
        [((8, height // 2, LANES), LOW)] * 4,
        scratch,
        wait=wait,
    )
    return pieces, part


def plus(a, b):
    return (a.astype(FULL) + b.astype(FULL)).astype(LOW)


def half_sum_kernel(coords, p, q, got_p, got_q, *outs):
    half = p.shape[0] // 2
    for kept, sent, mine, got in ((outs[0], outs[2], p, got_p), (outs[1], outs[3], q, got_q)):
        kept[...] = plus(mine[0:half], got[0:half])
        sent[...] = plus(mine[half:], got[half:])


def turn_sum_kernel(coords, p, q, got_p, got_q, *outs):
    for s, (mine, got) in enumerate(((p, got_p), (q, got_q))):
        for at in range(2):
            outs[s][at] = plus(mine[KEPT[s][at]], got[KEPT[s][at]])
            outs[2 + s][at] = plus(mine[SENT[s][at]], got[SENT[s][at]])


def last_sum_kernel(coords, p, q, got_p, got_q, other, mine):
    part, edge = other.shape[0], p.shape[1]
    p, q = plus(p[0], got_p[0]), plus(q[0], got_q[0])
    other[...] = p[:part]
    mine[0 : edge - part, :] = p[part:]
    mine[edge - part :, :] = q


def cross_sum_kernel(coords, ahead, behind, mine, far, p, q):
    part, edge = ahead.shape[0], p.shape[1]
    p[0, 0:part, :] = plus(ahead[...], behind[...])
    mine = plus(mine[...], far[...])
    p[0, part:, :] = mine[: edge - part]
    q[0] = mine[edge - part :]


def quarter_sum_kernel(coords, p, q, got_p, got_q, *outs):
    edge = p.shape[1]
    for n in range(4):
        outs[n][0:edge, :] = plus(p[n], got_p[n])
        outs[n][edge:, :] = plus(q[n], got_q[n])


def direct_sum_kernel(coords, a, b, c, d, other, mine):
    total = (a[...].astype(FULL) + b[...].astype(FULL) + c[...].astype(FULL) + d[...].astype(FULL)).astype(LOW)
    part = other.shape[0]
    other[...] = total[:part]
    mine[...] = total[part:]


def plain_sum_kernel(coords, ahead, behind, mine, far, out):
    part = ahead.shape[0]
    out[0:part, :] = plus(ahead[...], behind[...])
    out[part:, :] = plus(mine[...], far[...])


def direct_pack_kernel(coords, a, b, c, d, p, q):
    edge = p.shape[1]
    for n, ref in enumerate((a, b, c, d)):
        p[n] = ref[0:edge, :]
        q[n] = ref[edge:, :]


def direct(parts):
    return [parts[0]] + [swap_plane(parts[m], 1, m) for m in (1, 2, 3)]


def small_kernel_call(coords, kernel, got, shapes, wait, flops=4 * 10**9):
    return call(kernel, coords, got, [(shape, LOW) for shape in shapes], [], wait=wait, flops=flops)


def join_kernel(coords, p, q, got_p, got_q, both_p, both_q):
    half = p.shape[0]
    for both, mine, got in ((both_p, p, got_p), (both_q, q, got_q)):
        both[0:half] = mine[...]
        both[half:] = got[...]


def pack_kernel(coords, p, q, got_p, got_q, all_p, all_q):
    for s, (whole, mine, got) in enumerate(((all_p, p, got_p), (all_q, q, got_q))):
        for at in range(2):
            whole[KEPT[s][at]] = mine[at]
            whole[SENT[s][at]] = got[at]


def exchange(pieces, axis, step):
    return [*pieces[:2], *[swap_plane(pieces[2 + s], axis, MASKS[s][step]) for s in range(2)]]


def merge(coords, kernel, got, counts, wait, flops=4 * 10**9):
    outs = [((n, *got[0].shape[1:]), LOW) for n in counts]
    return call(kernel, coords, got, outs, [], wait=wait, flops=flops)


def send_across(other, mine):
    return [turn(other, 1), turn(other, -1), mine, turn(mine, 2)]


def last_sum(coords, got, part, wait):
    outs = [((part, LANES), LOW), ((2 * got[0].shape[1] - part, LANES), LOW)]
    return call(last_sum_kernel, coords, got, outs, [], wait=wait, flops=4 * 10**9)


def cross_sum(coords, got, wait):
    edge = (got[0].shape[0] + got[2].shape[0]) // 2
    return call(cross_sum_kernel, coords, got, [((1, edge, LANES), LOW)] * 2, [], wait=wait, flops=4 * 10**9)


def together(*values):
    return lax.optimization_barrier(values)


def settle_kernel(widths, with_small, coords, *refs):
    ins, outs = refs[:4], refs[4:]
    first, second, j = coords[0], coords[1], coords[2]
    panels = sum(widths) // LANES
    out_r = outs[len(widths)]
    rows_r = out_r.shape[0] // 16
    spots = []
    for kv in range(2 if with_small else 1):
        for w, width in enumerate(widths):
            count = width // LANES // (2 if with_small else 1)
            spots += [(w, (kv * count + i) * LANES) for i in range(count)]
    if with_small:
        total, heads = refs[-2:]
        total[...] = jnp.zeros_like(total)

    part = 2 * panels * 16 + (16 if with_small else 0)
    edge = ins[0].shape[1]

    def take(m, n, low, height):
        stream = 0 if low < edge else 1
        came = m in SENT[stream]
        at = (SENT if came else KEPT)[stream].index(m) * 4 + n
        low -= edge * stream
        return ins[2 * came + stream][at, low : low + height, :].astype(FULL)

    for m in range(4):
        for n in range(4):
            block = (first ^ m) * 4 + (second ^ n)
            line = rows(block, 16)
            for r in range(4):
                base = (1 - r // 2) * part + (r % 2) * panels * 16
                for p, (w, col) in enumerate(spots):
                    lane = pl.ds(pl.multiple_of((j ^ r) * widths[w] + col, LANES), LANES)
                    low = base + p * 16
                    outs[w][line, lane] = take(m, n, low, 16)
            for p in range(8):
                low = 2 * part + p * rows_r
                lane = slice(p * LANES, (p + 1) * LANES)
                out_r[rows(block, rows_r), lane] = take(m, n, low, rows_r)
            if with_small:
                for z in range(2):
                    tile = take(m, n, (1 - z) * part + part - 16, 16)
                    for src in range(2):
                        value = tile[src * 8 : src * 8 + 8]
                        heads[j ^ (2 * z + src), block] = value
                        total[block] += value
    if not with_small:
        outs[-1][...] = jnp.zeros((8, LANES), FULL)
    if with_small:
        gain_first, gain_second, gain_q, gain_k, bias, hw = outs[len(widths) + 1 : len(widths) + 7]
        for i in range(2):
            at = slice(i * 128, i * 128 + 128)
            gain_first[:, at] = total[j // 2, pl.ds(j % 2 * 2 + i, 1), :]
            gain_second[:, at] = total[2 + j // 2, pl.ds(j % 2 * 2 + i, 1), :]
        shift = (4 - j) * 32 & 127
        turned = pltpu.roll(total[4], shift, 1)
        gain_q[...] = turned[0:1, :32]
        gain_k[...] = turned[1:2, :32]
        bias[...] = heads[j, 4][2:3, :4]
        lines = []
        for q in range(4):
            for h in range(4):
                start = 24 + h * 8
                lines.append(
                    jnp.concatenate(
                        [heads[q, start // 4 + j // 2, pl.ds(j % 2 * 2 + i, 1), :] for i in range(2)], 1
                    )
                )
        whole = jnp.concatenate(lines, 0)
        hw[...] = whole


def settle(coords, pieces, widths, rows_r, with_small, wait):
    outs = [((256, 4 * w), FULL) for w in widths] + [((rows_r, 1024), FULL)]
    scratch = []
    if with_small:
        outs += [((1, n), FULL) for n in (256, 256, 32, 32, 4)] + [((16, 256), FULL)]
        scratch = [((16, 8, 128), FULL), ((4, 16, 8, 128), FULL)]
    else:
        outs += [((8, LANES), FULL)]
    return call(functools.partial(settle_kernel, widths, with_small), coords, pieces, outs, scratch, wait=wait)


def group_gather(part):
    beside = swap(part, "core")
    across = swap(part, "zl")
    return part, beside, across, swap(across, "core")


def add_kernel(coords, keep, got, total, low):
    value = keep[...] + got[...].astype(FULL)
    total[...] = value
    low[...] = value.astype(LOW)


def chip_sum(coords, keep, send, wait=()):
    outs = [((2, 128, 1024), FULL), ((2, 128, 1024), LOW)]
    return call(add_kernel, coords, [keep, swap(send, "core")], outs, [], wait=wait)


def own_kernel(coords, keep, got, more_keep, more_got, *outs):
    (mine, more, low) = outs
    for s, (kept, came, own) in enumerate(((keep, got, mine), (more_keep, more_got, more))):
        own[...] = kept[0] + came[0].astype(FULL)
        low[s] = (kept[1] + came[1].astype(FULL)).astype(LOW)


def group_scatter(coords, first, second, wait):
    ins = [first[0], swap(first[1], "core"), second[0], swap(second[1], "core")]
    outs = [((128, 1024), FULL)] * 2 + [((2, 128, 1024), LOW)]
    mine, more, low = call(own_kernel, coords, ins, outs, [], wait=wait)
    return mine, more, swap(low, "zl")


def end_kernel(coords, mine, more, got, resid, grad_resid, hidden, gains, output, input_grad, flag):
    flag[...] = jnp.zeros((8, LANES), FULL)
    output[...] = (resid[0] + (mine[...] + got[0].astype(FULL))).astype(LOW)
    x = hidden[...].astype(FULL)
    inverse = inverse_rms(x)
    grad = (more[...] + got[1].astype(FULL)) * gains[0:1, :]
    input_grad[...] = (grad_resid[...] + norm_back(grad, x * inverse, inverse)).astype(LOW)


def finish(coords, ins, wait):
    return call(end_kernel, coords, ins, [((128, 1024), LOW)] * 2 + [((8, LANES), FULL)], [], wait=wait)


def resid_kernel(coords, total, got, h0, h2, gains, resid, low):
    for d, hidden in enumerate((h0, h2)):
        value = hidden[...].astype(FULL) + (total[d] + got[1 - d].astype(FULL))
        resid[d] = value
        low[d] = (value * inverse_rms(value) * gains[1:2, :]).astype(LOW)


def residual(coords, total, got, h0, h2, gains, wait):
    outs = [((2, 128, 1024), FULL), ((2, 128, 1024), LOW)]
    return call(resid_kernel, coords, [total, got, h0, h2, gains], outs, [], wait=wait)


def turn_kernel(coords, total, got, g0, g2, resid, gains, grad_resid, low, gain_sum):
    for d, upstream in enumerate((g0, g2)):
        value = resid[d]
        inverse = inverse_rms(value)
        normal = value * inverse
        grad = total[d] + got[1 - d].astype(FULL)
        back = upstream[...].astype(FULL) + norm_back(grad * gains[1:2, :], normal, inverse)
        low[d] = back.astype(LOW)
        if d == 0:
            grad_resid[...] = back
            gain_sum[...] = jnp.sum(grad * normal, 0, keepdims=True)


def turn_back(coords, total, got, g0, g2, resid, gains, wait):
    outs = [((128, 1024), FULL), ((2, 128, 1024), LOW), ((1, 1024), FULL)]
    return call(turn_kernel, coords, [total, got, g0, g2, resid, gains], outs, [], wait=wait)


def body(
    hidden,
    cotangent,
    segment_ids,
    positions,
    attention_gain,
    query_weight,
    key_weight,
    value_weight,
    query_gain,
    key_gain,
    headgate_weight,
    headgate_bias,
    output_weight,
    feedforward_gain,
    gate_weight,
    up_weight,
    down_weight,
):
    core = lax.axis_index("core")
    x_at, y_at = lax.axis_index("x"), lax.axis_index("y")
    j = lax.axis_index("zl") * 2 + core
    coords = jnp.stack([jnp.where(core == 0, x_at, y_at), jnp.where(core == 0, y_at, x_at), j]).astype(jnp.int32)

    freq = jnp.power(jnp.float32(THETA), -jnp.arange(64, dtype=FULL) * 2.0 / HEAD)
    angle = positions.astype(FULL)[:, None] * freq[None, :]
    cosine, sine = jnp.cos(angle), jnp.sin(angle)
    cosine, sine = jnp.concatenate([cosine, cosine], 1), jnp.concatenate([-sine, sine], 1)
    across = swap(hidden, "zl")
    across, gate_weight, up_weight = together(across, gate_weight, up_weight)
    tokens = (hidden, swap(hidden, "core"), across, swap(across, "core"))
    line = [attention_gain, feedforward_gain, jnp.pad(query_gain, (0, 96)), jnp.pad(key_gain, (0, 96))]
    small = (headgate_weight.T, jnp.concatenate(line)[None])
    mine, got, near, far = take_columns(coords, (query_weight, key_weight, value_weight), (512, 256, 256), small)
    far, near = swap_far(far), swap(near, "zl")
    mine_gu, got_gu, last_gu, near_gu, far_gu, more_gu = take_columns(
        coords, (gate_weight, up_weight), (768, 768), (), (cosine,)
    )
    far, far_gu = together(far, far_gu)
    far_gu = swap_far(far_gu)
    near, cotangent, near_gu = together(near, cotangent, near_gu)
    grads = list(group_gather(cotangent))
    near_gu = swap(near_gu, "zl")
    weight_qkv = (mine, got, far, near)

    bias = jnp.pad(headgate_bias, (0, 124))[None]

    (keep, send, attn_in, raw, qk, val, probs, attended, gates, mixed, hw, gains, cosine, sine) = attention_forward(
        coords, tokens, weight_qkv, output_weight, cosine, sine, segment_ids.reshape(4, 128), bias
    )
    far_gu, last_gu, more_gu = together(far_gu, last_gu, more_gu)
    weight_gu = (mine_gu, got_gu, far_gu, swap_far(more_gu), swap_far(last_gu), near_gu)
    far_gu, near_gu, grads[2], send = together(far_gu, near_gu, grads[2], send)
    total, low = chip_sum(coords, keep, send)
    got = swap(low, "zl")
    resid, ffn_in = residual(coords, total, got, tokens[0], tokens[2], gains, weight_gu[3:5])
    keep, send, ffn, grads_all, grad_gu, act, wd_low = feed_forward(
        coords, (ffn_in, swap(ffn_in, "core")), weight_gu, down_weight, grads
    )
    total, low = chip_sum(coords, keep, send)
    low, grad_gu = together(low, grad_gu)
    pieces, part = spread(coords, ffn, [grad_gu], [swap(grad_gu, "core")], act, grads_all)
    got = swap(low, "zl")
    first = exchange(pieces, 0, 0)
    grad_resid, resid_low, grad_gain_second = turn_back(
        coords, total, got, grads[0], grads[2], resid, gains, (pieces[0],)
    )
    saved = (qk, val, probs, attended, gates, raw, gains, cosine, sine)
    front, resid_low, *others = back_first(coords, (resid_low, swap(resid_low, "core")), output_weight, saved)
    first = merge(coords, half_sum_kernel, first, (4,) * 4, (front,), 1)
    keep, send, back, small = back_second(
        coords,
        resid_low,
        output_weight,
        saved,
        (front, *others),
        (attn_in, hw, *weight_qkv, *tokens, grad_gain_second),
        first[:1],
    )
    first = exchange(first, 0, 1)
    pieces, part_second = spread(
        coords,
        attn_in,
        [front, back],
        [swap(front, "core"), swap(back, "core")],
        mixed,
        resid_low,
        (small, swap(small, "core")),
        first[2:],
    )
    second = exchange(pieces, 0, 0)
    first = exchange(merge(coords, turn_sum_kernel, first, (2,) * 4, pieces[:1], 1), 1, 0)
    sums = group_scatter(coords, down(coords, act, wd_low, first[:1]), (keep, send), ())
    first = exchange(merge(coords, half_sum_kernel, first, (1,) * 4, sums[:1], 1), 1, 1)
    second = exchange(merge(coords, half_sum_kernel, second, (4,) * 4, first[:1]), 0, 1)
    height = 2 * pieces[0].shape[1]
    first = send_across(*last_sum(coords, first, part, (second[0], sums[2])))
    second = direct(
        small_kernel_call(coords, quarter_sum_kernel, second, [(height, LANES)] * 4, first[2:3])
    )
    first = cross_sum(coords, first, second[:1])
    first = exchange(first * 2, 1, 1)
    shapes = [(part_second, LANES), (height - part_second, LANES)]
    second = send_across(*small_kernel_call(coords, direct_sum_kernel, second, shapes, first[:1]))
    first = merge(coords, join_kernel, first, (2, 2), second[2:3])
    first = exchange(first * 2, 1, 0)
    (second,) = small_kernel_call(coords, plain_sum_kernel, second, [(height, LANES)], first[:1])
    first = merge(coords, pack_kernel, first, (4, 4), (second,))
    first = exchange(first * 2, 0, 1)
    second = direct([second] * 4)
    first = merge(coords, join_kernel, first, (8, 8), second[:1])
    second = small_kernel_call(
        coords, direct_pack_kernel, second, [(4, height // 2, LANES)] * 2, first[:1]
    )
    first = exchange(first * 2, 0, 0)
    second = merge(coords, join_kernel, exchange(second * 2, 0, 1), (8, 8), ())
    output, input_grad, finished = finish(coords, [*sums, resid, grad_resid, hidden, gains], second[:1])
    grad_g, grad_u, grad_d, settled = settle(coords, first, (768, 768), 768, False, (finished,))
    second = exchange(second * 2, 0, 0)
    (grad_q, grad_k, grad_v, grad_o, small_first, small_second, small_q, small_k, small_bias, grad_hw) = settle(
        coords, second, (512, 256, 256), 512, True, (settled,)
    )
    return (
        output,
        input_grad,
        small_first.reshape(256),
        grad_q,
        grad_k,
        grad_v,
        small_q.reshape(32),
        small_k.reshape(32),
        grad_hw.T,
        small_bias.reshape(4),
        grad_o,
        small_second.reshape(256),
        grad_g,
        grad_u,
        grad_d,
    )


def solution(mesh):
    grid = Mesh(mesh.devices.reshape(2, 4, 4, 2, 2), AXES)
    tokens, split, copies = P(AXES, None), P(GROUP, None), P(("zh", "y", "x"))
    line = P(GROUP)
    weights = (line, split, split, split, line, line, split, line, split, line, split, split, split)
    return jax.shard_map(
        body,
        mesh=grid,
        in_specs=(tokens, tokens, copies, copies, *weights),
        out_specs=(tokens, tokens, *weights),
        check_vma=False,
    )
```

```python
import functools
import math

import jax
import jax.numpy as jnp
from jax import lax
from jax.experimental import pallas as pl
from jax.experimental.pallas import tpu as pltpu
from jax.sharding import Mesh
from jax.sharding import PartitionSpec as P

EPS = 1e-06
THETA = 1000000.0
MASKED = -1e30
HEAD = 128
SCALE = 1.0 / math.sqrt(HEAD)
LOW = jnp.bfloat16
FULL = jnp.float32
AXES = ("zh", "y", "x", "zl", "core")
GROUP = ("zl", "core")
LANES = 128


def swap(value, axis):
    return lax.ppermute(value, axis, [(0, 1), (1, 0)])


def turn(value, step):
    return lax.ppermute(value, ("zh", "zl"), [(i, (i + step) % 4) for i in range(4)])


def swap_far(value):
    return lax.ppermute(value, ("zh", "zl"), [(0, 3), (3, 0), (1, 2), (2, 1)])


def swap_plane(value, axis, mask):
    pairs = []
    for y in range(4):
        for x in range(4):
            for core in range(2):
                to_y, to_x = (y, x ^ mask) if axis == core else (y ^ mask, x)
                pairs.append(((y * 4 + x) * 2 + core, (to_y * 4 + to_x) * 2 + core))
    return lax.ppermute(value, ("y", "x", "core"), pairs)


def dot(left, right):
    return jnp.dot(left, right, preferred_element_type=FULL)


def dot_t(left, right):
    return lax.dot_general(left, right, (((1,), (1,)), ((), ())), preferred_element_type=FULL)


def dot_tn(left, right):
    return lax.dot_general(left, right, (((0,), (0,)), ((), ())), preferred_element_type=FULL)


VMEM = pl.BlockSpec(memory_space=pltpu.VMEM)
SMEM = pl.BlockSpec(memory_space=pltpu.SMEM)


def held_bytes(shape, kind):
    shape = (1,) * (2 - len(shape)) + tuple(shape)
    size = math.prod(shape[:-2]) * (-(-shape[-2] // 16) * 16) * (-(-shape[-1] // LANES) * LANES)
    return size * jnp.dtype(kind).itemsize


class Late:
    def __init__(self, source, target, done):
        self.copy, self.target, self.open = pltpu.make_async_copy(source, target, done), target, True
        self.copy.start()

    def ready(self):
        if self.open:
            self.copy.wait()
        self.open = False
        return self.target


class Early:
    def __init__(self, source, target, done):
        self.copy, self.source, self.sent = pltpu.make_async_copy(source, target, done), source, False

    def send(self):
        if not self.sent:
            self.copy.start()
        self.sent = True


def call(kernel, coords, ins, outs, scratch, late=(), early=(), least=0, wait=(), flops=1):
    ins = list(ins)
    n_ins, n_outs, n_scratch = len(ins), len(outs), len(scratch)
    moving = [(ins[i].shape, ins[i].dtype) for i in late] + [outs[i] for i in early]

    def run(coords, *refs):
        refs = list(refs)
        del refs[n_ins : n_ins + len(wait)]
        done = refs.pop() if moving else None
        buffers = refs[n_ins + n_outs + n_scratch :]
        refs = refs[: n_ins + n_outs + n_scratch]
        for k, i in enumerate(late):
            refs[i] = Late(refs[i], buffers[k], done.at[k])
        sending = []
        for k, i in enumerate(early):
            k += len(late)
            sending.append(Early(buffers[k], refs[n_ins + i], done.at[k]))
            refs[n_ins + i] = sending[-1]
        kernel(coords, *refs)
        for i in late:
            refs[i].ready()
        for out in sending:
            out.send()
        for out in sending:
            out.copy.wait()

    need = sum(held_bytes(a.shape, a.dtype) for a in ins) + sum(held_bytes(*o) for o in [*outs, *scratch])
    anywhere = pl.BlockSpec(memory_space=pltpu.HBM)
    buffers = [pltpu.VMEM(shape, kind) for shape, kind in [*scratch, *moving]]
    return pl.pallas_call(
        run,
        out_shape=[jax.ShapeDtypeStruct(shape, kind) for shape, kind in outs],
        in_specs=[SMEM] + [anywhere if i in late else VMEM for i in range(n_ins)] + [pl.BlockSpec(memory_space=pl.ANY)] * len(wait),
        out_specs=[anywhere if i in early else VMEM for i in range(n_outs)],
        scratch_shapes=buffers + ([pltpu.SemaphoreType.DMA((len(moving),))] if moving else []),
        compiler_params=pltpu.CompilerParams(vmem_limit_bytes=max(need + 8 * 2**20, least * 2**20)),
        cost_estimate=pl.CostEstimate(flops=flops, bytes_accessed=1, transcendentals=0),
    )(coords, *ins, *wait)


def lanes(index, width):
    return pl.ds(pl.multiple_of(index * width, LANES), width)


def rows(index, height):
    return pl.ds(pl.multiple_of(index * height, 16), height)


def inverse_rms(value):
    return lax.rsqrt(jnp.mean(value * value, -1, keepdims=True) + EPS)


def norm_back(grad, normal, inverse):
    return inverse * (grad - normal * jnp.mean(grad * normal, -1, keepdims=True))


def cut_kernel(widths, small, coords, *refs):
    ins, outs = refs[: len(widths)], refs[len(widths) + 2 * small :]
    j = coords[2]
    if small:
        heads, line = refs[len(widths) : len(widths) + 2]
        line = jnp.concatenate([line[...], jnp.zeros((15, 768), FULL)], 0)
        tile = jnp.concatenate([heads[...], line], 1).astype(LOW)
    third = [(3, 0, 256)] if small else [(3, 0, 128), (3, 128, 128)]
    for out, (r, first, count) in zip(outs, [(1, 0, 256), *third, (2, 0, 256), (0, 0, 256)]):
        at = 0
        for w, n in zip(ins, widths):
            out[0:count, at : at + n] = w[first : first + count, lanes(j ^ r, n)].astype(LOW)
            at += n
        if small:
            out[256:272, :] = tile


def take_columns(coords, weights, widths, small=(), wait=()):
    heights = (272,) * 4 if small else (256, 128, 128, 256, 256)
    beside, *across, other, mine = call(
        functools.partial(cut_kernel, widths, bool(small)),
        coords,
        [*weights, *small],
        [((n, sum(widths)), LOW) for n in heights],
        [],
        least=50,
        wait=wait,
    )
    return mine, swap(beside, "core"), other, *[swap(piece, "core") for piece in across]


def first_kernel(coords, t0, t1, t2, t3, w0, w1, w2, w3, wo, cos, sin, segs, bias, *refs):
    (keep, send, attn_in, raw, qk, val, probs, attended, gates, mixed, hw, gains, cos_rel, sin_rel) = refs[:14]
    (wo_low, mask) = refs[14:]
    (attn_out, raw_out, qk_out, val_out, probs_out, att_out, gates_out, mixed_out) = refs[2:10]
    attn_in, raw, qk, val, probs, attended, gates, mixed = [r.source for r in refs[2:10]]
    cos_out, sin_out = refs[12:14]
    cos_rel, sin_rel = cos_out.source, sin_out.source
    j = coords[2]
    tokens, weights = (t0, t1, t2, t3), (w0, w1, w2, w3)
    hw[...] = jnp.zeros_like(hw)
    gains[...] = jnp.zeros_like(gains)
    gain_q, gain_k = jnp.zeros((16, LANES), FULL), jnp.zeros((16, LANES), FULL)
    for r in range(4):
        small = weights[r][256:272, :]
        hw[0:16, lanes(j ^ r, 256)] = small[:, 0:256]
        small = small[:, 256:].astype(FULL)
        gains[0:1, lanes(j ^ r, 256)] = small[0:1, 0:256]
        gains[1:2, lanes(j ^ r, 256)] = small[0:1, 256:512]
        gain_q += pltpu.roll(small[:, 512:640], (j ^ r) * 32, 1)
        gain_k += pltpu.roll(small[:, 640:768], (j ^ r) * 32, 1)
        cos_rel[r * 128 : r * 128 + 128, :] = cos.ready()[rows(j ^ r, 128), :]
        sin_rel[r * 128 : r * 128 + 128, :] = sin.ready()[rows(j ^ r, 128), :]
    gains[2:3, 0:128] = gain_q[0:1]
    gains[2:3, 128:256] = gain_k[0:1]
    for r in range(4):
        x = tokens[r][0:128, :].astype(FULL)
        attn_in[r * 128 : r * 128 + 128, :] = (x * inverse_rms(x) * gains[0:1, :]).astype(LOW)

    attn_out.send()
    cos_out.send()
    sin_out.send()

    logit = dot_t(attn_in[...], hw[...])
    logit = pltpu.roll(logit, (32 - j) * 4 & 127, 1) + bias[...].astype(LOW).astype(FULL)
    gates[...] = jax.nn.sigmoid(logit)
    gates_out.send()
    for n in range(4):
        total = dot(attn_in[:, lanes(j, 256)], w0[0:256, n * 256 : n * 256 + 256])
        for r in range(1, 4):
            total += dot(attn_in[:, lanes(j ^ r, 256)], weights[r][0:256, n * 256 : n * 256 + 256])
        if n < 3:
            raw[:, n * 256 : n * 256 + 256] = total
        else:
            val[...] = total.astype(LOW)
    raw_out.send()
    val_out.send()
    for h in range(6):
        at = slice(h * 128, h * 128 + 128)
        part = raw[:, at]
        gain = gains[2:3, 0:128] if h < 4 else gains[2:3, 128:256]
        part = part * inverse_rms(part) * gain
        qk[:, at] = (part * cos_rel[...] + pltpu.roll(part, 64, 1) * sin_rel[...]).astype(LOW)

    qk_out.send()
    lane = lax.broadcasted_iota(jnp.int32, (128, 128), 1)
    line = lax.broadcasted_iota(jnp.int32, (128, 128), 0)
    for c in range(4):
        seg_q = jnp.broadcast_to(segs[pl.ds(j ^ c, 1), :], (128, 128)).T
        for b in range(4):
            seg_k = segs[pl.ds(j ^ b, 1), :]
            earlier = lane + (j ^ b) * 128 <= line + (j ^ c) * 128
            mask[c * 128 : c * 128 + 128, b * 128 : b * 128 + 128] = jnp.where(
                earlier & (seg_q == seg_k), 0.0, MASKED
            )
    for h in range(4):
        kv = h // 2
        for c in range(2):
            at = slice(c * 256, c * 256 + 256)
            scores = dot_t(qk[at, h * 128 : h * 128 + 128], qk[:, 512 + kv * 128 : 640 + kv * 128])
            scores = scores * SCALE + mask[at, :]
            expo = jnp.exp(scores - jnp.max(scores, -1, keepdims=True))
            part = (expo * (1.0 / jnp.sum(expo, -1, keepdims=True))).astype(LOW)
            probs[h, at, :] = part
            result = dot(part, val[:, kv * 128 : kv * 128 + 128])
            attended[at, h * 128 : h * 128 + 128] = result
            mixed[at, h * 128 : h * 128 + 128] = (result * gates[at, h : h + 1]).astype(LOW)
    probs_out.send()
    att_out.send()
    mixed_out.send()
    wo_low[...] = wo.ready()[...].astype(LOW)
    for n in range(4):
        at = slice(n * 256, n * 256 + 256)
        result = dot(mixed[...], wo_low[:, at])
        for c in range(2):
            keep[c, :, at] = result[c * 256 : c * 256 + 128]
            send[c, :, at] = result[c * 256 + 128 : c * 256 + 256].astype(LOW)


def attention_forward(coords, tokens, weights, wo, cos, sin, segs, bias):
    outs = [
        ((2, 128, 1024), FULL),
        ((2, 128, 1024), LOW),
        ((512, 1024), LOW),
        ((512, 768), FULL),
        ((512, 768), LOW),
        ((512, 256), LOW),
        ((4, 512, 512), LOW),
        ((512, 512), FULL),
        ((512, 128), FULL),
        ((512, 512), LOW),
        ((128, 1024), LOW),
        ((8, 1024), FULL),
        ((512, 128), FULL),
        ((512, 128), FULL),
    ]
    return call(
        first_kernel,
        coords,
        [*tokens, *weights, wo, cos, sin, segs, bias],
        outs,
        [((512, 1024), LOW), ((512, 512), FULL)],
        (9, 10, 8),
        (2, 3, 4, 5, 6, 7, 8, 9, 12, 13),
    )


def ffn_kernel(coords, f_own, f_got, w0, w1, w2, w3_low, w3_high, wd, g0, g1, g2, g3, *refs):
    (keep, send, ffn, grads, grad_gu, act, wd_low, w3) = refs
    j = coords[2]
    weights = (w0, w1, w2, w3)
    w3[0:128, :] = w3_low[...]
    w3[128:256, :] = w3_high[...]
    for r, g in enumerate((g0, g1, g2, g3)):
        ffn[r * 128 : r * 128 + 128, :] = (f_got if r % 2 else f_own)[r // 2]
        grads[r * 128 : r * 128 + 128, :] = g[...]
    wd_low[...] = wd[...].astype(LOW)
    for m in range(2):
        at = slice(m * 256, m * 256 + 256)
        for n in range(3):
            low, high = slice(n * 256, n * 256 + 256), slice(768 + n * 256, 1024 + n * 256)
            gate = dot(ffn[at, lanes(j, 256)], w0[:, low])
            up = dot(ffn[at, lanes(j, 256)], w0[:, high])
            for r in range(1, 4):
                gate += dot(ffn[at, lanes(j ^ r, 256)], weights[r][:, low])
                up += dot(ffn[at, lanes(j ^ r, 256)], weights[r][:, high])
            back = dot_t(grads[at, :], wd_low[low, :])
            sigma = jax.nn.sigmoid(gate)
            swish = gate * sigma
            act[at, low] = (swish * up).astype(LOW)
            grad_gu[at, low] = (back * up * sigma * (1.0 + gate * (1.0 - sigma))).astype(LOW)
            grad_gu[at, high] = (back * swish).astype(LOW)
    for r in range(4):
        part = dot_t(grad_gu[...], weights[r][...])
        for t in range(2):
            keep[t, :, lanes(j ^ r, 256)] = part[t * 256 : t * 256 + 128]
            send[t, :, lanes(j ^ r, 256)] = part[t * 256 + 128 : t * 256 + 256].astype(LOW)


def feed_forward(coords, ffn_in, weights, wd, grads):
    outs = [
        ((2, 128, 1024), FULL),
        ((2, 128, 1024), LOW),
        ((512, 1024), LOW),
        ((512, 1024), LOW),
        ((512, 1536), LOW),
        ((512, 768), LOW),
        ((768, 1024), LOW),
    ]
    return call(
        ffn_kernel,
        coords,
        [*ffn_in, *weights, wd, *grads],
        outs,
        [((256, 1536), LOW)],
    )


def down_kernel(coords, act, wd_low, keep, send):
    for c in range(4):
        result = dot(act[c * 128 : c * 128 + 128, :], wd_low[...])
        if c % 2:
            send[c // 2] = result.astype(LOW)
        else:
            keep[c // 2] = result


def down(coords, act, wd_low, wait):
    outs = [((2, 128, 1024), FULL), ((2, 128, 1024), LOW)]
    return call(down_kernel, coords, [act, wd_low], outs, [], wait=wait)


def heads_back(kv, refs, resid_low, wo_low, grad_scores, out):
    (qk, val, probs, attended, gates, raw, gains, cos, sin) = refs
    lane = lax.broadcasted_iota(jnp.int32, (512, LANES), 1)
    grad_logit = jnp.zeros((512, LANES), FULL)
    gain_sums = []

    def head_back(grad, at, gain, to):
        part = raw[:, at]
        inverse = inverse_rms(part)
        normal = part * inverse
        turned = grad * cos[...] - pltpu.roll(grad, 64, 1) * sin[...]
        gain_sums.append(jnp.sum(turned * normal, 0, keepdims=True))
        out[:, to : to + 128] = norm_back(turned * gain, normal, inverse).astype(LOW)

    key_at = slice(512 + kv * 128, 640 + kv * 128)
    grad_key = grad_value = None
    for n, h in enumerate((2 * kv, 2 * kv + 1)):
        at = slice(h * 128, h * 128 + 128)
        grad_mixed = dot_t(resid_low[...], wo_low[n * 128 : n * 128 + 128, :])
        gate = gates[:, h : h + 1]
        grad_gate = jnp.sum(grad_mixed * attended[:, at], -1, keepdims=True) * gate * (1.0 - gate)
        grad_logit = jnp.where(lane == h, grad_gate, grad_logit)
        grad_att = (grad_mixed * gate).astype(LOW)
        for c in range(2):
            line = slice(c * 256, c * 256 + 256)
            grad_probs = dot_t(grad_att[line], val[:, kv * 128 : kv * 128 + 128])
            part = probs[h, line, :].astype(FULL)
            inner = jnp.sum(part * grad_probs, -1, keepdims=True)
            grad_scores[line, :] = (part * (grad_probs - inner)).astype(LOW)
        head_back(dot(grad_scores[...], qk[:, key_at]) * SCALE, at, gains[2:3, 0:128], n * 128)
        more_key = dot_tn(grad_scores[...], qk[:, at])
        more_value = dot_tn(probs[h], grad_att)
        grad_key = more_key if grad_key is None else grad_key + more_key
        grad_value = more_value if grad_value is None else grad_value + more_value
    head_back(grad_key * SCALE, key_at, gains[2:3, 128:256], 256)
    out[:, 384:512] = grad_value.astype(LOW)
    return grad_logit, gain_sums


def back_first_kernel(coords, l_own, l_got, wo, qk, val, probs, attended, gates, raw, gains, cos, sin, *refs):
    (out, resid_low, logit, sums, wo_low, grad_scores) = refs
    wo_low[...] = wo.ready()[0:256, :].astype(LOW)
    for r in range(4):
        resid_low[r * 128 : r * 128 + 128, :] = (l_got if r % 2 else l_own)[r // 2]
    refs = [r.ready() for r in (qk, val, probs, attended, gates, raw, gains, cos, sin)]
    grad_logit, gain_sums = heads_back(0, refs, resid_low, wo_low, grad_scores, out)
    logit[...] = grad_logit
    sums[...] = jnp.zeros_like(sums)
    for i, value in enumerate(gain_sums):
        sums[i : i + 1, :] = value


def back_kernel(coords, *refs):
    (resid_low, wo, qk, val, probs, attended, gates, raw, gains, cos, sin, out_first, logit, sums) = refs[:14]
    (attn_in, hw, w0, w1, w2, w3, t0, t1, t2, t3, gain_second) = refs[14:25]
    (keep, send, out, small) = refs[25:29]
    (wo_low, grad_scores, grad_qkv) = refs[29:]
    j = coords[2]
    wo_low[...] = wo.ready()[256:512, :].astype(LOW)
    refs = [r.ready() for r in (qk, val, probs, attended, gates, raw, gains, cos, sin)]
    grad_logit, gain_sums = heads_back(1, refs, resid_low, wo_low, grad_scores, out)
    for kv, part in enumerate((out_first, out)):
        grad_qkv[:, kv * 256 : kv * 256 + 256] = part[:, 0:256]
        grad_qkv[:, 512 + kv * 128 : 640 + kv * 128] = part[:, 256:384]
        grad_qkv[:, 768 + kv * 128 : 896 + kv * 128] = part[:, 384:512]

    weights, tokens = [[r.ready() for r in group] for group in ((w0, w1, w2, w3), (t0, t1, t2, t3))]
    attn_in, hw = attn_in.ready(), hw.ready()
    grad_logit = (grad_logit + logit[...]).astype(LOW)
    grad_bias = jnp.sum(grad_logit.astype(FULL), 0, keepdims=True)
    grad_hw = dot_tn(grad_logit, attn_in[...])
    spread_logit = pltpu.roll(grad_logit.astype(FULL), j * 4, 1).astype(LOW)
    inverses = []
    for r in range(4):
        x = tokens[r][0:128, :].astype(FULL)
        inverses.append(inverse_rms(x))
    small[...] = jnp.zeros_like(small)

    def put(row, value):
        small[row // 4, row % 4 : row % 4 + 1, :] = value

    for r in range(4):
        at = lanes(j ^ r, 256)
        part = dot_t(grad_qkv[...], weights[r][0:256, :]) + dot(spread_logit, hw[:, at])
        total = jnp.zeros((1, 256), FULL)
        for t in range(4):
            piece = part[t * 128 : t * 128 + 128]
            normal = tokens[t][0:128, at].astype(FULL) * inverses[t]
            total += jnp.sum(piece * normal, 0, keepdims=True)
            if t % 2:
                send[t // 2, :, at] = piece.astype(LOW)
            else:
                keep[t // 2, :, at] = piece
        block = (j ^ r) // 2
        for i in range(2):
            small[block, pl.ds((j ^ r) % 2 * 2 + i, 1), :] = total[:, i * 128 : i * 128 + 128]
    for i in range(8):
        put(8 + i, gain_second[0:1, i * 128 : i * 128 + 128])
    put(16, gain_sums[0] + gain_sums[1] + sums[0:1, :] + sums[1:2, :])
    put(17, gain_sums[2] + sums[2:3, :])
    put(18, grad_bias)
    for h in range(4):
        for i in range(8):
            put(24 + h * 8 + i, grad_hw[h : h + 1, i * 128 : i * 128 + 128])


def back_first(coords, resid_low, wo, saved):
    outs = [((512, 512), LOW), ((512, 1024), LOW), ((512, 128), FULL), ((8, 128), FULL)]
    scratch = [((256, 1024), LOW), ((512, 512), LOW)]
    return call(back_first_kernel, coords, [*resid_low, wo, *saved], outs, scratch, range(2, 12), flops=3*10**9)


def back_second(coords, resid_low, wo, saved, first, others, wait):
    outs = [((2, 128, 1024), FULL), ((2, 128, 1024), LOW), ((512, 512), LOW), ((16, 8, 128), FULL)]
    scratch = [((256, 1024), LOW), ((512, 512), LOW), ((512, 1024), LOW)]
    ins = [resid_low, wo, *saved, *first, *others]
    late = [*range(1, 11), *range(14, 24)]
    return call(back_kernel, coords, ins, outs, scratch, late, wait=wait)


KEPT, SENT, MASKS = ((0, 3), (0, 1)), ((1, 2), (3, 2)), ((1, 3), (3, 1))


def spread_kernel(n_right, with_small, coords, left_c, *refs):
    rights, (left_r, right_r, *refs) = refs[: 2 * n_right], refs[2 * n_right :]
    if with_small:
        small_own, small_got, *refs = refs
    outs, (turned_c, turned_r, held_c, held_r) = refs[:4], refs[4:]
    first, second, j = coords[0], coords[1], coords[2]
    wide = rights[0].shape[1] // LANES
    panels = wide * n_right
    rows_r = left_r.shape[1] // 16
    part = 2 * panels * 16 + (16 if with_small else 0)
    edge = outs[0].shape[1]
    blocks = [(m, n, (first ^ m) * 4 + (second ^ n)) for m in (1, 2, 3, 0) for n in range(4)]

    def put(m, n, low, value):
        stream = 0 if low < edge else 1
        sent = m in SENT[stream]
        at = (SENT if sent else KEPT)[stream].index(m) * 4 + n
        low -= edge * stream
        outs[2 * sent + stream][at, low : low + value.shape[0], :] = value

    for d in range(2):
        turned = left_c[:, lanes(j ^ (2 * d), 256)].T
        turned_c[d] = turned
        for t in range(4):
            turned_c[2 + d, :, t * 128 : t * 128 + 128] = turned[:, (t ^ 1) * 128 : (t ^ 1) * 128 + 128]
    turned_r[...] = left_r[...].T
    for k, right in enumerate(rights):
        src, start = k // n_right, k % n_right * wide
        for d in range(2):
            held_c[...] = dot(turned_c[2 * src + d], right[...]).astype(LOW)
            for m, n, block in blocks:
                for p in range(wide):
                    low = (1 - d) * part + (src * panels + start + p) * 16
                    put(m, n, low, held_c[rows(block, 16), p * LANES : (p + 1) * LANES])
    held_r[...] = dot(turned_r[...], right_r[...]).astype(LOW)
    for m, n, block in blocks:
        if with_small:
            tile = jnp.concatenate([small_own[block], small_got[block]], 0).astype(LOW)
            put(m, n, part - 16, tile)
            put(m, n, 2 * part - 16, tile)
        for p in range(8):
            put(m, n, 2 * part + p * rows_r, held_r[rows(block, rows_r), p * LANES : (p + 1) * LANES])


def spread(coords, left_c, own, got, left_r, right_r, small=(), wait=()):
    wide = own[0].shape[1]
    panels = wide * len(own) // LANES
    part = 2 * panels * 16 + (16 if small else 0)
    height = 2 * part + left_r.shape[1] // 2
    scratch = [
        ((4, 256, 512), LOW),
        ((left_r.shape[1], 512), LOW),
        ((256, wide), LOW),
        ((left_r.shape[1], 1024), LOW),
    ]
    pieces = call(
        functools.partial(spread_kernel, len(own), bool(small)),
        coords,
        [left_c, *own, *got, left_r, right_r, *small],
        [((8, height // 2, LANES), LOW)] * 4,
        scratch,
        wait=wait,
    )
    return pieces, part


def plus(a, b):
    return (a.astype(FULL) + b.astype(FULL)).astype(LOW)


def half_sum_kernel(coords, p, q, got_p, got_q, *outs):
    half = p.shape[0] // 2
    for kept, sent, mine, got in ((outs[0], outs[2], p, got_p), (outs[1], outs[3], q, got_q)):
        kept[...] = plus(mine[0:half], got[0:half])
        sent[...] = plus(mine[half:], got[half:])


def turn_sum_kernel(coords, p, q, got_p, got_q, *outs):
    for s, (mine, got) in enumerate(((p, got_p), (q, got_q))):
        for at in range(2):
            outs[s][at] = plus(mine[KEPT[s][at]], got[KEPT[s][at]])
            outs[2 + s][at] = plus(mine[SENT[s][at]], got[SENT[s][at]])


def last_sum_kernel(coords, p, q, got_p, got_q, other, mine):
    part, edge = other.shape[0], p.shape[1]
    p, q = plus(p[0], got_p[0]), plus(q[0], got_q[0])
    other[...] = p[:part]
    mine[0 : edge - part, :] = p[part:]
    mine[edge - part :, :] = q


def cross_sum_kernel(coords, ahead, behind, mine, far, p, q):
    part, edge = ahead.shape[0], p.shape[1]
    p[0, 0:part, :] = plus(ahead[...], behind[...])
    mine = plus(mine[...], far[...])
    p[0, part:, :] = mine[: edge - part]
    q[0] = mine[edge - part :]


def quarter_sum_kernel(coords, p, q, got_p, got_q, *outs):
    edge = p.shape[1]
    for n in range(4):
        outs[n][0:edge, :] = plus(p[n], got_p[n])
        outs[n][edge:, :] = plus(q[n], got_q[n])


def direct_sum_kernel(coords, a, b, c, d, other, mine):
    total = (a[...].astype(FULL) + b[...].astype(FULL) + c[...].astype(FULL) + d[...].astype(FULL)).astype(LOW)
    part = other.shape[0]
    other[...] = total[:part]
    mine[...] = total[part:]


def plain_sum_kernel(coords, ahead, behind, mine, far, out):
    part = ahead.shape[0]
    out[0:part, :] = plus(ahead[...], behind[...])
    out[part:, :] = plus(mine[...], far[...])


def direct_pack_kernel(coords, a, b, c, d, p, q):
    edge = p.shape[1]
    for n, ref in enumerate((a, b, c, d)):
        p[n] = ref[0:edge, :]
        q[n] = ref[edge:, :]


def direct(parts):
    return [parts[0]] + [swap_plane(parts[m], 1, m) for m in (1, 2, 3)]


def small_kernel_call(coords, kernel, got, shapes, wait, flops=4 * 10**9):
    return call(kernel, coords, got, [(shape, LOW) for shape in shapes], [], wait=wait, flops=flops)


def join_kernel(coords, p, q, got_p, got_q, both_p, both_q):
    half = p.shape[0]
    for both, mine, got in ((both_p, p, got_p), (both_q, q, got_q)):
        both[0:half] = mine[...]
        both[half:] = got[...]


def pack_kernel(coords, p, q, got_p, got_q, all_p, all_q):
    for s, (whole, mine, got) in enumerate(((all_p, p, got_p), (all_q, q, got_q))):
        for at in range(2):
            whole[KEPT[s][at]] = mine[at]
            whole[SENT[s][at]] = got[at]


def exchange(pieces, axis, step):
    return [*pieces[:2], *[swap_plane(pieces[2 + s], axis, MASKS[s][step]) for s in range(2)]]


def merge(coords, kernel, got, counts, wait, flops=4 * 10**9):
    outs = [((n, *got[0].shape[1:]), LOW) for n in counts]
    return call(kernel, coords, got, outs, [], wait=wait, flops=flops)


def send_across(other, mine):
    return [turn(other, 1), turn(other, -1), mine, turn(mine, 2)]


def last_sum(coords, got, part, wait):
    outs = [((part, LANES), LOW), ((2 * got[0].shape[1] - part, LANES), LOW)]
    return call(last_sum_kernel, coords, got, outs, [], wait=wait, flops=4 * 10**9)


def cross_sum(coords, got, wait):
    edge = (got[0].shape[0] + got[2].shape[0]) // 2
    return call(cross_sum_kernel, coords, got, [((1, edge, LANES), LOW)] * 2, [], wait=wait, flops=4 * 10**9)


def together(*values):
    return lax.optimization_barrier(values)


def settle_kernel(widths, with_small, coords, *refs):
    ins, outs = refs[:4], refs[4:]
    first, second, j = coords[0], coords[1], coords[2]
    panels = sum(widths) // LANES
    out_r = outs[len(widths)]
    rows_r = out_r.shape[0] // 16
    spots = []
    for kv in range(2 if with_small else 1):
        for w, width in enumerate(widths):
            count = width // LANES // (2 if with_small else 1)
            spots += [(w, (kv * count + i) * LANES) for i in range(count)]
    if with_small:
        total, heads = refs[-2:]
        total[...] = jnp.zeros_like(total)

    part = 2 * panels * 16 + (16 if with_small else 0)
    edge = ins[0].shape[1]

    def take(m, n, low, height):
        stream = 0 if low < edge else 1
        came = m in SENT[stream]
        at = (SENT if came else KEPT)[stream].index(m) * 4 + n
        low -= edge * stream
        return ins[2 * came + stream][at, low : low + height, :].astype(FULL)

    for m in range(4):
        for n in range(4):
            block = (first ^ m) * 4 + (second ^ n)
            line = rows(block, 16)
            for r in range(4):
                base = (1 - r // 2) * part + (r % 2) * panels * 16
                for p, (w, col) in enumerate(spots):
                    lane = pl.ds(pl.multiple_of((j ^ r) * widths[w] + col, LANES), LANES)
                    low = base + p * 16
                    outs[w][line, lane] = take(m, n, low, 16)
            for p in range(8):
                low = 2 * part + p * rows_r
                lane = slice(p * LANES, (p + 1) * LANES)
                out_r[rows(block, rows_r), lane] = take(m, n, low, rows_r)
            if with_small:
                for z in range(2):
                    tile = take(m, n, (1 - z) * part + part - 16, 16)
                    for src in range(2):
                        value = tile[src * 8 : src * 8 + 8]
                        heads[j ^ (2 * z + src), block] = value
                        total[block] += value
    if not with_small:
        outs[-1][...] = jnp.zeros((8, LANES), FULL)
    if with_small:
        gain_first, gain_second, gain_q, gain_k, bias, hw = outs[len(widths) + 1 : len(widths) + 7]
        for i in range(2):
            at = slice(i * 128, i * 128 + 128)
            gain_first[:, at] = total[j // 2, pl.ds(j % 2 * 2 + i, 1), :]
            gain_second[:, at] = total[2 + j // 2, pl.ds(j % 2 * 2 + i, 1), :]
        shift = (4 - j) * 32 & 127
        turned = pltpu.roll(total[4], shift, 1)
        gain_q[...] = turned[0:1, :32]
        gain_k[...] = turned[1:2, :32]
        bias[...] = heads[j, 4][2:3, :4]
        lines = []
        for q in range(4):
            for h in range(4):
                start = 24 + h * 8
                lines.append(
                    jnp.concatenate(
                        [heads[q, start // 4 + j // 2, pl.ds(j % 2 * 2 + i, 1), :] for i in range(2)], 1
                    )
                )
        whole = jnp.concatenate(lines, 0)
        hw[...] = whole


def settle(coords, pieces, widths, rows_r, with_small, wait):
    outs = [((256, 4 * w), FULL) for w in widths] + [((rows_r, 1024), FULL)]
    scratch = []
    if with_small:
        outs += [((1, n), FULL) for n in (256, 256, 32, 32, 4)] + [((16, 256), FULL)]
        scratch = [((16, 8, 128), FULL), ((4, 16, 8, 128), FULL)]
    else:
        outs += [((8, LANES), FULL)]
    return call(functools.partial(settle_kernel, widths, with_small), coords, pieces, outs, scratch, wait=wait)


def group_gather(part):
    beside = swap(part, "core")
    across = swap(part, "zl")
    return part, beside, across, swap(across, "core")


def add_kernel(coords, keep, got, total, low):
    value = keep[...] + got[...].astype(FULL)
    total[...] = value
    low[...] = value.astype(LOW)


def chip_sum(coords, keep, send, wait=()):
    outs = [((2, 128, 1024), FULL), ((2, 128, 1024), LOW)]
    return call(add_kernel, coords, [keep, swap(send, "core")], outs, [], wait=wait)


def own_kernel(coords, keep, got, more_keep, more_got, *outs):
    (mine, more, low) = outs
    for s, (kept, came, own) in enumerate(((keep, got, mine), (more_keep, more_got, more))):
        own[...] = kept[0] + came[0].astype(FULL)
        low[s] = (kept[1] + came[1].astype(FULL)).astype(LOW)


def group_scatter(coords, first, second, wait):
    ins = [first[0], swap(first[1], "core"), second[0], swap(second[1], "core")]
    outs = [((128, 1024), FULL)] * 2 + [((2, 128, 1024), LOW)]
    mine, more, low = call(own_kernel, coords, ins, outs, [], wait=wait)
    return mine, more, swap(low, "zl")


def end_kernel(coords, mine, more, got, resid, grad_resid, hidden, gains, output, input_grad, flag):
    flag[...] = jnp.zeros((8, LANES), FULL)
    output[...] = (resid[0] + (mine[...] + got[0].astype(FULL))).astype(LOW)
    x = hidden[...].astype(FULL)
    inverse = inverse_rms(x)
    grad = (more[...] + got[1].astype(FULL)) * gains[0:1, :]
    input_grad[...] = (grad_resid[...] + norm_back(grad, x * inverse, inverse)).astype(LOW)


def finish(coords, ins, wait):
    return call(end_kernel, coords, ins, [((128, 1024), LOW)] * 2 + [((8, LANES), FULL)], [], wait=wait)


def resid_kernel(coords, total, got, h0, h2, gains, resid, low):
    for d, hidden in enumerate((h0, h2)):
        value = hidden[...].astype(FULL) + (total[d] + got[1 - d].astype(FULL))
        resid[d] = value
        low[d] = (value * inverse_rms(value) * gains[1:2, :]).astype(LOW)


def residual(coords, total, got, h0, h2, gains, wait):
    outs = [((2, 128, 1024), FULL), ((2, 128, 1024), LOW)]
    return call(resid_kernel, coords, [total, got, h0, h2, gains], outs, [], wait=wait)


def turn_kernel(coords, total, got, g0, g2, resid, gains, grad_resid, low, gain_sum):
    for d, upstream in enumerate((g0, g2)):
        value = resid[d]
        inverse = inverse_rms(value)
        normal = value * inverse
        grad = total[d] + got[1 - d].astype(FULL)
        back = upstream[...].astype(FULL) + norm_back(grad * gains[1:2, :], normal, inverse)
        low[d] = back.astype(LOW)
        if d == 0:
            grad_resid[...] = back
            gain_sum[...] = jnp.sum(grad * normal, 0, keepdims=True)


def turn_back(coords, total, got, g0, g2, resid, gains, wait):
    outs = [((128, 1024), FULL), ((2, 128, 1024), LOW), ((1, 1024), FULL)]
    return call(turn_kernel, coords, [total, got, g0, g2, resid, gains], outs, [], wait=wait)


def body(
    hidden,
    cotangent,
    segment_ids,
    positions,
    attention_gain,
    query_weight,
    key_weight,
    value_weight,
    query_gain,
    key_gain,
    headgate_weight,
    headgate_bias,
    output_weight,
    feedforward_gain,
    gate_weight,
    up_weight,
    down_weight,
):
    core = lax.axis_index("core")
    x_at, y_at = lax.axis_index("x"), lax.axis_index("y")
    j = lax.axis_index("zl") * 2 + core
    coords = jnp.stack([jnp.where(core == 0, x_at, y_at), jnp.where(core == 0, y_at, x_at), j]).astype(jnp.int32)

    freq = jnp.power(jnp.float32(THETA), -jnp.arange(64, dtype=FULL) * 2.0 / HEAD)
    angle = positions.astype(FULL)[:, None] * freq[None, :]
    cosine, sine = jnp.cos(angle), jnp.sin(angle)
    cosine, sine = jnp.concatenate([cosine, cosine], 1), jnp.concatenate([-sine, sine], 1)
    across = swap(hidden, "zl")
    across, gate_weight, up_weight = together(across, gate_weight, up_weight)
    tokens = (hidden, swap(hidden, "core"), across, swap(across, "core"))
    line = [attention_gain, feedforward_gain, jnp.pad(query_gain, (0, 96)), jnp.pad(key_gain, (0, 96))]
    small = (headgate_weight.T, jnp.concatenate(line)[None])
    mine, got, far, near = take_columns(coords, (query_weight, key_weight, value_weight), (512, 256, 256), small)
    far, near = swap_far(far), swap(near, "zl")
    mine_gu, got_gu, far_gu, last_gu, near_gu = take_columns(
        coords, (gate_weight, up_weight), (768, 768), (), (cosine,)
    )
    far, far_gu = together(far, far_gu)
    far_gu = swap_far(far_gu)
    near, cotangent, near_gu = together(near, cotangent, near_gu)
    grads = list(group_gather(cotangent))
    near_gu = swap(near_gu, "zl")
    weight_qkv = (mine, got, far, near)

    bias = jnp.pad(headgate_bias, (0, 124))[None]

    (keep, send, attn_in, raw, qk, val, probs, attended, gates, mixed, hw, gains, cosine, sine) = attention_forward(
        coords, tokens, weight_qkv, output_weight, cosine, sine, segment_ids.reshape(4, 128), bias
    )
    far_gu, last_gu = together(far_gu, last_gu)
    weight_gu = (mine_gu, got_gu, far_gu, swap_far(last_gu), near_gu)
    far_gu, near_gu, grads[2], send = together(far_gu, near_gu, grads[2], send)
    total, low = chip_sum(coords, keep, send)
    got = swap(low, "zl")
    resid, ffn_in = residual(coords, total, got, tokens[0], tokens[2], gains, weight_gu[3:4])
    keep, send, ffn, grads_all, grad_gu, act, wd_low = feed_forward(
        coords, (ffn_in, swap(ffn_in, "core")), weight_gu, down_weight, grads
    )
    total, low = chip_sum(coords, keep, send)
    low, grad_gu = together(low, grad_gu)
    pieces, part = spread(coords, ffn, [grad_gu], [swap(grad_gu, "core")], act, grads_all)
    got = swap(low, "zl")
    first = exchange(pieces, 0, 0)
    grad_resid, resid_low, grad_gain_second = turn_back(
        coords, total, got, grads[0], grads[2], resid, gains, (pieces[0],)
    )
    saved = (qk, val, probs, attended, gates, raw, gains, cosine, sine)
    front, resid_low, *others = back_first(coords, (resid_low, swap(resid_low, "core")), output_weight, saved)
    first = merge(coords, half_sum_kernel, first, (4,) * 4, (front,), 1)
    keep, send, back, small = back_second(
        coords,
        resid_low,
        output_weight,
        saved,
        (front, *others),
        (attn_in, hw, *weight_qkv, *tokens, grad_gain_second),
        first[:1],
    )
    first = exchange(first, 0, 1)
    pieces, part_second = spread(
        coords,
        attn_in,
        [front, back],
        [swap(front, "core"), swap(back, "core")],
        mixed,
        resid_low,
        (small, swap(small, "core")),
        first[2:],
    )
    second = exchange(pieces, 0, 0)
    first = exchange(merge(coords, turn_sum_kernel, first, (2,) * 4, pieces[:1], 1), 1, 0)
    sums = group_scatter(coords, down(coords, act, wd_low, first[:1]), (keep, send), ())
    first = exchange(merge(coords, half_sum_kernel, first, (1,) * 4, sums[:1], 1), 1, 1)
    second = exchange(merge(coords, half_sum_kernel, second, (4,) * 4, first[:1]), 0, 1)
    height = 2 * pieces[0].shape[1]
    first = send_across(*last_sum(coords, first, part, (second[0], sums[2])))
    second = direct(
        small_kernel_call(coords, quarter_sum_kernel, second, [(height, LANES)] * 4, first[2:3])
    )
    first = cross_sum(coords, first, second[:1])
    first = exchange(first * 2, 1, 1)
    shapes = [(part_second, LANES), (height - part_second, LANES)]
    second = send_across(*small_kernel_call(coords, direct_sum_kernel, second, shapes, first[:1]))
    first = merge(coords, join_kernel, first, (2, 2), second[2:3])
    first = exchange(first * 2, 1, 0)
    (second,) = small_kernel_call(coords, plain_sum_kernel, second, [(height, LANES)], first[:1])
    first = merge(coords, pack_kernel, first, (4, 4), (second,))
    first = exchange(first * 2, 0, 1)
    second = direct([second] * 4)
    first = merge(coords, join_kernel, first, (8, 8), second[:1])
    second = small_kernel_call(
        coords, direct_pack_kernel, second, [(4, height // 2, LANES)] * 2, first[:1]
    )
    first = exchange(first * 2, 0, 0)
    second = merge(coords, join_kernel, exchange(second * 2, 0, 1), (8, 8), ())
    output, input_grad, finished = finish(coords, [*sums, resid, grad_resid, hidden, gains], second[:1])
    grad_g, grad_u, grad_d, settled = settle(coords, first, (768, 768), 768, False, (finished,))
    second = exchange(second * 2, 0, 0)
    (grad_q, grad_k, grad_v, grad_o, small_first, small_second, small_q, small_k, small_bias, grad_hw) = settle(
        coords, second, (512, 256, 256), 512, True, (settled,)
    )
    return (
        output,
        input_grad,
        small_first.reshape(256),
        grad_q,
        grad_k,
        grad_v,
        small_q.reshape(32),
        small_k.reshape(32),
        grad_hw.T,
        small_bias.reshape(4),
        grad_o,
        small_second.reshape(256),
        grad_g,
        grad_u,
        grad_d,
    )


def solution(mesh):
    grid = Mesh(mesh.devices.reshape(2, 4, 4, 2, 2), AXES)
    tokens, split, copies = P(AXES, None), P(GROUP, None), P(("zh", "y", "x"))
    line = P(GROUP)
    weights = (line, split, split, split, line, line, split, line, split, line, split, split, split)
    return jax.shard_map(
        body,
        mesh=grid,
        in_specs=(tokens, tokens, copies, copies, *weights),
        out_specs=(tokens, tokens, *weights),
        check_vma=False,
    )
```

```python
import functools
import math

import jax
import jax.numpy as jnp
from jax import lax
from jax.experimental import pallas as pl
from jax.experimental.pallas import tpu as pltpu
from jax.sharding import Mesh
from jax.sharding import PartitionSpec as P

EPS = 1e-06
THETA = 1000000.0
MASKED = -1e30
HEAD = 128
SCALE = 1.0 / math.sqrt(HEAD)
LOW = jnp.bfloat16
FULL = jnp.float32
AXES = ("zh", "y", "x", "zl", "core")
GROUP = ("zl", "core")
LANES = 128


def swap(value, axis):
    return lax.ppermute(value, axis, [(0, 1), (1, 0)])


def turn(value, step):
    return lax.ppermute(value, ("zh", "zl"), [(i, (i + step) % 4) for i in range(4)])


def swap_far(value):
    return lax.ppermute(value, ("zh", "zl"), [(0, 3), (3, 0), (1, 2), (2, 1)])


def swap_plane(value, axis, mask):
    pairs = []
    for y in range(4):
        for x in range(4):
            for core in range(2):
                to_y, to_x = (y, x ^ mask) if axis == core else (y ^ mask, x)
                pairs.append(((y * 4 + x) * 2 + core, (to_y * 4 + to_x) * 2 + core))
    return lax.ppermute(value, ("y", "x", "core"), pairs)


def dot(left, right):
    return jnp.dot(left, right, preferred_element_type=FULL)


def dot_t(left, right):
    return lax.dot_general(left, right, (((1,), (1,)), ((), ())), preferred_element_type=FULL)


def dot_tn(left, right):
    return lax.dot_general(left, right, (((0,), (0,)), ((), ())), preferred_element_type=FULL)


VMEM = pl.BlockSpec(memory_space=pltpu.VMEM)
SMEM = pl.BlockSpec(memory_space=pltpu.SMEM)


def held_bytes(shape, kind):
    shape = (1,) * (2 - len(shape)) + tuple(shape)
    size = math.prod(shape[:-2]) * (-(-shape[-2] // 16) * 16) * (-(-shape[-1] // LANES) * LANES)
    return size * jnp.dtype(kind).itemsize


class Late:
    def __init__(self, source, target, done):
        self.copy, self.target, self.open = pltpu.make_async_copy(source, target, done), target, True
        self.copy.start()

    def ready(self):
        if self.open:
            self.copy.wait()
        self.open = False
        return self.target


class Early:
    def __init__(self, source, target, done):
        self.copy, self.source, self.sent = pltpu.make_async_copy(source, target, done), source, False

    def send(self):
        if not self.sent:
            self.copy.start()
        self.sent = True


def call(kernel, coords, ins, outs, scratch, late=(), early=(), least=0, wait=(), flops=1):
    ins = list(ins)
    n_ins, n_outs, n_scratch = len(ins), len(outs), len(scratch)
    moving = [(ins[i].shape, ins[i].dtype) for i in late] + [outs[i] for i in early]

    def run(coords, *refs):
        refs = list(refs)
        del refs[n_ins : n_ins + len(wait)]
        done = refs.pop() if moving else None
        buffers = refs[n_ins + n_outs + n_scratch :]
        refs = refs[: n_ins + n_outs + n_scratch]
        for k, i in enumerate(late):
            refs[i] = Late(refs[i], buffers[k], done.at[k])
        sending = []
        for k, i in enumerate(early):
            k += len(late)
            sending.append(Early(buffers[k], refs[n_ins + i], done.at[k]))
            refs[n_ins + i] = sending[-1]
        kernel(coords, *refs)
        for i in late:
            refs[i].ready()
        for out in sending:
            out.send()
        for out in sending:
            out.copy.wait()

    need = sum(held_bytes(a.shape, a.dtype) for a in ins) + sum(held_bytes(*o) for o in [*outs, *scratch])
    anywhere = pl.BlockSpec(memory_space=pltpu.HBM)
    buffers = [pltpu.VMEM(shape, kind) for shape, kind in [*scratch, *moving]]
    return pl.pallas_call(
        run,
        out_shape=[jax.ShapeDtypeStruct(shape, kind) for shape, kind in outs],
        in_specs=[SMEM] + [anywhere if i in late else VMEM for i in range(n_ins)] + [pl.BlockSpec(memory_space=pl.ANY)] * len(wait),
        out_specs=[anywhere if i in early else VMEM for i in range(n_outs)],
        scratch_shapes=buffers + ([pltpu.SemaphoreType.DMA((len(moving),))] if moving else []),
        compiler_params=pltpu.CompilerParams(vmem_limit_bytes=max(need + 8 * 2**20, least * 2**20)),
        cost_estimate=pl.CostEstimate(flops=flops, bytes_accessed=1, transcendentals=0),
    )(coords, *ins, *wait)


def lanes(index, width):
    return pl.ds(pl.multiple_of(index * width, LANES), width)


def rows(index, height):
    return pl.ds(pl.multiple_of(index * height, 16), height)


def inverse_rms(value):
    return lax.rsqrt(jnp.mean(value * value, -1, keepdims=True) + EPS)


def norm_back(grad, normal, inverse):
    return inverse * (grad - normal * jnp.mean(grad * normal, -1, keepdims=True))


def cut_kernel(widths, small, coords, *refs):
    ins, outs = refs[: len(widths)], refs[len(widths) + 2 * small :]
    j = coords[2]
    if small:
        heads, line = refs[len(widths) : len(widths) + 2]
        line = jnp.concatenate([line[...], jnp.zeros((15, 768), FULL)], 0)
        tile = jnp.concatenate([heads[...], line], 1).astype(LOW)
    third = [(3, 0, 256)] if small else [(3, 0, 128), (3, 128, 128)]
    for out, (r, first, count) in zip(outs, [(1, 0, 256), *third, (2, 0, 256), (0, 0, 256)]):
        at = 0
        for w, n in zip(ins, widths):
            out[0:count, at : at + n] = w[first : first + count, lanes(j ^ r, n)].astype(LOW)
            at += n
        if small:
            out[256:272, :] = tile


def take_columns(coords, weights, widths, small=(), wait=()):
    heights = (272,) * 4 if small else (256, 128, 128, 256, 256)
    beside, *across, other, mine = call(
        functools.partial(cut_kernel, widths, bool(small)),
        coords,
        [*weights, *small],
        [((n, sum(widths)), LOW) for n in heights],
        [],
        least=50,
        wait=wait,
    )
    return mine, swap(beside, "core"), other, *[swap(piece, "core") for piece in across]


def first_kernel(coords, t0, t1, t2, t3, w0, w1, w2, w3, wo, cos, sin, segs, bias, *refs):
    (keep, send, attn_in, raw, qk, val, probs, attended, gates, mixed, hw, gains, cos_rel, sin_rel) = refs[:14]
    (wo_low, mask) = refs[14:]
    (attn_out, raw_out, qk_out, val_out, probs_out, att_out, gates_out, mixed_out) = refs[2:10]
    attn_in, raw, qk, val, probs, attended, gates, mixed = [r.source for r in refs[2:10]]
    cos_out, sin_out = refs[12:14]
    cos_rel, sin_rel = cos_out.source, sin_out.source
    j = coords[2]
    tokens, weights = (t0, t1, t2, t3), (w0, w1, w2, w3)
    hw[...] = jnp.zeros_like(hw)
    gains[...] = jnp.zeros_like(gains)
    gain_q, gain_k = jnp.zeros((16, LANES), FULL), jnp.zeros((16, LANES), FULL)
    for r in range(4):
        small = weights[r][256:272, :]
        hw[0:16, lanes(j ^ r, 256)] = small[:, 0:256]
        small = small[:, 256:].astype(FULL)
        gains[0:1, lanes(j ^ r, 256)] = small[0:1, 0:256]
        gains[1:2, lanes(j ^ r, 256)] = small[0:1, 256:512]
        gain_q += pltpu.roll(small[:, 512:640], (j ^ r) * 32, 1)
        gain_k += pltpu.roll(small[:, 640:768], (j ^ r) * 32, 1)
        cos_rel[r * 128 : r * 128 + 128, :] = cos.ready()[rows(j ^ r, 128), :]
        sin_rel[r * 128 : r * 128 + 128, :] = sin.ready()[rows(j ^ r, 128), :]
    gains[2:3, 0:128] = gain_q[0:1]
    gains[2:3, 128:256] = gain_k[0:1]
    for r in range(4):
        x = tokens[r][0:128, :].astype(FULL)
        attn_in[r * 128 : r * 128 + 128, :] = (x * inverse_rms(x) * gains[0:1, :]).astype(LOW)

    attn_out.send()
    cos_out.send()
    sin_out.send()

    logit = dot_t(attn_in[...], hw[...])
    logit = pltpu.roll(logit, (32 - j) * 4 & 127, 1) + bias[...].astype(LOW).astype(FULL)
    gates[...] = jax.nn.sigmoid(logit)
    gates_out.send()
    for n in range(4):
        total = dot(attn_in[:, lanes(j, 256)], w0[0:256, n * 256 : n * 256 + 256])
        for r in range(1, 4):
            total += dot(attn_in[:, lanes(j ^ r, 256)], weights[r][0:256, n * 256 : n * 256 + 256])
        if n < 3:
            raw[:, n * 256 : n * 256 + 256] = total
        else:
            val[...] = total.astype(LOW)
    raw_out.send()
    val_out.send()
    for h in range(6):
        at = slice(h * 128, h * 128 + 128)
        part = raw[:, at]
        gain = gains[2:3, 0:128] if h < 4 else gains[2:3, 128:256]
        part = part * inverse_rms(part) * gain
        qk[:, at] = (part * cos_rel[...] + pltpu.roll(part, 64, 1) * sin_rel[...]).astype(LOW)

    qk_out.send()
    lane = lax.broadcasted_iota(jnp.int32, (128, 128), 1)
    line = lax.broadcasted_iota(jnp.int32, (128, 128), 0)
    for c in range(4):
        seg_q = jnp.broadcast_to(segs[pl.ds(j ^ c, 1), :], (128, 128)).T
        for b in range(4):
            seg_k = segs[pl.ds(j ^ b, 1), :]
            earlier = lane + (j ^ b) * 128 <= line + (j ^ c) * 128
            mask[c * 128 : c * 128 + 128, b * 128 : b * 128 + 128] = jnp.where(
                earlier & (seg_q == seg_k), 0.0, MASKED
            )
    for h in range(4):
        kv = h // 2
        for c in range(2):
            at = slice(c * 256, c * 256 + 256)
            scores = dot_t(qk[at, h * 128 : h * 128 + 128], qk[:, 512 + kv * 128 : 640 + kv * 128])
            scores = scores * SCALE + mask[at, :]
            expo = jnp.exp(scores - jnp.max(scores, -1, keepdims=True))
            part = (expo * (1.0 / jnp.sum(expo, -1, keepdims=True))).astype(LOW)
            probs[h, at, :] = part
            result = dot(part, val[:, kv * 128 : kv * 128 + 128])
            attended[at, h * 128 : h * 128 + 128] = result
            mixed[at, h * 128 : h * 128 + 128] = (result * gates[at, h : h + 1]).astype(LOW)
    probs_out.send()
    att_out.send()
    mixed_out.send()
    wo_low[...] = wo.ready()[...].astype(LOW)
    for n in range(4):
        at = slice(n * 256, n * 256 + 256)
        result = dot(mixed[...], wo_low[:, at])
        for c in range(2):
            keep[c, :, at] = result[c * 256 : c * 256 + 128]
            send[c, :, at] = result[c * 256 + 128 : c * 256 + 256].astype(LOW)


def attention_forward(coords, tokens, weights, wo, cos, sin, segs, bias):
    outs = [
        ((2, 128, 1024), FULL),
        ((2, 128, 1024), LOW),
        ((512, 1024), LOW),
        ((512, 768), FULL),
        ((512, 768), LOW),
        ((512, 256), LOW),
        ((4, 512, 512), LOW),
        ((512, 512), FULL),
        ((512, 128), FULL),
        ((512, 512), LOW),
        ((128, 1024), LOW),
        ((8, 1024), FULL),
        ((512, 128), FULL),
        ((512, 128), FULL),
    ]
    return call(
        first_kernel,
        coords,
        [*tokens, *weights, wo, cos, sin, segs, bias],
        outs,
        [((512, 1024), LOW), ((512, 512), FULL)],
        (9, 10, 8),
        (2, 3, 4, 5, 6, 7, 8, 9, 12, 13),
    )


def ffn_kernel(coords, f_own, f_got, w0, w1, w2, w3_low, w3_high, wd, g0, g1, g2, g3, *refs):
    (keep, send, ffn, grads, grad_gu, act, wd_low, w3) = refs
    j = coords[2]
    weights = (w0, w1, w2, w3)
    w3[0:128, :] = w3_low[...]
    w3[128:256, :] = w3_high[...]
    for r, g in enumerate((g0, g1, g2, g3)):
        ffn[r * 128 : r * 128 + 128, :] = (f_got if r % 2 else f_own)[r // 2]
        grads[r * 128 : r * 128 + 128, :] = g[...]
    wd_low[...] = wd[...].astype(LOW)
    for m in range(2):
        at = slice(m * 256, m * 256 + 256)
        for n in range(3):
            low, high = slice(n * 256, n * 256 + 256), slice(768 + n * 256, 1024 + n * 256)
            gate = dot(ffn[at, lanes(j, 256)], w0[:, low])
            up = dot(ffn[at, lanes(j, 256)], w0[:, high])
            for r in range(1, 4):
                gate += dot(ffn[at, lanes(j ^ r, 256)], weights[r][:, low])
                up += dot(ffn[at, lanes(j ^ r, 256)], weights[r][:, high])
            back = dot_t(grads[at, :], wd_low[low, :])
            sigma = jax.nn.sigmoid(gate)
            swish = gate * sigma
            act[at, low] = (swish * up).astype(LOW)
            grad_gu[at, low] = (back * up * sigma * (1.0 + gate * (1.0 - sigma))).astype(LOW)
            grad_gu[at, high] = (back * swish).astype(LOW)
    for r in range(4):
        part = dot_t(grad_gu[...], weights[r][...])
        for t in range(2):
            keep[t, :, lanes(j ^ r, 256)] = part[t * 256 : t * 256 + 128]
            send[t, :, lanes(j ^ r, 256)] = part[t * 256 + 128 : t * 256 + 256].astype(LOW)


def feed_forward(coords, ffn_in, weights, wd, grads):
    outs = [
        ((2, 128, 1024), FULL),
        ((2, 128, 1024), LOW),
        ((512, 1024), LOW),
        ((512, 1024), LOW),
        ((512, 1536), LOW),
        ((512, 768), LOW),
        ((768, 1024), LOW),
    ]
    return call(
        ffn_kernel,
        coords,
        [*ffn_in, *weights, wd, *grads],
        outs,
        [((256, 1536), LOW)],
    )


def down_kernel(coords, act, wd_low, keep, send):
    for c in range(4):
        result = dot(act[c * 128 : c * 128 + 128, :], wd_low[...])
        if c % 2:
            send[c // 2] = result.astype(LOW)
        else:
            keep[c // 2] = result


def down(coords, act, wd_low, wait):
    outs = [((2, 128, 1024), FULL), ((2, 128, 1024), LOW)]
    return call(down_kernel, coords, [act, wd_low], outs, [], wait=wait)


def heads_back(kv, refs, resid_low, wo_low, grad_scores, out):
    (qk, val, probs, attended, gates, raw, gains, cos, sin) = refs
    lane = lax.broadcasted_iota(jnp.int32, (512, LANES), 1)
    grad_logit = jnp.zeros((512, LANES), FULL)
    gain_sums = []

    def head_back(grad, at, gain, to):
        part = raw[:, at]
        inverse = inverse_rms(part)
        normal = part * inverse
        turned = grad * cos[...] - pltpu.roll(grad, 64, 1) * sin[...]
        gain_sums.append(jnp.sum(turned * normal, 0, keepdims=True))
        out[:, to : to + 128] = norm_back(turned * gain, normal, inverse).astype(LOW)

    key_at = slice(512 + kv * 128, 640 + kv * 128)
    grad_key = grad_value = None
    for n, h in enumerate((2 * kv, 2 * kv + 1)):
        at = slice(h * 128, h * 128 + 128)
        grad_mixed = dot_t(resid_low[...], wo_low[n * 128 : n * 128 + 128, :])
        gate = gates[:, h : h + 1]
        grad_gate = jnp.sum(grad_mixed * attended[:, at], -1, keepdims=True) * gate * (1.0 - gate)
        grad_logit = jnp.where(lane == h, grad_gate, grad_logit)
        grad_att = (grad_mixed * gate).astype(LOW)
        for c in range(2):
            line = slice(c * 256, c * 256 + 256)
            grad_probs = dot_t(grad_att[line], val[:, kv * 128 : kv * 128 + 128])
            part = probs[h, line, :].astype(FULL)
            inner = jnp.sum(part * grad_probs, -1, keepdims=True)
            grad_scores[line, :] = (part * (grad_probs - inner)).astype(LOW)
        head_back(dot(grad_scores[...], qk[:, key_at]) * SCALE, at, gains[2:3, 0:128], n * 128)
        more_key = dot_tn(grad_scores[...], qk[:, at])
        more_value = dot_tn(probs[h], grad_att)
        grad_key = more_key if grad_key is None else grad_key + more_key
        grad_value = more_value if grad_value is None else grad_value + more_value
    head_back(grad_key * SCALE, key_at, gains[2:3, 128:256], 256)
    out[:, 384:512] = grad_value.astype(LOW)
    return grad_logit, gain_sums


def back_first_kernel(coords, l_own, l_got, wo, qk, val, probs, attended, gates, raw, gains, cos, sin, *refs):
    (out, resid_low, logit, sums, wo_low, grad_scores) = refs
    wo_low[...] = wo.ready()[0:256, :].astype(LOW)
    for r in range(4):
        resid_low[r * 128 : r * 128 + 128, :] = (l_got if r % 2 else l_own)[r // 2]
    refs = [r.ready() for r in (qk, val, probs, attended, gates, raw, gains, cos, sin)]
    grad_logit, gain_sums = heads_back(0, refs, resid_low, wo_low, grad_scores, out)
    logit[...] = grad_logit
    sums[...] = jnp.zeros_like(sums)
    for i, value in enumerate(gain_sums):
        sums[i : i + 1, :] = value


def back_kernel(coords, *refs):
    (resid_low, wo, qk, val, probs, attended, gates, raw, gains, cos, sin, out_first, logit, sums) = refs[:14]
    (attn_in, hw, w0, w1, w2, w3, t0, t1, t2, t3, gain_second) = refs[14:25]
    (keep, send, out, small) = refs[25:29]
    (wo_low, grad_scores, grad_qkv) = refs[29:]
    j = coords[2]
    wo_low[...] = wo.ready()[256:512, :].astype(LOW)
    refs = [r.ready() for r in (qk, val, probs, attended, gates, raw, gains, cos, sin)]
    grad_logit, gain_sums = heads_back(1, refs, resid_low, wo_low, grad_scores, out)
    for kv, part in enumerate((out_first, out)):
        grad_qkv[:, kv * 256 : kv * 256 + 256] = part[:, 0:256]
        grad_qkv[:, 512 + kv * 128 : 640 + kv * 128] = part[:, 256:384]
        grad_qkv[:, 768 + kv * 128 : 896 + kv * 128] = part[:, 384:512]

    weights, tokens = [[r.ready() for r in group] for group in ((w0, w1, w2, w3), (t0, t1, t2, t3))]
    attn_in, hw = attn_in.ready(), hw.ready()
    grad_logit = (grad_logit + logit[...]).astype(LOW)
    grad_bias = jnp.sum(grad_logit.astype(FULL), 0, keepdims=True)
    grad_hw = dot_tn(grad_logit, attn_in[...])
    spread_logit = pltpu.roll(grad_logit.astype(FULL), j * 4, 1).astype(LOW)
    inverses = []
    for r in range(4):
        x = tokens[r][0:128, :].astype(FULL)
        inverses.append(inverse_rms(x))
    small[...] = jnp.zeros_like(small)

    def put(row, value):
        small[row // 4, row % 4 : row % 4 + 1, :] = value

    for r in range(4):
        at = lanes(j ^ r, 256)
        part = dot_t(grad_qkv[...], weights[r][0:256, :]) + dot(spread_logit, hw[:, at])
        total = jnp.zeros((1, 256), FULL)
        for t in range(4):
            piece = part[t * 128 : t * 128 + 128]
            normal = tokens[t][0:128, at].astype(FULL) * inverses[t]
            total += jnp.sum(piece * normal, 0, keepdims=True)
            if t % 2:
                send[t // 2, :, at] = piece.astype(LOW)
            else:
                keep[t // 2, :, at] = piece
        block = (j ^ r) // 2
        for i in range(2):
            small[block, pl.ds((j ^ r) % 2 * 2 + i, 1), :] = total[:, i * 128 : i * 128 + 128]
    for i in range(8):
        put(8 + i, gain_second[0:1, i * 128 : i * 128 + 128])
    put(16, gain_sums[0] + gain_sums[1] + sums[0:1, :] + sums[1:2, :])
    put(17, gain_sums[2] + sums[2:3, :])
    put(18, grad_bias)
    for h in range(4):
        for i in range(8):
            put(24 + h * 8 + i, grad_hw[h : h + 1, i * 128 : i * 128 + 128])


def back_first(coords, resid_low, wo, saved):
    outs = [((512, 512), LOW), ((512, 1024), LOW), ((512, 128), FULL), ((8, 128), FULL)]
    scratch = [((256, 1024), LOW), ((512, 512), LOW)]
    return call(back_first_kernel, coords, [*resid_low, wo, *saved], outs, scratch, range(2, 12), flops=3*10**9)


def back_second(coords, resid_low, wo, saved, first, others, wait):
    outs = [((2, 128, 1024), FULL), ((2, 128, 1024), LOW), ((512, 512), LOW), ((16, 8, 128), FULL)]
    scratch = [((256, 1024), LOW), ((512, 512), LOW), ((512, 1024), LOW)]
    ins = [resid_low, wo, *saved, *first, *others]
    late = [*range(1, 11), *range(14, 24)]
    return call(back_kernel, coords, ins, outs, scratch, late, wait=wait)


KEPT, SENT, MASKS = ((0, 3), (0, 1)), ((1, 2), (3, 2)), ((1, 3), (3, 1))


def spread_kernel(n_right, with_small, coords, left_c, *refs):
    rights, (left_r, right_r, *refs) = refs[: 2 * n_right], refs[2 * n_right :]
    if with_small:
        small_own, small_got, *refs = refs
    outs, (turned_c, turned_r, held_c, held_r) = refs[:4], refs[4:]
    first, second, j = coords[0], coords[1], coords[2]
    wide = rights[0].shape[1] // LANES
    panels = wide * n_right
    rows_r = left_r.shape[1] // 16
    part = 2 * panels * 16 + (16 if with_small else 0)
    edge = outs[0].shape[1]
    blocks = [(m, n, (first ^ m) * 4 + (second ^ n)) for m in (1, 2, 3, 0) for n in range(4)]

    def put(m, n, low, value):
        stream = 0 if low < edge else 1
        sent = m in SENT[stream]
        at = (SENT if sent else KEPT)[stream].index(m) * 4 + n
        low -= edge * stream
        outs[2 * sent + stream][at, low : low + value.shape[0], :] = value

    for d in range(2):
        turned = left_c[:, lanes(j ^ (2 * d), 256)].T
        turned_c[d] = turned
        for t in range(4):
            turned_c[2 + d, :, t * 128 : t * 128 + 128] = turned[:, (t ^ 1) * 128 : (t ^ 1) * 128 + 128]
    turned_r[...] = left_r[...].T
    for k, right in enumerate(rights):
        src, start = k // n_right, k % n_right * wide
        for d in range(2):
            held_c[...] = dot(turned_c[2 * src + d], right[...]).astype(LOW)
            for m, n, block in blocks:
                for p in range(wide):
                    low = (1 - d) * part + (src * panels + start + p) * 16
                    put(m, n, low, held_c[rows(block, 16), p * LANES : (p + 1) * LANES])
    held_r[...] = dot(turned_r[...], right_r[...]).astype(LOW)
    for m, n, block in blocks:
        if with_small:
            tile = jnp.concatenate([small_own[block], small_got[block]], 0).astype(LOW)
            put(m, n, part - 16, tile)
            put(m, n, 2 * part - 16, tile)
        for p in range(8):
            put(m, n, 2 * part + p * rows_r, held_r[rows(block, rows_r), p * LANES : (p + 1) * LANES])


def spread(coords, left_c, own, got, left_r, right_r, small=(), wait=()):
    wide = own[0].shape[1]
    panels = wide * len(own) // LANES
    part = 2 * panels * 16 + (16 if small else 0)
    height = 2 * part + left_r.shape[1] // 2
    scratch = [
        ((4, 256, 512), LOW),
        ((left_r.shape[1], 512), LOW),
        ((256, wide), LOW),
        ((left_r.shape[1], 1024), LOW),
    ]
    pieces = call(
        functools.partial(spread_kernel, len(own), bool(small)),
        coords,
        [left_c, *own, *got, left_r, right_r, *small],
        [((8, height // 2, LANES), LOW)] * 4,
        scratch,
        wait=wait,
    )
    return pieces, part


def plus(a, b):
    return (a.astype(FULL) + b.astype(FULL)).astype(LOW)


def half_sum_kernel(coords, p, q, got_p, got_q, *outs):
    half = p.shape[0] // 2
    for kept, sent, mine, got in ((outs[0], outs[2], p, got_p), (outs[1], outs[3], q, got_q)):
        kept[...] = plus(mine[0:half], got[0:half])
        sent[...] = plus(mine[half:], got[half:])


def turn_sum_kernel(coords, p, q, got_p, got_q, *outs):
    for s, (mine, got) in enumerate(((p, got_p), (q, got_q))):
        for at in range(2):
            outs[s][at] = plus(mine[KEPT[s][at]], got[KEPT[s][at]])
            outs[2 + s][at] = plus(mine[SENT[s][at]], got[SENT[s][at]])


def last_sum_kernel(coords, p, q, got_p, got_q, other, mine):
    part, edge = other.shape[0], p.shape[1]
    p, q = plus(p[0], got_p[0]), plus(q[0], got_q[0])
    other[...] = p[:part]
    mine[0 : edge - part, :] = p[part:]
    mine[edge - part :, :] = q


def cross_sum_kernel(coords, ahead, behind, mine, far, p, q):
    part, edge = ahead.shape[0], p.shape[1]
    p[0, 0:part, :] = plus(ahead[...], behind[...])
    mine = plus(mine[...], far[...])
    p[0, part:, :] = mine[: edge - part]
    q[0] = mine[edge - part :]


def quarter_sum_kernel(coords, p, q, got_p, got_q, *outs):
    edge = p.shape[1]
    for n in range(4):
        outs[n][0:edge, :] = plus(p[n], got_p[n])
        outs[n][edge:, :] = plus(q[n], got_q[n])


def direct_sum_kernel(coords, a, b, c, d, other, mine):
    total = (a[...].astype(FULL) + b[...].astype(FULL) + c[...].astype(FULL) + d[...].astype(FULL)).astype(LOW)
    part = other.shape[0]
    other[...] = total[:part]
    mine[...] = total[part:]


def plain_sum_kernel(coords, ahead, behind, mine, far, out):
    part = ahead.shape[0]
    out[0:part, :] = plus(ahead[...], behind[...])
    out[part:, :] = plus(mine[...], far[...])


def direct_pack_kernel(coords, a, b, c, d, p, q):
    edge = p.shape[1]
    for n, ref in enumerate((a, b, c, d)):
        p[n] = ref[0:edge, :]
        q[n] = ref[edge:, :]


def direct(parts):
    return [parts[0]] + [swap_plane(parts[m], 1, m) for m in (1, 2, 3)]


def small_kernel_call(coords, kernel, got, shapes, wait, flops=4 * 10**9):
    return call(kernel, coords, got, [(shape, LOW) for shape in shapes], [], wait=wait, flops=flops)


def join_kernel(coords, p, q, got_p, got_q, both_p, both_q):
    half = p.shape[0]
    for both, mine, got in ((both_p, p, got_p), (both_q, q, got_q)):
        both[0:half] = mine[...]
        both[half:] = got[...]


def pack_kernel(coords, p, q, got_p, got_q, all_p, all_q):
    for s, (whole, mine, got) in enumerate(((all_p, p, got_p), (all_q, q, got_q))):
        for at in range(2):
            whole[KEPT[s][at]] = mine[at]
            whole[SENT[s][at]] = got[at]


def exchange(pieces, axis, step):
    return [*pieces[:2], *[swap_plane(pieces[2 + s], axis, MASKS[s][step]) for s in range(2)]]


def merge(coords, kernel, got, counts, wait, flops=4 * 10**9):
    outs = [((n, *got[0].shape[1:]), LOW) for n in counts]
    return call(kernel, coords, got, outs, [], wait=wait, flops=flops)


def send_across(other, mine):
    return [turn(other, 1), turn(other, -1), mine, turn(mine, 2)]


def last_sum(coords, got, part, wait, flops=1):
    outs = [((part, LANES), LOW), ((2 * got[0].shape[1] - part, LANES), LOW)]
    return call(last_sum_kernel, coords, got, outs, [], wait=wait, flops=flops)


def cross_sum(coords, got, wait):
    edge = (got[0].shape[0] + got[2].shape[0]) // 2
    return call(cross_sum_kernel, coords, got, [((1, edge, LANES), LOW)] * 2, [], wait=wait, flops=4 * 10**9)


def together(*values):
    return lax.optimization_barrier(values)


def settle_kernel(widths, with_small, coords, *refs):
    ins, outs = refs[:4], refs[4:]
    first, second, j = coords[0], coords[1], coords[2]
    panels = sum(widths) // LANES
    out_r = outs[len(widths)]
    rows_r = out_r.shape[0] // 16
    spots = []
    for kv in range(2 if with_small else 1):
        for w, width in enumerate(widths):
            count = width // LANES // (2 if with_small else 1)
            spots += [(w, (kv * count + i) * LANES) for i in range(count)]
    if with_small:
        total, heads = refs[-2:]
        total[...] = jnp.zeros_like(total)

    part = 2 * panels * 16 + (16 if with_small else 0)
    edge = ins[0].shape[1]

    def take(m, n, low, height):
        stream = 0 if low < edge else 1
        came = m in SENT[stream]
        at = (SENT if came else KEPT)[stream].index(m) * 4 + n
        low -= edge * stream
        return ins[2 * came + stream][at, low : low + height, :].astype(FULL)

    for m in range(4):
        for n in range(4):
            block = (first ^ m) * 4 + (second ^ n)
            line = rows(block, 16)
            for r in range(4):
                base = (1 - r // 2) * part + (r % 2) * panels * 16
                for p, (w, col) in enumerate(spots):
                    lane = pl.ds(pl.multiple_of((j ^ r) * widths[w] + col, LANES), LANES)
                    low = base + p * 16
                    outs[w][line, lane] = take(m, n, low, 16)
            for p in range(8):
                low = 2 * part + p * rows_r
                lane = slice(p * LANES, (p + 1) * LANES)
                out_r[rows(block, rows_r), lane] = take(m, n, low, rows_r)
            if with_small:
                for z in range(2):
                    tile = take(m, n, (1 - z) * part + part - 16, 16)
                    for src in range(2):
                        value = tile[src * 8 : src * 8 + 8]
                        heads[j ^ (2 * z + src), block] = value
                        total[block] += value
    if not with_small:
        outs[-1][...] = jnp.zeros((8, LANES), FULL)
    if with_small:
        gain_first, gain_second, gain_q, gain_k, bias, hw = outs[len(widths) + 1 : len(widths) + 7]
        for i in range(2):
            at = slice(i * 128, i * 128 + 128)
            gain_first[:, at] = total[j // 2, pl.ds(j % 2 * 2 + i, 1), :]
            gain_second[:, at] = total[2 + j // 2, pl.ds(j % 2 * 2 + i, 1), :]
        shift = (4 - j) * 32 & 127
        turned = pltpu.roll(total[4], shift, 1)
        gain_q[...] = turned[0:1, :32]
        gain_k[...] = turned[1:2, :32]
        bias[...] = heads[j, 4][2:3, :4]
        lines = []
        for q in range(4):
            for h in range(4):
                start = 24 + h * 8
                lines.append(
                    jnp.concatenate(
                        [heads[q, start // 4 + j // 2, pl.ds(j % 2 * 2 + i, 1), :] for i in range(2)], 1
                    )
                )
        whole = jnp.concatenate(lines, 0)
        hw[...] = whole


def settle(coords, pieces, widths, rows_r, with_small, wait):
    outs = [((256, 4 * w), FULL) for w in widths] + [((rows_r, 1024), FULL)]
    scratch = []
    if with_small:
        outs += [((1, n), FULL) for n in (256, 256, 32, 32, 4)] + [((16, 256), FULL)]
        scratch = [((16, 8, 128), FULL), ((4, 16, 8, 128), FULL)]
    else:
        outs += [((8, LANES), FULL)]
    return call(functools.partial(settle_kernel, widths, with_small), coords, pieces, outs, scratch, wait=wait)


def group_gather(part):
    beside = swap(part, "core")
    across = swap(part, "zl")
    return part, beside, across, swap(across, "core")


def add_kernel(coords, keep, got, total, low):
    value = keep[...] + got[...].astype(FULL)
    total[...] = value
    low[...] = value.astype(LOW)


def chip_sum(coords, keep, send, wait=()):
    outs = [((2, 128, 1024), FULL), ((2, 128, 1024), LOW)]
    return call(add_kernel, coords, [keep, swap(send, "core")], outs, [], wait=wait)


def own_kernel(coords, keep, got, more_keep, more_got, *outs):
    (mine, more, low) = outs
    for s, (kept, came, own) in enumerate(((keep, got, mine), (more_keep, more_got, more))):
        own[...] = kept[0] + came[0].astype(FULL)
        low[s] = (kept[1] + came[1].astype(FULL)).astype(LOW)


def group_scatter(coords, first, second, wait):
    ins = [first[0], swap(first[1], "core"), second[0], swap(second[1], "core")]
    outs = [((128, 1024), FULL)] * 2 + [((2, 128, 1024), LOW)]
    mine, more, low = call(own_kernel, coords, ins, outs, [], wait=wait)
    return mine, more, swap(low, "zl")


def end_kernel(coords, mine, more, got, resid, grad_resid, hidden, gains, output, input_grad, flag):
    flag[...] = jnp.zeros((8, LANES), FULL)
    output[...] = (resid[0] + (mine[...] + got[0].astype(FULL))).astype(LOW)
    x = hidden[...].astype(FULL)
    inverse = inverse_rms(x)
    grad = (more[...] + got[1].astype(FULL)) * gains[0:1, :]
    input_grad[...] = (grad_resid[...] + norm_back(grad, x * inverse, inverse)).astype(LOW)


def finish(coords, ins, wait):
    return call(end_kernel, coords, ins, [((128, 1024), LOW)] * 2 + [((8, LANES), FULL)], [], wait=wait)


def resid_kernel(coords, total, got, h0, h2, gains, resid, low):
    for d, hidden in enumerate((h0, h2)):
        value = hidden[...].astype(FULL) + (total[d] + got[1 - d].astype(FULL))
        resid[d] = value
        low[d] = (value * inverse_rms(value) * gains[1:2, :]).astype(LOW)


def residual(coords, total, got, h0, h2, gains, wait):
    outs = [((2, 128, 1024), FULL), ((2, 128, 1024), LOW)]
    return call(resid_kernel, coords, [total, got, h0, h2, gains], outs, [], wait=wait)


def turn_kernel(coords, total, got, g0, g2, resid, gains, grad_resid, low, gain_sum):
    for d, upstream in enumerate((g0, g2)):
        value = resid[d]
        inverse = inverse_rms(value)
        normal = value * inverse
        grad = total[d] + got[1 - d].astype(FULL)
        back = upstream[...].astype(FULL) + norm_back(grad * gains[1:2, :], normal, inverse)
        low[d] = back.astype(LOW)
        if d == 0:
            grad_resid[...] = back
            gain_sum[...] = jnp.sum(grad * normal, 0, keepdims=True)


def turn_back(coords, total, got, g0, g2, resid, gains, wait):
    outs = [((128, 1024), FULL), ((2, 128, 1024), LOW), ((1, 1024), FULL)]
    return call(turn_kernel, coords, [total, got, g0, g2, resid, gains], outs, [], wait=wait)


def body(
    hidden,
    cotangent,
    segment_ids,
    positions,
    attention_gain,
    query_weight,
    key_weight,
    value_weight,
    query_gain,
    key_gain,
    headgate_weight,
    headgate_bias,
    output_weight,
    feedforward_gain,
    gate_weight,
    up_weight,
    down_weight,
):
    core = lax.axis_index("core")
    x_at, y_at = lax.axis_index("x"), lax.axis_index("y")
    j = lax.axis_index("zl") * 2 + core
    coords = jnp.stack([jnp.where(core == 0, x_at, y_at), jnp.where(core == 0, y_at, x_at), j]).astype(jnp.int32)

    freq = jnp.power(jnp.float32(THETA), -jnp.arange(64, dtype=FULL) * 2.0 / HEAD)
    angle = positions.astype(FULL)[:, None] * freq[None, :]
    cosine, sine = jnp.cos(angle), jnp.sin(angle)
    cosine, sine = jnp.concatenate([cosine, cosine], 1), jnp.concatenate([-sine, sine], 1)
    across = swap(hidden, "zl")
    across, gate_weight, up_weight = together(across, gate_weight, up_weight)
    tokens = (hidden, swap(hidden, "core"), across, swap(across, "core"))
    line = [attention_gain, feedforward_gain, jnp.pad(query_gain, (0, 96)), jnp.pad(key_gain, (0, 96))]
    small = (headgate_weight.T, jnp.concatenate(line)[None])
    mine, got, far, near = take_columns(coords, (query_weight, key_weight, value_weight), (512, 256, 256), small)
    far, near = swap_far(far), swap(near, "zl")
    mine_gu, got_gu, far_gu, last_gu, near_gu = take_columns(
        coords, (gate_weight, up_weight), (768, 768), (), (cosine,)
    )
    far, far_gu = together(far, far_gu)
    far_gu = swap_far(far_gu)
    near, cotangent, near_gu = together(near, cotangent, near_gu)
    grads = list(group_gather(cotangent))
    near_gu = swap(near_gu, "zl")
    weight_qkv = (mine, got, far, near)

    bias = jnp.pad(headgate_bias, (0, 124))[None]

    (keep, send, attn_in, raw, qk, val, probs, attended, gates, mixed, hw, gains, cosine, sine) = attention_forward(
        coords, tokens, weight_qkv, output_weight, cosine, sine, segment_ids.reshape(4, 128), bias
    )
    far_gu, last_gu = together(far_gu, last_gu)
    weight_gu = (mine_gu, got_gu, far_gu, swap_far(last_gu), near_gu)
    far_gu, near_gu, grads[2], send = together(far_gu, near_gu, grads[2], send)
    total, low = chip_sum(coords, keep, send)
    got = swap(low, "zl")
    resid, ffn_in = residual(coords, total, got, tokens[0], tokens[2], gains, weight_gu[3:4])
    keep, send, ffn, grads_all, grad_gu, act, wd_low = feed_forward(
        coords, (ffn_in, swap(ffn_in, "core")), weight_gu, down_weight, grads
    )
    total, low = chip_sum(coords, keep, send)
    low, grad_gu = together(low, grad_gu)
    pieces, part = spread(coords, ffn, [grad_gu], [swap(grad_gu, "core")], act, grads_all)
    got = swap(low, "zl")
    first = exchange(pieces, 0, 0)
    grad_resid, resid_low, grad_gain_second = turn_back(
        coords, total, got, grads[0], grads[2], resid, gains, (pieces[0],)
    )
    saved = (qk, val, probs, attended, gates, raw, gains, cosine, sine)
    front, resid_low, *others = back_first(coords, (resid_low, swap(resid_low, "core")), output_weight, saved)
    first = merge(coords, half_sum_kernel, first, (4,) * 4, (front,), 1)
    keep, send, back, small = back_second(
        coords,
        resid_low,
        output_weight,
        saved,
        (front, *others),
        (attn_in, hw, *weight_qkv, *tokens, grad_gain_second),
        first[:1],
    )
    first = exchange(first, 0, 1)
    first = exchange(merge(coords, turn_sum_kernel, first, (2,) * 4, (back,), 1), 1, 0)
    pieces, part_second = spread(
        coords,
        attn_in,
        [front, back],
        [swap(front, "core"), swap(back, "core")],
        mixed,
        resid_low,
        (small, swap(small, "core")),
        first[:1],
    )
    height = 2 * pieces[0].shape[1]
    second = exchange(pieces, 0, 0)
    first = exchange(merge(coords, half_sum_kernel, first, (1,) * 4, pieces[:1], 1), 1, 1)
    sums = group_scatter(coords, down(coords, act, wd_low, first[:1]), (keep, send), ())
    first = send_across(*last_sum(coords, first, part, sums[:1]))
    second = exchange(merge(coords, half_sum_kernel, second, (4,) * 4, first[2:3]), 0, 1)
    first = exchange(cross_sum(coords, first, second[:1]) * 2, 1, 1)
    second = direct(small_kernel_call(coords, quarter_sum_kernel, second, [(height, LANES)] * 4, first[:1]))
    first = exchange(merge(coords, join_kernel, first, (2, 2), second[:1]) * 2, 1, 0)
    shapes = [(part_second, LANES), (height - part_second, LANES)]
    second = send_across(*small_kernel_call(coords, direct_sum_kernel, second, shapes, first[:1]))
    first = exchange(merge(coords, pack_kernel, first, (4, 4), second[2:3]) * 2, 0, 1)
    second = direct(small_kernel_call(coords, plain_sum_kernel, second, [(height, LANES)], first[:1], 2 * 10**10) * 4)
    second = small_kernel_call(
        coords, direct_pack_kernel, second, [(4, height // 2, LANES)] * 2, first[2:], 2 * 10**10
    )
    second = exchange(second * 2, 0, 1)
    first = exchange(merge(coords, join_kernel, first, (8, 8), second[:1]) * 2, 0, 0)
    second = merge(coords, join_kernel, second, (8, 8), first[:1], 2 * 10**10)
    output, input_grad, finished = finish(coords, [*sums, resid, grad_resid, hidden, gains], second[:1])
    grad_g, grad_u, grad_d, settled = settle(coords, first, (768, 768), 768, False, (finished,))
    second = exchange(second * 2, 0, 0)
    (grad_q, grad_k, grad_v, grad_o, small_first, small_second, small_q, small_k, small_bias, grad_hw) = settle(
        coords, second, (512, 256, 256), 512, True, (settled,)
    )
    return (
        output,
        input_grad,
        small_first.reshape(256),
        grad_q,
        grad_k,
        grad_v,
        small_q.reshape(32),
        small_k.reshape(32),
        grad_hw.T,
        small_bias.reshape(4),
        grad_o,
        small_second.reshape(256),
        grad_g,
        grad_u,
        grad_d,
    )


def solution(mesh):
    grid = Mesh(mesh.devices.reshape(2, 4, 4, 2, 2), AXES)
    tokens, split, copies = P(AXES, None), P(GROUP, None), P(("zh", "y", "x"))
    line = P(GROUP)
    weights = (line, split, split, split, line, line, split, line, split, line, split, split, split)
    return jax.shard_map(
        body,
        mesh=grid,
        in_specs=(tokens, tokens, copies, copies, *weights),
        out_specs=(tokens, tokens, *weights),
        check_vma=False,
    )
```

```python
import functools
import math

import jax
import jax.numpy as jnp
from jax import lax
from jax.experimental import pallas as pl
from jax.experimental.pallas import tpu as pltpu
from jax.sharding import Mesh
from jax.sharding import PartitionSpec as P

EPS = 1e-06
THETA = 1000000.0
MASKED = -1e30
HEAD = 128
SCALE = 1.0 / math.sqrt(HEAD)
LOW = jnp.bfloat16
FULL = jnp.float32
AXES = ("zh", "y", "x", "zl", "core")
GROUP = ("zl", "core")
LANES = 128


def swap(value, axis):
    return lax.ppermute(value, axis, [(0, 1), (1, 0)])


def turn(value, step):
    return lax.ppermute(value, ("zh", "zl"), [(i, (i + step) % 4) for i in range(4)])


def swap_far(value):
    return lax.ppermute(value, ("zh", "zl"), [(0, 3), (3, 0), (1, 2), (2, 1)])


def swap_plane(value, axis, mask):
    pairs = []
    for y in range(4):
        for x in range(4):
            for core in range(2):
                to_y, to_x = (y, x ^ mask) if axis == core else (y ^ mask, x)
                pairs.append(((y * 4 + x) * 2 + core, (to_y * 4 + to_x) * 2 + core))
    return lax.ppermute(value, ("y", "x", "core"), pairs)


def dot(left, right):
    return jnp.dot(left, right, preferred_element_type=FULL)


def dot_t(left, right):
    return lax.dot_general(left, right, (((1,), (1,)), ((), ())), preferred_element_type=FULL)


def dot_tn(left, right):
    return lax.dot_general(left, right, (((0,), (0,)), ((), ())), preferred_element_type=FULL)


VMEM = pl.BlockSpec(memory_space=pltpu.VMEM)
SMEM = pl.BlockSpec(memory_space=pltpu.SMEM)


def held_bytes(shape, kind):
    shape = (1,) * (2 - len(shape)) + tuple(shape)
    size = math.prod(shape[:-2]) * (-(-shape[-2] // 16) * 16) * (-(-shape[-1] // LANES) * LANES)
    return size * jnp.dtype(kind).itemsize


class Late:
    def __init__(self, source, target, done):
        self.copy, self.target, self.open = pltpu.make_async_copy(source, target, done), target, True
        self.copy.start()

    def ready(self):
        if self.open:
            self.copy.wait()
        self.open = False
        return self.target


class Early:
    def __init__(self, source, target, done):
        self.copy, self.source, self.sent = pltpu.make_async_copy(source, target, done), source, False

    def send(self):
        if not self.sent:
            self.copy.start()
        self.sent = True


def call(kernel, coords, ins, outs, scratch, late=(), early=(), least=0, wait=(), flops=1):
    ins = list(ins)
    n_ins, n_outs, n_scratch = len(ins), len(outs), len(scratch)
    moving = [(ins[i].shape, ins[i].dtype) for i in late] + [outs[i] for i in early]

    def run(coords, *refs):
        refs = list(refs)
        del refs[n_ins : n_ins + len(wait)]
        done = refs.pop() if moving else None
        buffers = refs[n_ins + n_outs + n_scratch :]
        refs = refs[: n_ins + n_outs + n_scratch]
        for k, i in enumerate(late):
            refs[i] = Late(refs[i], buffers[k], done.at[k])
        sending = []
        for k, i in enumerate(early):
            k += len(late)
            sending.append(Early(buffers[k], refs[n_ins + i], done.at[k]))
            refs[n_ins + i] = sending[-1]
        kernel(coords, *refs)
        for i in late:
            refs[i].ready()
        for out in sending:
            out.send()
        for out in sending:
            out.copy.wait()

    need = sum(held_bytes(a.shape, a.dtype) for a in ins) + sum(held_bytes(*o) for o in [*outs, *scratch])
    anywhere = pl.BlockSpec(memory_space=pltpu.HBM)
    buffers = [pltpu.VMEM(shape, kind) for shape, kind in [*scratch, *moving]]
    return pl.pallas_call(
        run,
        out_shape=[jax.ShapeDtypeStruct(shape, kind) for shape, kind in outs],
        in_specs=[SMEM] + [anywhere if i in late else VMEM for i in range(n_ins)] + [pl.BlockSpec(memory_space=pl.ANY)] * len(wait),
        out_specs=[anywhere if i in early else VMEM for i in range(n_outs)],
        scratch_shapes=buffers + ([pltpu.SemaphoreType.DMA((len(moving),))] if moving else []),
        compiler_params=pltpu.CompilerParams(vmem_limit_bytes=max(need + 8 * 2**20, least * 2**20)),
        cost_estimate=pl.CostEstimate(flops=flops, bytes_accessed=1, transcendentals=0),
    )(coords, *ins, *wait)


def lanes(index, width):
    return pl.ds(pl.multiple_of(index * width, LANES), width)


def rows(index, height):
    return pl.ds(pl.multiple_of(index * height, 16), height)


def inverse_rms(value):
    return lax.rsqrt(jnp.mean(value * value, -1, keepdims=True) + EPS)


def norm_back(grad, normal, inverse):
    return inverse * (grad - normal * jnp.mean(grad * normal, -1, keepdims=True))


def cut_kernel(widths, small, coords, *refs):
    ins, outs = refs[: len(widths)], refs[len(widths) + 2 * small :]
    j = coords[2]
    if small:
        heads, line = refs[len(widths) : len(widths) + 2]
        line = jnp.concatenate([line[...], jnp.zeros((15, 768), FULL)], 0)
        tile = jnp.concatenate([heads[...], line], 1).astype(LOW)
    third = [(3, 0, 256)] if small else [(3, 0, 128), (3, 128, 128)]
    for out, (r, first, count) in zip(outs, [(1, 0, 256), *third, (2, 0, 256), (0, 0, 256)]):
        at = 0
        for w, n in zip(ins, widths):
            out[0:count, at : at + n] = w[first : first + count, lanes(j ^ r, n)].astype(LOW)
            at += n
        if small:
            out[256:272, :] = tile


def take_columns(coords, weights, widths, small=(), wait=()):
    heights = (272,) * 4 if small else (256, 128, 128, 256, 256)
    beside, *across, other, mine = call(
        functools.partial(cut_kernel, widths, bool(small)),
        coords,
        [*weights, *small],
        [((n, sum(widths)), LOW) for n in heights],
        [],
        least=50,
        wait=wait,
    )
    return mine, swap(beside, "core"), other, *[swap(piece, "core") for piece in across]


def first_kernel(coords, t0, t1, t2, t3, w0, w1, w2, w3, wo, cos, sin, segs, bias, *refs):
    (keep, send, attn_in, raw, qk, val, probs, attended, gates, mixed, hw, gains, cos_rel, sin_rel) = refs[:14]
    (wo_low, mask) = refs[14:]
    (attn_out, raw_out, qk_out, val_out, probs_out, att_out, gates_out, mixed_out) = refs[2:10]
    attn_in, raw, qk, val, probs, attended, gates, mixed = [r.source for r in refs[2:10]]
    cos_out, sin_out = refs[12:14]
    cos_rel, sin_rel = cos_out.source, sin_out.source
    j = coords[2]
    tokens, weights = (t0, t1, t2, t3), (w0, w1, w2, w3)
    hw[...] = jnp.zeros_like(hw)
    gains[...] = jnp.zeros_like(gains)
    gain_q, gain_k = jnp.zeros((16, LANES), FULL), jnp.zeros((16, LANES), FULL)
    for r in range(4):
        small = weights[r][256:272, :]
        hw[0:16, lanes(j ^ r, 256)] = small[:, 0:256]
        small = small[:, 256:].astype(FULL)
        gains[0:1, lanes(j ^ r, 256)] = small[0:1, 0:256]
        gains[1:2, lanes(j ^ r, 256)] = small[0:1, 256:512]
        gain_q += pltpu.roll(small[:, 512:640], (j ^ r) * 32, 1)
        gain_k += pltpu.roll(small[:, 640:768], (j ^ r) * 32, 1)
        cos_rel[r * 128 : r * 128 + 128, :] = cos.ready()[rows(j ^ r, 128), :]
        sin_rel[r * 128 : r * 128 + 128, :] = sin.ready()[rows(j ^ r, 128), :]
    gains[2:3, 0:128] = gain_q[0:1]
    gains[2:3, 128:256] = gain_k[0:1]
    for r in range(4):
        x = tokens[r][0:128, :].astype(FULL)
        attn_in[r * 128 : r * 128 + 128, :] = (x * inverse_rms(x) * gains[0:1, :]).astype(LOW)

    attn_out.send()
    cos_out.send()
    sin_out.send()

    logit = dot_t(attn_in[...], hw[...])
    logit = pltpu.roll(logit, (32 - j) * 4 & 127, 1) + bias[...].astype(LOW).astype(FULL)
    gates[...] = jax.nn.sigmoid(logit)
    gates_out.send()
    for n in range(4):
        total = dot(attn_in[:, lanes(j, 256)], w0[0:256, n * 256 : n * 256 + 256])
        for r in range(1, 4):
            total += dot(attn_in[:, lanes(j ^ r, 256)], weights[r][0:256, n * 256 : n * 256 + 256])
        if n < 3:
            raw[:, n * 256 : n * 256 + 256] = total
        else:
            val[...] = total.astype(LOW)
    raw_out.send()
    val_out.send()
    for h in range(6):
        at = slice(h * 128, h * 128 + 128)
        part = raw[:, at]
        gain = gains[2:3, 0:128] if h < 4 else gains[2:3, 128:256]
        part = part * inverse_rms(part) * gain
        qk[:, at] = (part * cos_rel[...] + pltpu.roll(part, 64, 1) * sin_rel[...]).astype(LOW)

    qk_out.send()
    lane = lax.broadcasted_iota(jnp.int32, (128, 128), 1)
    line = lax.broadcasted_iota(jnp.int32, (128, 128), 0)
    for c in range(4):
        seg_q = jnp.broadcast_to(segs[pl.ds(j ^ c, 1), :], (128, 128)).T
        for b in range(4):
            seg_k = segs[pl.ds(j ^ b, 1), :]
            earlier = lane + (j ^ b) * 128 <= line + (j ^ c) * 128
            mask[c * 128 : c * 128 + 128, b * 128 : b * 128 + 128] = jnp.where(
                earlier & (seg_q == seg_k), 0.0, MASKED
            )
    for h in range(4):
        kv = h // 2
        for c in range(2):
            at = slice(c * 256, c * 256 + 256)
            scores = dot_t(qk[at, h * 128 : h * 128 + 128], qk[:, 512 + kv * 128 : 640 + kv * 128])
            scores = scores * SCALE + mask[at, :]
            expo = jnp.exp(scores - jnp.max(scores, -1, keepdims=True))
            part = (expo * (1.0 / jnp.sum(expo, -1, keepdims=True))).astype(LOW)
            probs[h, at, :] = part
            result = dot(part, val[:, kv * 128 : kv * 128 + 128])
            attended[at, h * 128 : h * 128 + 128] = result
            mixed[at, h * 128 : h * 128 + 128] = (result * gates[at, h : h + 1]).astype(LOW)
    probs_out.send()
    att_out.send()
    mixed_out.send()
    wo_low[...] = wo.ready()[...].astype(LOW)
    for n in range(4):
        at = slice(n * 256, n * 256 + 256)
        result = dot(mixed[...], wo_low[:, at])
        for c in range(2):
            keep[c, :, at] = result[c * 256 : c * 256 + 128]
            send[c, :, at] = result[c * 256 + 128 : c * 256 + 256].astype(LOW)


def attention_forward(coords, tokens, weights, wo, cos, sin, segs, bias):
    outs = [
        ((2, 128, 1024), FULL),
        ((2, 128, 1024), LOW),
        ((512, 1024), LOW),
        ((512, 768), FULL),
        ((512, 768), LOW),
        ((512, 256), LOW),
        ((4, 512, 512), LOW),
        ((512, 512), FULL),
        ((512, 128), FULL),
        ((512, 512), LOW),
        ((128, 1024), LOW),
        ((8, 1024), FULL),
        ((512, 128), FULL),
        ((512, 128), FULL),
    ]
    return call(
        first_kernel,
        coords,
        [*tokens, *weights, wo, cos, sin, segs, bias],
        outs,
        [((512, 1024), LOW), ((512, 512), FULL)],
        (9, 10, 8),
        (2, 3, 4, 5, 6, 7, 8, 9, 12, 13),
    )


def ffn_kernel(coords, f_own, f_got, w0, w1, w2, w3_low, w3_high, wd, g0, g1, g2, g3, *refs):
    (keep, send, ffn, grads, grad_gu, act, wd_low, w3) = refs
    j = coords[2]
    weights = (w0, w1, w2, w3)
    w3[0:128, :] = w3_low[...]
    w3[128:256, :] = w3_high[...]
    for r, g in enumerate((g0, g1, g2, g3)):
        ffn[r * 128 : r * 128 + 128, :] = (f_got if r % 2 else f_own)[r // 2]
        grads[r * 128 : r * 128 + 128, :] = g[...]
    wd_low[...] = wd[...].astype(LOW)
    for m in range(2):
        at = slice(m * 256, m * 256 + 256)
        for n in range(3):
            low, high = slice(n * 256, n * 256 + 256), slice(768 + n * 256, 1024 + n * 256)
            gate = dot(ffn[at, lanes(j, 256)], w0[:, low])
            up = dot(ffn[at, lanes(j, 256)], w0[:, high])
            for r in range(1, 4):
                gate += dot(ffn[at, lanes(j ^ r, 256)], weights[r][:, low])
                up += dot(ffn[at, lanes(j ^ r, 256)], weights[r][:, high])
            back = dot_t(grads[at, :], wd_low[low, :])
            sigma = jax.nn.sigmoid(gate)
            swish = gate * sigma
            act[at, low] = (swish * up).astype(LOW)
            grad_gu[at, low] = (back * up * sigma * (1.0 + gate * (1.0 - sigma))).astype(LOW)
            grad_gu[at, high] = (back * swish).astype(LOW)
    for r in range(4):
        part = dot_t(grad_gu[...], weights[r][...])
        for t in range(2):
            keep[t, :, lanes(j ^ r, 256)] = part[t * 256 : t * 256 + 128]
            send[t, :, lanes(j ^ r, 256)] = part[t * 256 + 128 : t * 256 + 256].astype(LOW)


def feed_forward(coords, ffn_in, weights, wd, grads):
    outs = [
        ((2, 128, 1024), FULL),
        ((2, 128, 1024), LOW),
        ((512, 1024), LOW),
        ((512, 1024), LOW),
        ((512, 1536), LOW),
        ((512, 768), LOW),
        ((768, 1024), LOW),
    ]
    return call(
        ffn_kernel,
        coords,
        [*ffn_in, *weights, wd, *grads],
        outs,
        [((256, 1536), LOW)],
    )


def down_kernel(coords, act, wd_low, keep, send):
    for c in range(4):
        result = dot(act[c * 128 : c * 128 + 128, :], wd_low[...])
        if c % 2:
            send[c // 2] = result.astype(LOW)
        else:
            keep[c // 2] = result


def down(coords, act, wd_low, wait):
    outs = [((2, 128, 1024), FULL), ((2, 128, 1024), LOW)]
    return call(down_kernel, coords, [act, wd_low], outs, [], wait=wait)


def heads_back(kv, refs, resid_low, wo_low, grad_scores, out):
    (qk, val, probs, attended, gates, raw, gains, cos, sin) = refs
    lane = lax.broadcasted_iota(jnp.int32, (512, LANES), 1)
    grad_logit = jnp.zeros((512, LANES), FULL)
    gain_sums = []

    def head_back(grad, at, gain, to):
        part = raw.ready()[:, at]
        inverse = inverse_rms(part)
        normal = part * inverse
        turned = grad * cos.ready()[...] - pltpu.roll(grad, 64, 1) * sin.ready()[...]
        gain_sums.append(jnp.sum(turned * normal, 0, keepdims=True))
        out[:, to : to + 128] = norm_back(turned * gain, normal, inverse).astype(LOW)

    key_at = slice(512 + kv * 128, 640 + kv * 128)
    grad_key = grad_value = None
    for n, h in enumerate((2 * kv, 2 * kv + 1)):
        at = slice(h * 128, h * 128 + 128)
        grad_mixed = dot_t(resid_low[...], wo_low[n * 128 : n * 128 + 128, :])
        gate = gates.ready()[:, h : h + 1]
        grad_gate = jnp.sum(grad_mixed * attended.ready()[:, at], -1, keepdims=True) * gate * (1.0 - gate)
        grad_logit = jnp.where(lane == h, grad_gate, grad_logit)
        grad_att = (grad_mixed * gate).astype(LOW)
        for c in range(2):
            line = slice(c * 256, c * 256 + 256)
            grad_probs = dot_t(grad_att[line], val.ready()[:, kv * 128 : kv * 128 + 128])
            part = probs.ready()[h, line, :].astype(FULL)
            inner = jnp.sum(part * grad_probs, -1, keepdims=True)
            grad_scores[line, :] = (part * (grad_probs - inner)).astype(LOW)
        head_back(dot(grad_scores[...], qk.ready()[:, key_at]) * SCALE, at, gains.ready()[2:3, 0:128], n * 128)
        more_key = dot_tn(grad_scores[...], qk.ready()[:, at])
        more_value = dot_tn(probs.ready()[h], grad_att)
        grad_key = more_key if grad_key is None else grad_key + more_key
        grad_value = more_value if grad_value is None else grad_value + more_value
    head_back(grad_key * SCALE, key_at, gains.ready()[2:3, 128:256], 256)
    out[:, 384:512] = grad_value.astype(LOW)
    return grad_logit, gain_sums


def back_first_kernel(coords, l_own, l_got, wo, qk, val, probs, attended, gates, raw, gains, cos, sin, *refs):
    (out, resid_low, logit, sums, wo_low, grad_scores) = refs
    wo_low[...] = wo.ready()[0:256, :].astype(LOW)
    for r in range(4):
        resid_low[r * 128 : r * 128 + 128, :] = (l_got if r % 2 else l_own)[r // 2]
    refs = (qk, val, probs, attended, gates, raw, gains, cos, sin)
    grad_logit, gain_sums = heads_back(0, refs, resid_low, wo_low, grad_scores, out)
    logit[...] = grad_logit
    sums[...] = jnp.zeros_like(sums)
    for i, value in enumerate(gain_sums):
        sums[i : i + 1, :] = value


def back_kernel(coords, *refs):
    (resid_low, wo, qk, val, probs, attended, gates, raw, gains, cos, sin, out_first, logit, sums) = refs[:14]
    (attn_in, hw, w0, w1, w2, w3, t0, t1, t2, t3, gain_second) = refs[14:25]
    (keep, send, out, small) = refs[25:29]
    (wo_low, grad_scores, grad_qkv) = refs[29:]
    j = coords[2]
    wo_low[...] = wo.ready()[256:512, :].astype(LOW)
    refs = (qk, val, probs, attended, gates, raw, gains, cos, sin)
    grad_logit, gain_sums = heads_back(1, refs, resid_low, wo_low, grad_scores, out)
    for kv, part in enumerate((out_first, out)):
        grad_qkv[:, kv * 256 : kv * 256 + 256] = part[:, 0:256]
        grad_qkv[:, 512 + kv * 128 : 640 + kv * 128] = part[:, 256:384]
        grad_qkv[:, 768 + kv * 128 : 896 + kv * 128] = part[:, 384:512]

    weights, tokens = [[r.ready() for r in group] for group in ((w0, w1, w2, w3), (t0, t1, t2, t3))]
    attn_in, hw = attn_in.ready(), hw.ready()
    grad_logit = (grad_logit + logit[...]).astype(LOW)
    grad_bias = jnp.sum(grad_logit.astype(FULL), 0, keepdims=True)
    grad_hw = dot_tn(grad_logit, attn_in[...])
    spread_logit = pltpu.roll(grad_logit.astype(FULL), j * 4, 1).astype(LOW)
    inverses = []
    for r in range(4):
        x = tokens[r][0:128, :].astype(FULL)
        inverses.append(inverse_rms(x))
    small[...] = jnp.zeros_like(small)

    def put(row, value):
        small[row // 4, row % 4 : row % 4 + 1, :] = value

    for r in range(4):
        at = lanes(j ^ r, 256)
        part = dot_t(grad_qkv[...], weights[r][0:256, :]) + dot(spread_logit, hw[:, at])
        total = jnp.zeros((1, 256), FULL)
        for t in range(4):
            piece = part[t * 128 : t * 128 + 128]
            normal = tokens[t][0:128, at].astype(FULL) * inverses[t]
            total += jnp.sum(piece * normal, 0, keepdims=True)
            if t % 2:
                send[t // 2, :, at] = piece.astype(LOW)
            else:
                keep[t // 2, :, at] = piece
        block = (j ^ r) // 2
        for i in range(2):
            small[block, pl.ds((j ^ r) % 2 * 2 + i, 1), :] = total[:, i * 128 : i * 128 + 128]
    for i in range(8):
        put(8 + i, gain_second[0:1, i * 128 : i * 128 + 128])
    put(16, gain_sums[0] + gain_sums[1] + sums[0:1, :] + sums[1:2, :])
    put(17, gain_sums[2] + sums[2:3, :])
    put(18, grad_bias)
    for h in range(4):
        for i in range(8):
            put(24 + h * 8 + i, grad_hw[h : h + 1, i * 128 : i * 128 + 128])


def back_first(coords, resid_low, wo, saved):
    outs = [((512, 512), LOW), ((512, 1024), LOW), ((512, 128), FULL), ((8, 128), FULL)]
    scratch = [((256, 1024), LOW), ((512, 512), LOW)]
    return call(back_first_kernel, coords, [*resid_low, wo, *saved], outs, scratch, (2, 7, 6, 4, 5, 3, 8, 9, 10, 11), flops=3*10**9)


def back_second(coords, resid_low, wo, saved, first, others, wait):
    outs = [((2, 128, 1024), FULL), ((2, 128, 1024), LOW), ((512, 512), LOW), ((16, 8, 128), FULL)]
    scratch = [((256, 1024), LOW), ((512, 512), LOW), ((512, 1024), LOW)]
    ins = [resid_low, wo, *saved, *first, *others]
    late = [1, 6, 5, 3, 4, 2, *range(7, 11), *range(16, 24), 14, 15]
    return call(back_kernel, coords, ins, outs, scratch, late, wait=wait)


KEPT, SENT, MASKS = ((0, 3), (0, 1)), ((1, 2), (3, 2)), ((1, 3), (3, 1))


def spread_kernel(n_right, with_small, coords, left_c, *refs):
    rights, (left_r, right_r, *refs) = refs[: 2 * n_right], refs[2 * n_right :]
    if with_small:
        small_own, small_got, *refs = refs
    outs, (turned_c, turned_r, held_c, held_r) = refs[:4], refs[4:]
    first, second, j = coords[0], coords[1], coords[2]
    wide = rights[0].shape[1] // LANES
    panels = wide * n_right
    rows_r = left_r.shape[1] // 16
    part = 2 * panels * 16 + (16 if with_small else 0)
    edge = outs[0].shape[1]
    blocks = [(m, n, (first ^ m) * 4 + (second ^ n)) for m in (1, 2, 3, 0) for n in range(4)]

    def put(m, n, low, value):
        stream = 0 if low < edge else 1
        sent = m in SENT[stream]
        at = (SENT if sent else KEPT)[stream].index(m) * 4 + n
        low -= edge * stream
        outs[2 * sent + stream][at, low : low + value.shape[0], :] = value

    for d in range(2):
        turned = left_c[:, lanes(j ^ (2 * d), 256)].T
        turned_c[d] = turned
        for t in range(4):
            turned_c[2 + d, :, t * 128 : t * 128 + 128] = turned[:, (t ^ 1) * 128 : (t ^ 1) * 128 + 128]
    turned_r[...] = left_r[...].T
    for k, right in enumerate(rights):
        src, start = k // n_right, k % n_right * wide
        for d in range(2):
            held_c[...] = dot(turned_c[2 * src + d], right[...]).astype(LOW)
            for m, n, block in blocks:
                for p in range(wide):
                    low = (1 - d) * part + (src * panels + start + p) * 16
                    put(m, n, low, held_c[rows(block, 16), p * LANES : (p + 1) * LANES])
    held_r[...] = dot(turned_r[...], right_r[...]).astype(LOW)
    for m, n, block in blocks:
        if with_small:
            tile = jnp.concatenate([small_own[block], small_got[block]], 0).astype(LOW)
            put(m, n, part - 16, tile)
            put(m, n, 2 * part - 16, tile)
        for p in range(8):
            put(m, n, 2 * part + p * rows_r, held_r[rows(block, rows_r), p * LANES : (p + 1) * LANES])


def spread(coords, left_c, own, got, left_r, right_r, small=(), wait=()):
    wide = own[0].shape[1]
    panels = wide * len(own) // LANES
    part = 2 * panels * 16 + (16 if small else 0)
    height = 2 * part + left_r.shape[1] // 2
    scratch = [
        ((4, 256, 512), LOW),
        ((left_r.shape[1], 512), LOW),
        ((256, wide), LOW),
        ((left_r.shape[1], 1024), LOW),
    ]
    pieces = call(
        functools.partial(spread_kernel, len(own), bool(small)),
        coords,
        [left_c, *own, *got, left_r, right_r, *small],
        [((8, height // 2, LANES), LOW)] * 4,
        scratch,
        wait=wait,
    )
    return pieces, part


def plus(a, b):
    return (a.astype(FULL) + b.astype(FULL)).astype(LOW)


def half_sum_kernel(coords, p, q, got_p, got_q, *outs):
    half = p.shape[0] // 2
    for kept, sent, mine, got in ((outs[0], outs[2], p, got_p), (outs[1], outs[3], q, got_q)):
        kept[...] = plus(mine[0:half], got[0:half])
        sent[...] = plus(mine[half:], got[half:])


def turn_sum_kernel(coords, p, q, got_p, got_q, *outs):
    for s, (mine, got) in enumerate(((p, got_p), (q, got_q))):
        for at in range(2):
            outs[s][at] = plus(mine[KEPT[s][at]], got[KEPT[s][at]])
            outs[2 + s][at] = plus(mine[SENT[s][at]], got[SENT[s][at]])


def last_sum_kernel(coords, p, q, got_p, got_q, other, mine):
    part, edge = other.shape[0], p.shape[1]
    p, q = plus(p[0], got_p[0]), plus(q[0], got_q[0])
    other[...] = p[:part]
    mine[0 : edge - part, :] = p[part:]
    mine[edge - part :, :] = q


def cross_sum_kernel(coords, ahead, behind, mine, far, p, q):
    part, edge = ahead.shape[0], p.shape[1]
    p[0, 0:part, :] = plus(ahead[...], behind[...])
    mine = plus(mine[...], far[...])
    p[0, part:, :] = mine[: edge - part]
    q[0] = mine[edge - part :]


def quarter_sum_kernel(coords, p, q, got_p, got_q, *outs):
    edge = p.shape[1]
    for n in range(4):
        outs[n][0:edge, :] = plus(p[n], got_p[n])
        outs[n][edge:, :] = plus(q[n], got_q[n])


def direct_sum_kernel(coords, a, b, c, d, other, mine):
    total = (a[...].astype(FULL) + b[...].astype(FULL) + c[...].astype(FULL) + d[...].astype(FULL)).astype(LOW)
    part = other.shape[0]
    other[...] = total[:part]
    mine[...] = total[part:]


def plain_sum_kernel(coords, ahead, behind, mine, far, out):
    part = ahead.shape[0]
    out[0:part, :] = plus(ahead[...], behind[...])
    out[part:, :] = plus(mine[...], far[...])


def direct_pack_kernel(coords, a, b, c, d, p, q):
    edge = p.shape[1]
    for n, ref in enumerate((a, b, c, d)):
        p[n] = ref[0:edge, :]
        q[n] = ref[edge:, :]


def direct(parts):
    return [parts[0]] + [swap_plane(parts[m], 1, m) for m in (1, 2, 3)]


def small_kernel_call(coords, kernel, got, shapes, wait, flops=4 * 10**9):
    return call(kernel, coords, got, [(shape, LOW) for shape in shapes], [], wait=wait, flops=flops)


def join_kernel(coords, p, q, got_p, got_q, both_p, both_q):
    half = p.shape[0]
    for both, mine, got in ((both_p, p, got_p), (both_q, q, got_q)):
        both[0:half] = mine[...]
        both[half:] = got[...]


def pack_kernel(coords, p, q, got_p, got_q, all_p, all_q):
    for s, (whole, mine, got) in enumerate(((all_p, p, got_p), (all_q, q, got_q))):
        for at in range(2):
            whole[KEPT[s][at]] = mine[at]
            whole[SENT[s][at]] = got[at]


def exchange(pieces, axis, step):
    return [*pieces[:2], *[swap_plane(pieces[2 + s], axis, MASKS[s][step]) for s in range(2)]]


def merge(coords, kernel, got, counts, wait, flops=4 * 10**9):
    outs = [((n, *got[0].shape[1:]), LOW) for n in counts]
    return call(kernel, coords, got, outs, [], wait=wait, flops=flops)


def send_across(other, mine):
    return [turn(other, 1), turn(other, -1), mine, turn(mine, 2)]


def last_sum(coords, got, part, wait, flops=1):
    outs = [((part, LANES), LOW), ((2 * got[0].shape[1] - part, LANES), LOW)]
    return call(last_sum_kernel, coords, got, outs, [], wait=wait, flops=flops)


def cross_sum(coords, got, wait):
    edge = (got[0].shape[0] + got[2].shape[0]) // 2
    return call(cross_sum_kernel, coords, got, [((1, edge, LANES), LOW)] * 2, [], wait=wait, flops=4 * 10**9)


def together(*values):
    return lax.optimization_barrier(values)


def settle_kernel(widths, with_small, coords, *refs):
    ins, outs = refs[:4], refs[4:]
    first, second, j = coords[0], coords[1], coords[2]
    panels = sum(widths) // LANES
    out_r = outs[len(widths)]
    rows_r = out_r.shape[0] // 16
    spots = []
    for kv in range(2 if with_small else 1):
        for w, width in enumerate(widths):
            count = width // LANES // (2 if with_small else 1)
            spots += [(w, (kv * count + i) * LANES) for i in range(count)]
    if with_small:
        total, heads = refs[-2:]
        total[...] = jnp.zeros_like(total)

    part = 2 * panels * 16 + (16 if with_small else 0)
    edge = ins[0].shape[1]

    def take(m, n, low, height):
        stream = 0 if low < edge else 1
        came = m in SENT[stream]
        at = (SENT if came else KEPT)[stream].index(m) * 4 + n
        low -= edge * stream
        return ins[2 * came + stream][at, low : low + height, :].astype(FULL)

    for m in range(4):
        for n in range(4):
            block = (first ^ m) * 4 + (second ^ n)
            line = rows(block, 16)
            for r in range(4):
                base = (1 - r // 2) * part + (r % 2) * panels * 16
                for p, (w, col) in enumerate(spots):
                    lane = pl.ds(pl.multiple_of((j ^ r) * widths[w] + col, LANES), LANES)
                    low = base + p * 16
                    outs[w][line, lane] = take(m, n, low, 16)
            for p in range(8):
                low = 2 * part + p * rows_r
                lane = slice(p * LANES, (p + 1) * LANES)
                out_r[rows(block, rows_r), lane] = take(m, n, low, rows_r)
            if with_small:
                for z in range(2):
                    tile = take(m, n, (1 - z) * part + part - 16, 16)
                    for src in range(2):
                        value = tile[src * 8 : src * 8 + 8]
                        heads[j ^ (2 * z + src), block] = value
                        total[block] += value
    if not with_small:
        outs[-1][...] = jnp.zeros((8, LANES), FULL)
    if with_small:
        gain_first, gain_second, gain_q, gain_k, bias, hw = outs[len(widths) + 1 : len(widths) + 7]
        for i in range(2):
            at = slice(i * 128, i * 128 + 128)
            gain_first[:, at] = total[j // 2, pl.ds(j % 2 * 2 + i, 1), :]
            gain_second[:, at] = total[2 + j // 2, pl.ds(j % 2 * 2 + i, 1), :]
        shift = (4 - j) * 32 & 127
        turned = pltpu.roll(total[4], shift, 1)
        gain_q[...] = turned[0:1, :32]
        gain_k[...] = turned[1:2, :32]
        bias[...] = heads[j, 4][2:3, :4]
        lines = []
        for q in range(4):
            for h in range(4):
                start = 24 + h * 8
                lines.append(
                    jnp.concatenate(
                        [heads[q, start // 4 + j // 2, pl.ds(j % 2 * 2 + i, 1), :] for i in range(2)], 1
                    )
                )
        whole = jnp.concatenate(lines, 0)
        hw[...] = whole


def settle(coords, pieces, widths, rows_r, with_small, wait):
    outs = [((256, 4 * w), FULL) for w in widths] + [((rows_r, 1024), FULL)]
    scratch = []
    if with_small:
        outs += [((1, n), FULL) for n in (256, 256, 32, 32, 4)] + [((16, 256), FULL)]
        scratch = [((16, 8, 128), FULL), ((4, 16, 8, 128), FULL)]
    else:
        outs += [((8, LANES), FULL)]
    return call(functools.partial(settle_kernel, widths, with_small), coords, pieces, outs, scratch, wait=wait)


def group_gather(part):
    beside = swap(part, "core")
    across = swap(part, "zl")
    return part, beside, across, swap(across, "core")


def add_kernel(coords, keep, got, total, low):
    value = keep[...] + got[...].astype(FULL)
    total[...] = value
    low[...] = value.astype(LOW)


def chip_sum(coords, keep, send, wait=()):
    outs = [((2, 128, 1024), FULL), ((2, 128, 1024), LOW)]
    return call(add_kernel, coords, [keep, swap(send, "core")], outs, [], wait=wait)


def own_kernel(coords, keep, got, more_keep, more_got, *outs):
    (mine, more, low) = outs
    for s, (kept, came, own) in enumerate(((keep, got, mine), (more_keep, more_got, more))):
        own[...] = kept[0] + came[0].astype(FULL)
        low[s] = (kept[1] + came[1].astype(FULL)).astype(LOW)


def group_scatter(coords, first, second, wait):
    ins = [first[0], swap(first[1], "core"), second[0], swap(second[1], "core")]
    outs = [((128, 1024), FULL)] * 2 + [((2, 128, 1024), LOW)]
    mine, more, low = call(own_kernel, coords, ins, outs, [], wait=wait)
    return mine, more, swap(low, "zl")


def end_kernel(coords, mine, more, got, resid, grad_resid, hidden, gains, output, input_grad, flag):
    flag[...] = jnp.zeros((8, LANES), FULL)
    output[...] = (resid[0] + (mine[...] + got[0].astype(FULL))).astype(LOW)
    x = hidden[...].astype(FULL)
    inverse = inverse_rms(x)
    grad = (more[...] + got[1].astype(FULL)) * gains[0:1, :]
    input_grad[...] = (grad_resid[...] + norm_back(grad, x * inverse, inverse)).astype(LOW)


def finish(coords, ins, wait):
    return call(end_kernel, coords, ins, [((128, 1024), LOW)] * 2 + [((8, LANES), FULL)], [], wait=wait)


def resid_kernel(coords, total, got, h0, h2, gains, resid, low):
    for d, hidden in enumerate((h0, h2)):
        value = hidden[...].astype(FULL) + (total[d] + got[1 - d].astype(FULL))
        resid[d] = value
        low[d] = (value * inverse_rms(value) * gains[1:2, :]).astype(LOW)


def residual(coords, total, got, h0, h2, gains, wait):
    outs = [((2, 128, 1024), FULL), ((2, 128, 1024), LOW)]
    return call(resid_kernel, coords, [total, got, h0, h2, gains], outs, [], wait=wait)


def turn_kernel(coords, total, got, g0, g2, resid, gains, grad_resid, low, gain_sum):
    for d, upstream in enumerate((g0, g2)):
        value = resid[d]
        inverse = inverse_rms(value)
        normal = value * inverse
        grad = total[d] + got[1 - d].astype(FULL)
        back = upstream[...].astype(FULL) + norm_back(grad * gains[1:2, :], normal, inverse)
        low[d] = back.astype(LOW)
        if d == 0:
            grad_resid[...] = back
            gain_sum[...] = jnp.sum(grad * normal, 0, keepdims=True)


def turn_back(coords, total, got, g0, g2, resid, gains, wait):
    outs = [((128, 1024), FULL), ((2, 128, 1024), LOW), ((1, 1024), FULL)]
    return call(turn_kernel, coords, [total, got, g0, g2, resid, gains], outs, [], wait=wait)


def body(
    hidden,
    cotangent,
    segment_ids,
    positions,
    attention_gain,
    query_weight,
    key_weight,
    value_weight,
    query_gain,
    key_gain,
    headgate_weight,
    headgate_bias,
    output_weight,
    feedforward_gain,
    gate_weight,
    up_weight,
    down_weight,
):
    core = lax.axis_index("core")
    x_at, y_at = lax.axis_index("x"), lax.axis_index("y")
    j = lax.axis_index("zl") * 2 + core
    coords = jnp.stack([jnp.where(core == 0, x_at, y_at), jnp.where(core == 0, y_at, x_at), j]).astype(jnp.int32)

    freq = jnp.power(jnp.float32(THETA), -jnp.arange(64, dtype=FULL) * 2.0 / HEAD)
    angle = positions.astype(FULL)[:, None] * freq[None, :]
    cosine, sine = jnp.cos(angle), jnp.sin(angle)
    cosine, sine = jnp.concatenate([cosine, cosine], 1), jnp.concatenate([-sine, sine], 1)
    across = swap(hidden, "zl")
    across, gate_weight, up_weight = together(across, gate_weight, up_weight)
    tokens = (hidden, swap(hidden, "core"), across, swap(across, "core"))
    line = [attention_gain, feedforward_gain, jnp.pad(query_gain, (0, 96)), jnp.pad(key_gain, (0, 96))]
    small = (headgate_weight.T, jnp.concatenate(line)[None])
    mine, got, far, near = take_columns(coords, (query_weight, key_weight, value_weight), (512, 256, 256), small)
    far, near = swap_far(far), swap(near, "zl")
    mine_gu, got_gu, far_gu, last_gu, near_gu = take_columns(
        coords, (gate_weight, up_weight), (768, 768), (), (cosine,)
    )
    far, far_gu = together(far, far_gu)
    far_gu = swap_far(far_gu)
    near, cotangent, near_gu = together(near, cotangent, near_gu)
    grads = list(group_gather(cotangent))
    near_gu = swap(near_gu, "zl")
    weight_qkv = (mine, got, far, near)

    bias = jnp.pad(headgate_bias, (0, 124))[None]

    (keep, send, attn_in, raw, qk, val, probs, attended, gates, mixed, hw, gains, cosine, sine) = attention_forward(
        coords, tokens, weight_qkv, output_weight, cosine, sine, segment_ids.reshape(4, 128), bias
    )
    far_gu, last_gu = together(far_gu, last_gu)
    weight_gu = (mine_gu, got_gu, far_gu, swap_far(last_gu), near_gu)
    far_gu, near_gu, grads[2], send = together(far_gu, near_gu, grads[2], send)
    total, low = chip_sum(coords, keep, send)
    got = swap(low, "zl")
    resid, ffn_in = residual(coords, total, got, tokens[0], tokens[2], gains, weight_gu[3:4])
    keep, send, ffn, grads_all, grad_gu, act, wd_low = feed_forward(
        coords, (ffn_in, swap(ffn_in, "core")), weight_gu, down_weight, grads
    )
    total, low = chip_sum(coords, keep, send)
    low, grad_gu = together(low, grad_gu)
    pieces, part = spread(coords, ffn, [grad_gu], [swap(grad_gu, "core")], act, grads_all)
    got = swap(low, "zl")
    first = exchange(pieces, 0, 0)
    grad_resid, resid_low, grad_gain_second = turn_back(
        coords, total, got, grads[0], grads[2], resid, gains, (pieces[0],)
    )
    saved = (qk, val, probs, attended, gates, raw, gains, cosine, sine)
    front, resid_low, *others = back_first(coords, (resid_low, swap(resid_low, "core")), output_weight, saved)
    first = merge(coords, half_sum_kernel, first, (4,) * 4, (front,), 1)
    keep, send, back, small = back_second(
        coords,
        resid_low,
        output_weight,
        saved,
        (front, *others),
        (attn_in, hw, *weight_qkv, *tokens, grad_gain_second),
        first[:1],
    )
    first = exchange(first, 0, 1)
    first = exchange(merge(coords, turn_sum_kernel, first, (2,) * 4, (back,), 1), 1, 0)
    pieces, part_second = spread(
        coords,
        attn_in,
        [front, back],
        [swap(front, "core"), swap(back, "core")],
        mixed,
        resid_low,
        (small, swap(small, "core")),
        first[:1],
    )
    height = 2 * pieces[0].shape[1]
    second = exchange(pieces, 0, 0)
    first = exchange(merge(coords, half_sum_kernel, first, (1,) * 4, pieces[:1], 1), 1, 1)
    sums = group_scatter(coords, down(coords, act, wd_low, first[:1]), (keep, send), ())
    first = send_across(*last_sum(coords, first, part, sums[:1]))
    second = exchange(merge(coords, half_sum_kernel, second, (4,) * 4, first[2:3]), 0, 1)
    first = exchange(cross_sum(coords, first, second[:1]) * 2, 1, 1)
    second = direct(small_kernel_call(coords, quarter_sum_kernel, second, [(height, LANES)] * 4, first[:1]))
    first = exchange(merge(coords, join_kernel, first, (2, 2), second[:1]) * 2, 1, 0)
    shapes = [(part_second, LANES), (height - part_second, LANES)]
    second = send_across(*small_kernel_call(coords, direct_sum_kernel, second, shapes, first[:1]))
    first = exchange(merge(coords, pack_kernel, first, (4, 4), second[2:3]) * 2, 0, 1)
    second = direct(small_kernel_call(coords, plain_sum_kernel, second, [(height, LANES)], first[:1], 2 * 10**10) * 4)
    second = small_kernel_call(
        coords, direct_pack_kernel, second, [(4, height // 2, LANES)] * 2, first[2:], 2 * 10**10
    )
    second = exchange(second * 2, 0, 1)
    first = exchange(merge(coords, join_kernel, first, (8, 8), second[:1]) * 2, 0, 0)
    second = merge(coords, join_kernel, second, (8, 8), first[:1], 2 * 10**10)
    output, input_grad, finished = finish(coords, [*sums, resid, grad_resid, hidden, gains], second[:1])
    grad_g, grad_u, grad_d, settled = settle(coords, first, (768, 768), 768, False, (finished,))
    second = exchange(second * 2, 0, 0)
    (grad_q, grad_k, grad_v, grad_o, small_first, small_second, small_q, small_k, small_bias, grad_hw) = settle(
        coords, second, (512, 256, 256), 512, True, (settled,)
    )
    return (
        output,
        input_grad,
        small_first.reshape(256),
        grad_q,
        grad_k,
        grad_v,
        small_q.reshape(32),
        small_k.reshape(32),
        grad_hw.T,
        small_bias.reshape(4),
        grad_o,
        small_second.reshape(256),
        grad_g,
        grad_u,
        grad_d,
    )


def solution(mesh):
    grid = Mesh(mesh.devices.reshape(2, 4, 4, 2, 2), AXES)
    tokens, split, copies = P(AXES, None), P(GROUP, None), P(("zh", "y", "x"))
    line = P(GROUP)
    weights = (line, split, split, split, line, line, split, line, split, line, split, split, split)
    return jax.shard_map(
        body,
        mesh=grid,
        in_specs=(tokens, tokens, copies, copies, *weights),
        out_specs=(tokens, tokens, *weights),
        check_vma=False,
    )
```
